512 devices in a mesh: view: 4 (over x), space: 128 (over y, z, core).
Axes of the slice: x: 4, y: 8, z: 8, core: 2. Of those that a mesh axis runs over, the one named last changes fastest.
Arguments:
- estimate: bfloat16 [512, 512, 256], P('space'), may hold values from 0.1 to 10
- measured: bfloat16 [4, 512, 512, 256], P('view', 'space'), may hold values from 0.1 to 10
- psf_x: float32 [4, 31], P('view'), may hold values from 0.05 to 1
- psf_y: float32 [4, 31], P('view'), may hold values from 0.05 to 1
- psf_z: float32 [4, 63], P('view'), may hold values from 0.05 to 1
- tissue_mask: int32 [8], replicated, may hold values from 0 to 1, as said below
- column_owner: int32 [1024], replicated, may hold values from 0 to 127, as said below
Outputs:
- updated: bfloat16 [512, 512, 256], P('space')
- column_blur: bfloat16 [4, 512, 1024, 128], P('view', None, 'space')
The draws below stay inside these ranges and needn't reach their ends.
Inputs may be any that keep to these rules, and one draw needn't show every extreme that they name: `tissue_mask`: exactly half of the 8 tiles are tissue. `column_owner`: each index of space owns at most 8 tissue units, and some own exactly 8. Owners of units in non-tissue tiles carry no meaning.
All inputs are finite; a program needn't handle non-finite values.
Results may differ from the reference program's by a relative error of at most 0.001.
The reference program's roundings to bfloat16 on the way count: a program that leaves them out, or rounds other values in their place, can miss the bound.
Values may be sent and summed in bfloat16 or wider, within the bound.
No kernel may reach another device: no remote copies, remote signals or barrier semaphores. Data moves between devices by JAX's collectives and lax.ppermute only.
A program may use at most 64 MiB of HBM per device.

```python
import math
import jax
import jax.numpy as jnp
from jax import lax

PX = 512
PY = 256
TILE = 128
TAPS_XY = 31
TAPS_Z = 63
VIEWS = 4
NZ = 512
TILES = 8
UNITS = 1024
TISSUE_UNITS = 512
CAP = 8
N_SPACE = 128


def tissue_flags(key):
    ordering = jax.random.permutation(key, TILES)
    return jnp.where(ordering < TILES // 2, 1, 0).astype(jnp.int32)


def wave_field(key, leading, amplitude):
    freq_key, sign_key, phase_key = jax.random.split(key, 3)
    wave_count = 4
    log_freq = jax.random.uniform(freq_key, (leading, wave_count, 3), minval=math.log(1.0 / 512.0), maxval=math.log(1.0 / 32.0))
    sign_values = (2 * jax.random.randint(sign_key, (leading, wave_count, 3), 0, 2) - 1).astype(jnp.float32)
    frequency = jnp.exp(log_freq) * sign_values
    phases = jax.random.uniform(phase_key, (leading, wave_count), minval=0.0, maxval=2.0 * math.pi)
    depth_axis = jnp.arange(NZ, dtype=jnp.float32)[None, :, None, None]
    row_axis = jnp.arange(PX, dtype=jnp.float32)[None, None, :, None]
    col_axis = jnp.arange(PY, dtype=jnp.float32)[None, None, None, :]
    total = jnp.zeros((leading, NZ, PX, PY), jnp.float32)
    for index in range(wave_count):
        along_z = frequency[:, index, 0][:, None, None, None] * depth_axis
        along_x = frequency[:, index, 1][:, None, None, None] * row_axis
        along_y = frequency[:, index, 2][:, None, None, None] * col_axis
        phase_now = phases[:, index][:, None, None, None]
        total = total + amplitude * jnp.sin(2.0 * math.pi * (along_z + along_x + along_y) + phase_now)
    return total


def draw_estimate(key, part):
    key = jax.random.fold_in(key, 11)
    smooth_key, rough_key = jax.random.split(key)
    smooth = wave_field(smooth_key, 1, 0.35)[0]
    rough = jnp.exp(jax.random.uniform(rough_key, (NZ, PX, PY), minval=-0.7, maxval=0.7))
    return (jnp.exp(smooth) * rough).astype(jnp.bfloat16)


def draw_measured(key, part):
    key = jax.random.fold_in(key, 13)
    smooth_key, rough_key = jax.random.split(key)
    smooth = wave_field(smooth_key, VIEWS, 0.35)
    rough = jnp.exp(jax.random.uniform(rough_key, (VIEWS, NZ, PX, PY), minval=-0.7, maxval=0.7))
    return (jnp.exp(smooth) * rough).astype(jnp.bfloat16)


def draw_tissue_mask(key, part):
    return tissue_flags(key)


def draw_column_owner(key, part):
    tile_flags = tissue_flags(key)
    key = jax.random.fold_in(key, 7)
    perm_key, rank_key, rest_key = jax.random.split(key, 3)
    tiles_y = PY // TILE
    unit_index = jnp.arange(UNITS, dtype=jnp.int32)
    tile_index = unit_index // tiles_y // TILE * tiles_y + unit_index % tiles_y
    tissue = jnp.take(tile_flags, tile_index)
    scores = jax.random.permutation(perm_key, UNITS).astype(jnp.int32) + (1 - tissue) * UNITS
    ordering = jnp.argsort(scores)
    mean_load = TISSUE_UNITS // N_SPACE
    quarter = N_SPACE // 4
    places = jnp.arange(N_SPACE, dtype=jnp.int32)
    loads = jnp.where(places < quarter, 2 * mean_load, jnp.where(places < 3 * quarter, mean_load, 0)).astype(jnp.int32)
    boundaries = jnp.cumsum(loads).astype(jnp.int32)
    device_rank = jax.random.permutation(rank_key, N_SPACE).astype(jnp.int32)
    slot_place = jnp.searchsorted(boundaries, jnp.arange(TISSUE_UNITS, dtype=jnp.int32), side='right')
    assigned = jnp.take(device_rank, slot_place)
    others = jax.random.randint(rest_key, (UNITS - TISSUE_UNITS,), 0, N_SPACE, dtype=jnp.int32)
    values = jnp.concatenate([assigned, others]).astype(jnp.int32)
    return jnp.zeros((UNITS,), jnp.int32).at[ordering].set(values)


def level_of(stream_key, dims, cuts, least, high):
    loudness, own = 1.0, jax.random.fold_in(stream_key, 6)
    for dim, blocks in cuts:
        steps = jnp.exp(jax.random.uniform(jax.random.fold_in(own, dim), (blocks,), jnp.float32, least / len(cuts), high / len(cuts)))
        loudness = loudness * jnp.repeat(steps, dims[dim] // blocks).reshape([-1 if axis == dim else 1 for axis in range(len(dims))])
    return loudness


def setup_inputs(seed: int = 0) -> dict:
    streams_of = jax.random.split(jax.random.key(seed), 8)
    estimate = draw_estimate(jax.random.fold_in(streams_of[7], 71), 0)
    measured = draw_measured(jax.random.fold_in(streams_of[7], 71), 0)
    psf_x = jnp.clip(jnp.exp(math.log(1.0) - 2.9957323 * jax.random.uniform(streams_of[2], (VIEWS, TAPS_XY), jnp.float32) ** level_of(streams_of[2], (VIEWS, TAPS_XY), ((0, 4),), -0.2, 0.2)), 0.05, 1.0)
    psf_y = jnp.clip(jnp.exp(math.log(1.0) - 2.9957323 * jax.random.uniform(streams_of[3], (VIEWS, TAPS_XY), jnp.float32) ** level_of(streams_of[3], (VIEWS, TAPS_XY), ((0, 4),), -0.2, 0.2)), 0.05, 1.0)
    psf_z = jnp.clip(jnp.exp(math.log(1.0) - 2.9957323 * jax.random.uniform(streams_of[4], (VIEWS, TAPS_Z), jnp.float32) ** level_of(streams_of[4], (VIEWS, TAPS_Z), ((0, 4),), -0.2, 0.2)), 0.05, 1.0)
    tissue_mask = draw_tissue_mask(jax.random.fold_in(streams_of[7], 71), 0)
    column_owner = draw_column_owner(jax.random.fold_in(streams_of[7], 71), 0)
    return {"estimate": estimate, "measured": measured, "psf_x": psf_x, "psf_y": psf_y, "psf_z": psf_z, "tissue_mask": tissue_mask, "column_owner": column_owner}


def kernel_matrix(tap_values, length):
    normed = tap_values / jnp.sum(tap_values)
    rounded = lax.optimization_barrier(normed.astype(jnp.bfloat16)).astype(jnp.float32)
    half_len = tap_values.shape[0] // 2
    offset = jnp.arange(length, dtype=jnp.int32)[None, :] - jnp.arange(length, dtype=jnp.int32)[:, None] + half_len
    inside = (offset >= 0) & (offset < tap_values.shape[0])
    picked = jnp.take(rounded, jnp.clip(offset, 0, tap_values.shape[0] - 1).astype(jnp.int32))
    return jnp.where(inside, picked, jnp.zeros_like(picked))


def unit_tissue(tissue_mask, rows_x, tiles_y):
    unit_index = jnp.arange(rows_x * tiles_y, dtype=jnp.int32)
    tile_index = (unit_index // tiles_y) // TILE * tiles_y + unit_index % tiles_y
    matching = tile_index[:, None] == jnp.arange(tissue_mask.shape[0], dtype=jnp.int32)[None, :]
    return jnp.sum(jnp.where(matching, tissue_mask[None, :], 0), axis=1).astype(jnp.int32)


def slot_layout(tissue, column_owner, devices, capacity):
    unit_count = tissue.shape[0]
    unit_index = jnp.arange(unit_count, dtype=jnp.int32)
    member = ((column_owner[:, None] == jnp.arange(devices, dtype=jnp.int32)[None, :]) & (tissue[:, None] > 0)).astype(jnp.int32)
    before = (jnp.cumsum(member, axis=0) - member).astype(jnp.int32)
    position = jnp.sum(before * member, axis=1).astype(jnp.int32)
    target = jnp.where(tissue > 0, column_owner * capacity + position, devices * capacity).astype(jnp.int32)
    return jnp.full((devices * capacity,), unit_count, jnp.int32).at[target].set(unit_index, mode="drop")


def reference(estimate, measured, psf_x, psf_y, psf_z, tissue_mask, column_owner):
    tiles_y = PY // TILE
    unit_count = PX * tiles_y
    tissue = unit_tissue(tissue_mask, PX, tiles_y)
    slot_table = slot_layout(tissue, column_owner, N_SPACE, CAP)
    tissue_xy = jnp.repeat(tissue.reshape(PX, tiles_y), TILE, axis=1) > 0
    current = estimate.astype(jnp.float32)
    best = lax.Precision.HIGHEST

    def one_view(inputs):
        observed, taps_x, taps_y, taps_z = inputs
        matrix_x = kernel_matrix(taps_x, PX)
        matrix_y = kernel_matrix(taps_y, PY)
        matrix_z = kernel_matrix(taps_z, NZ)
        along_x = jnp.einsum("ab,kby->kay", matrix_x, current, precision=best).astype(jnp.bfloat16)
        blurred_xy = jnp.einsum("kxb,ab->kxa", along_x.astype(jnp.float32), matrix_y, precision=best).astype(jnp.bfloat16)
        blurred = jnp.einsum("wz,zxy->wxy", matrix_z, blurred_xy.astype(jnp.float32), precision=best)
        ratio_values = (observed.astype(jnp.float32) / blurred).astype(jnp.bfloat16)
        back_z = jnp.einsum("wz,wxy->zxy", matrix_z, ratio_values.astype(jnp.float32), precision=best).astype(jnp.bfloat16)
        back_z = jnp.where(tissue_xy[None, :, :], back_z, jnp.ones_like(back_z))
        back_y = jnp.einsum("kxa,ab->kxb", back_z.astype(jnp.float32), matrix_y, precision=best).astype(jnp.bfloat16)
        back_x = jnp.einsum("kay,ab->kby", back_y.astype(jnp.float32), matrix_x, precision=best)
        blurred_units = blurred.astype(jnp.bfloat16).reshape(NZ, unit_count, TILE)
        columns = jnp.take(blurred_units, slot_table, axis=1, mode="fill", fill_value=0)
        return back_x, columns

    backs, columns = lax.map(one_view, (measured, psf_x, psf_y, psf_z))
    summed = jnp.sum(backs, axis=0)
    updated = (current * summed / VIEWS).astype(jnp.bfloat16)
    return updated, columns
```

```python
import jax
import jax.numpy as jnp
from jax import lax
from jax.experimental import pallas as pl
from jax.experimental.pallas import tpu as pltpu
from jax.sharding import PartitionSpec as P

F32 = jnp.float32
BF16 = jnp.bfloat16
I32 = jnp.int32

VIEWS, DEVS = 4, 128
SLAB, NX, NY, TILE = 4, 512, 256, 128
UNITS = 1024
HALF = 4
MSG = 3 * SLAB * HALF
TAPS_XY, TAPS_Z = 31, 63
ZB = 256
VMEM_LIMIT = 48 * 1024 * 1024


def iota(shape, dim):
    return lax.broadcasted_iota(I32, shape, dim)


def placed_taps(read, count, lanes, place):
    lane = iota((1, lanes), 1)
    total = read(0)
    for m in range(1, count):
        total = total + read(m)
    row = jnp.zeros((1, lanes), F32)
    for m in range(count):
        row = jnp.where(lane == place(m) % lanes, read(m), row)
    return (row / jnp.full((1, lanes), total, F32)).astype(BF16).astype(F32)


def rolled(row, rows):
    return pltpu.roll(
        jnp.broadcast_to(row, (rows, row.shape[1])), 0, 1, stride=1, stride_axis=0
    )


def band(row, n, half):
    distance = jnp.abs(iota((n, n), 1) - iota((n, n), 0))
    return jnp.where(distance <= half, rolled(row, n), 0.0).astype(BF16)


def dot(a, b, dims=((1,), (0,))):
    return lax.dot_general(a, b, (dims, ((), ())), preferred_element_type=F32)


def one_hot(condition):
    return jnp.where(condition, 1.0, 0.0).astype(BF16)


def slot_tables(mask_ref, owner_ref):
    device = iota((DEVS, ZB), 0)
    lane = iota((DEVS, ZB), 1)
    before_tri = one_hot(iota((ZB, ZB), 0) < iota((ZB, ZB), 1))
    count = jnp.zeros((DEVS, 1), F32)
    unit_of = [jnp.zeros((DEVS, 1), F32) for _ in range(2 * HALF)]
    for block in range(UNITS // ZB):
        tissue = jnp.where(lane % 2 == 0, mask_ref[2 * block], mask_ref[2 * block + 1])
        owner = owner_ref[0:1, block * ZB : (block + 1) * ZB]
        member = (owner == device) & (tissue > 0)
        before = dot(one_hot(member), before_tri) + count
        unit = (lane + block * ZB).astype(F32)
        for slot in range(2 * HALF):
            here = member & (before == float(slot))
            unit_of[slot] += jnp.sum(jnp.where(here, unit, 0.0), axis=1, keepdims=True)
        count += jnp.sum(jnp.where(member, 1.0, 0.0), axis=1, keepdims=True)
    over = jnp.maximum(count - HALF, 0.0)
    free = jnp.maximum(HALF - count, 0.0)
    lower = one_hot(iota((DEVS, DEVS), 1) < iota((DEVS, DEVS), 0))
    square = (DEVS, DEVS)
    starts = dot(
        lower,
        jnp.where(iota(square, 1) == 0, over, jnp.where(iota(square, 1) == 1, free, 0.0)).astype(BF16),
    )
    over_start, free_start = starts[:, 0:1], starts[:, 1:2]
    columns = jnp.zeros(square, F32)
    for i, column in enumerate([over_start, over, *unit_of[HALF:]]):
        columns = jnp.where(iota(square, 1) == i, column, columns)
    rows = columns.T
    balanced = []
    for slot in range(HALF):
        rank = free_start + (slot - count)
        filler = jnp.zeros((DEVS, 1), F32)
        for extra in range(HALF):
            match = (rows[0:1] + extra == rank) & (rows[1:2] > extra)
            filler += jnp.sum(jnp.where(match, rows[2 + extra : 3 + extra], 0.0), axis=1, keepdims=True)
        balanced.append(jnp.where(count > slot, unit_of[slot], filler))
    return balanced, unit_of[HALF:], count


def pack_kernel(mask_ref, px_ref, py_ref, owner_ref, est_ref, meas_ref, out_ref, table_ref, count_ref, wide):
    balanced, overflow, count = slot_tables(mask_ref, owner_ref)
    count_ref[...] = jnp.broadcast_to(count, (DEVS, TILE)).astype(I32)
    units = jnp.concatenate(balanced + overflow, axis=0).astype(I32)
    row_x = units // 2
    odd = units % 2 == 1
    slots = HALF * DEVS
    lane = iota((DEVS, slots), 1)
    along = jnp.zeros((DEVS, slots), F32)
    for slot in range(HALF):
        mine = (lane // HALF == iota((DEVS, slots), 0)) & (lane % HALF == slot)
        along = jnp.where(mine, balanced[slot], along)
    table_ref[...] = jnp.broadcast_to(jnp.sum(along, axis=0, keepdims=True), (8, slots)).astype(I32)

    half_xy = TAPS_XY // 2
    matrix_x = band(placed_taps(lambda m: px_ref[0, m], TAPS_XY, NX, lambda m: m - half_xy), NX, half_xy)
    matrix_y = band(placed_taps(lambda m: py_ref[0, m], TAPS_XY, NY, lambda m: m - half_xy), NY, half_xy)
    pick = one_hot(row_x == iota((2 * slots, NX), 1))
    picked_x = dot(pick, matrix_x).astype(BF16)
    for plane in range(SLAB):
        along_x = dot(picked_x, est_ref[plane]).astype(BF16)
        blurred = dot(along_x, matrix_y, ((1,), (1,)))
        blurred = jnp.where(odd, blurred[:, TILE:], blurred[:, :TILE])
        seen = dot(pick[:slots], meas_ref[0, plane])
        seen = jnp.where(odd[:slots], seen[:, TILE:], seen[:, :TILE])
        for slot in range(HALF):
            row = plane * HALF + slot
            here = slice(slot * DEVS, (slot + 1) * DEVS)
            past = slice(slots + slot * DEVS, slots + (slot + 1) * DEVS)
            wide[pl.ds(row, DEVS, stride=MSG), :] = blurred[here]
            wide[pl.ds(SLAB * HALF + row, DEVS, stride=MSG), :] = blurred[past]
            wide[pl.ds(2 * SLAB * HALF + row, DEVS, stride=MSG), :] = seen[here]
    out_ref[...] = wide[...].astype(BF16).reshape(DEVS, MSG, TILE)


def z_kernel(me_ref, pz_ref, count_ref, in_ref, column_ref, back_ref, padded, ratio):
    group = SLAB * HALF
    rows = DEVS * group
    edge = ZB // 2
    half_z = TAPS_Z // 2
    near = edge - HALF * half_z
    far = edge + HALF * half_z
    forward = rolled(placed_taps(lambda m: pz_ref[0, m], TAPS_Z, 2 * ZB, lambda m: near + HALF * m), ZB).astype(BF16)
    adjoint = rolled(placed_taps(lambda m: pz_ref[0, m], TAPS_Z, 2 * ZB, lambda m: far - HALF * m), ZB).astype(BF16)
    r = iota((ZB, ZB), 0)
    part = ZB // SLAB
    source = r % part // HALF * group + r // part * HALF + r % HALF
    adjoint = dot(one_hot(iota((ZB, ZB), 1) == source), adjoint).astype(BF16)

    padded[0:edge, :] = jnp.zeros((edge, 2 * TILE), BF16)
    padded[edge + rows :, :] = jnp.zeros((edge, 2 * TILE), BF16)
    ratio[0:edge, :] = jnp.zeros((edge, TILE), BF16)
    ratio[edge + rows :, :] = jnp.zeros((edge, TILE), BF16)
    padded[edge : edge + rows, 0:TILE] = in_ref[:, 0:group, :].reshape(rows, TILE)
    padded[edge : edge + rows, TILE:] = in_ref[:, group : 2 * group, :].reshape(rows, TILE)
    count = count_ref[pl.ds(me_ref[0], 1), :].reshape(1, 1, TILE)
    planes = ZB // HALF
    pairs = planes // 2
    sub = iota((pairs, 8, TILE), 1)
    live = sub < count
    for block in range(rows // ZB):
        values = dot(forward, padded[block * ZB : block * ZB + 2 * ZB, :])
        own = values[:, :TILE]
        seen = in_ref[block * ZB // group : (block + 1) * ZB // group, 2 * group :, :].reshape(ZB, TILE)
        ratio[edge + block * ZB : edge + (block + 1) * ZB, :] = (seen.astype(F32) / own).astype(BF16)
        own = own.reshape(pairs, 8, TILE)
        more = values[:, TILE:].reshape(pairs, 8, TILE)
        first = jnp.where(sub < HALF, own, pltpu.roll(more, HALF, 1))
        second = jnp.where(sub < HALF, pltpu.roll(own, HALF, 1), more)
        both = jnp.stack([jnp.where(live, first, 0.0), jnp.where(live, second, 0.0)], axis=1)
        column_ref[block * planes : (block + 1) * planes] = both.reshape(planes, 8, TILE).astype(BF16)
    for block in range(rows // ZB):
        values = dot(adjoint, ratio[block * ZB : block * ZB + 2 * ZB, :]).astype(BF16)
        for plane in range(SLAB):
            back_ref[plane, block * part : (block + 1) * part, :] = values[plane * part : (plane + 1) * part]


def back_kernel(me_ref, mask_ref, px_ref, py_ref, table_ref, est_ref, in_ref, out_ref, stacked_x, stacked_y):
    half_xy = TAPS_XY // 2
    units = table_ref[0:1, :]
    row_x = units // 2
    slots = units.shape[1]
    here = row_x == iota((NX, slots), 0)
    cols = jnp.concatenate([in_ref[view] for view in range(VIEWS)], axis=1)
    tile_row = iota((NX, 1), 0) // TILE
    spread = []
    for t in range(2):
        found = dot(one_hot(here & (units % 2 == t)), cols)
        tissue = jnp.zeros((NX, 1), I32)
        for i in range(NX // TILE):
            tissue = jnp.where(tile_row == i, mask_ref[2 * i + t], tissue)
        spread.append(jnp.where(tissue > 0, found, 1.0).astype(BF16))
    for view in range(VIEWS):
        matrix_y = band(
            placed_taps(lambda m: py_ref[view, m], TAPS_XY, NY, lambda m: m - half_xy), NY, half_xy
        )
        stacked_x[:, view * NX : (view + 1) * NX] = band(
            placed_taps(lambda m: px_ref[view, m], TAPS_XY, NX, lambda m: half_xy - m), NX, half_xy
        )
        lanes = slice(view * TILE, (view + 1) * TILE)
        back_z = jnp.concatenate([spread[0][:, lanes], spread[1][:, lanes]], axis=1)
        stacked_y[view * NX : (view + 1) * NX, :] = dot(back_z, matrix_y).astype(BF16)
    summed = dot(stacked_x[...], stacked_y[...])
    out_ref[0] = (est_ref[0].astype(F32) * summed / VIEWS).astype(BF16)


def shards(estimate, measured, psf_x, psf_y, psf_z, tissue_mask, column_owner):
    smem = pl.BlockSpec(memory_space=pltpu.SMEM)
    vmem = pl.BlockSpec(memory_space=pltpu.VMEM)
    params = pltpu.CompilerParams(vmem_limit_bytes=VMEM_LIMIT)
    taps = lax.all_gather(jnp.concatenate([psf_x, psf_y], axis=1), "view", axis=0, tiled=True)
    slots = HALF * DEVS
    message, table, count = pl.pallas_call(
        pack_kernel,
        out_shape=(
            jax.ShapeDtypeStruct((DEVS, MSG, TILE), BF16),
            jax.ShapeDtypeStruct((8, slots), I32),
            jax.ShapeDtypeStruct((DEVS, TILE), I32),
        ),
        in_specs=[smem, smem, smem, vmem, vmem, vmem],
        out_specs=(vmem, vmem, vmem),
        scratch_shapes=[pltpu.VMEM((DEVS * MSG, TILE), F32)],
        compiler_params=params,
        name="pack",
    )(tissue_mask, psf_x, psf_y, column_owner.reshape(1, UNITS), estimate, measured)
    arrived = lax.all_to_all(message, "space", split_axis=0, concat_axis=0, tiled=True)
    rows = DEVS * SLAB * HALF
    space_index = lax.axis_index("space").astype(I32).reshape(1)
    view_index = lax.axis_index("view").astype(I32).reshape(1)
    column_blur, back = pl.pallas_call(
        z_kernel,
        out_shape=(
            jax.ShapeDtypeStruct((SLAB * DEVS, 2 * HALF, TILE), BF16),
            jax.ShapeDtypeStruct((VIEWS, slots, TILE), BF16),
        ),
        in_specs=[smem, smem, vmem, vmem],
        out_specs=(vmem, vmem),
        scratch_shapes=[
            pltpu.VMEM((rows + ZB, 2 * TILE), BF16),
            pltpu.VMEM((rows + ZB, TILE), BF16),
        ],
        compiler_params=params,
        name="zpair",
    )(space_index, psf_z, count, arrived)
    returned = lax.all_to_all(
        back.reshape(VIEWS * DEVS, HALF, TILE),
        ("view", "space"),
        split_axis=0,
        concat_axis=0,
        tiled=True,
    ).reshape(VIEWS, slots, TILE)
    updated = pl.pallas_call(
        back_kernel,
        grid_spec=pltpu.PrefetchScalarGridSpec(
            num_scalar_prefetch=1,
            grid=(1,),
            in_specs=[
                smem,
                smem,
                smem,
                pl.BlockSpec((8, slots), lambda i, me: (0, 0)),
                pl.BlockSpec((1, NX, NY), lambda i, me: (me[0], 0, 0)),
                pl.BlockSpec((VIEWS, slots, TILE), lambda i, me: (0, 0, 0)),
            ],
            out_specs=pl.BlockSpec((1, NX, NY), lambda i, me: (0, 0, 0)),
            scratch_shapes=[
                pltpu.VMEM((NX, VIEWS * NX), BF16),
                pltpu.VMEM((VIEWS * NX, NY), BF16),
            ],
        ),
        out_shape=jax.ShapeDtypeStruct((1, NX, NY), BF16),
        compiler_params=params,
        name="back",
    )(view_index, tissue_mask, taps[:, :TAPS_XY], taps[:, TAPS_XY:], table, estimate, returned)
    updated = lax.all_gather(updated, "view", axis=0, tiled=True)
    return updated, column_blur[None]


def solution(mesh):
    placed = (
        P("space", None, None),
        P("view", "space", None, None),
        P("view", None),
        P("view", None),
        P("view", None),
        P(),
        P(),
    )
    return jax.shard_map(
        shards,
        mesh=mesh,
        in_specs=placed,
        out_specs=(P("space", None, None), P("view", None, "space", None)),
        check_vma=False,
    )
```

```python
import jax
import jax.numpy as jnp
from jax import lax
from jax.experimental import pallas as pl
from jax.experimental.pallas import tpu as pltpu
from jax.sharding import PartitionSpec as P

F32 = jnp.float32
BF16 = jnp.bfloat16
I32 = jnp.int32

VIEWS, DEVS = 4, 128
SLAB, NX, NY, TILE = 4, 512, 256, 128
UNITS = 1024
HALF = 4
MSG = 3 * SLAB * HALF
TAPS_XY, TAPS_Z = 31, 63
ZB = 256
PACK_LIMIT, LIMIT = 60, 24
OUT_PARTS = 4

SMEM = pl.BlockSpec(memory_space=pltpu.SMEM)
VMEM = pl.BlockSpec(memory_space=pltpu.VMEM)
ANY = pl.BlockSpec(memory_space=pl.ANY)


def shape(*dims, dtype=BF16):
    return jax.ShapeDtypeStruct(dims, dtype)


def iota(shape, dim):
    return lax.broadcasted_iota(I32, shape, dim)


def placed_taps(read, count, lanes, place):
    lane = iota((1, lanes), 1)
    total = read(0)
    for m in range(1, count):
        total = total + read(m)
    row = jnp.zeros((1, lanes), F32)
    for m in range(count):
        row = jnp.where(lane == place(m) % lanes, read(m), row)
    return (row / jnp.full((1, lanes), total, F32)).astype(BF16).astype(F32)


def rolled(row, rows):
    return pltpu.roll(
        jnp.broadcast_to(row, (rows, row.shape[1])), 0, 1, stride=1, stride_axis=0
    )


def band(row, n, half):
    distance = jnp.abs(iota((n, n), 1) - iota((n, n), 0))
    return jnp.where(distance <= half, rolled(row, n), 0.0).astype(BF16)


def dot(a, b, dims=((1,), (0,))):
    return lax.dot_general(a, b, (dims, ((), ())), preferred_element_type=F32)


def one_hot(condition):
    return jnp.where(condition, 1.0, 0.0).astype(BF16)


def slot_tables(mask_ref, owner_ref):
    device = iota((DEVS, ZB), 0)
    lane = iota((DEVS, ZB), 1)
    before_tri = one_hot(iota((ZB, ZB), 0) < iota((ZB, ZB), 1))
    count = jnp.zeros((DEVS, 1), F32)
    unit_of = [jnp.zeros((DEVS, 1), F32) for _ in range(2 * HALF)]
    for block in range(UNITS // ZB):
        tissue = jnp.where(lane % 2 == 0, mask_ref[2 * block], mask_ref[2 * block + 1])
        owner = owner_ref[0:1, block * ZB : (block + 1) * ZB]
        member = (owner == device) & (tissue > 0)
        before = dot(one_hot(member), before_tri) + count
        unit = (lane + block * ZB).astype(F32)
        for slot in range(2 * HALF):
            here = member & (before == float(slot))
            unit_of[slot] += jnp.sum(jnp.where(here, unit, 0.0), axis=1, keepdims=True)
        count += jnp.sum(jnp.where(member, 1.0, 0.0), axis=1, keepdims=True)
    over = jnp.maximum(count - HALF, 0.0)
    free = jnp.maximum(HALF - count, 0.0)
    lower = one_hot(iota((DEVS, DEVS), 1) < iota((DEVS, DEVS), 0))
    square = (DEVS, DEVS)
    starts = dot(
        lower,
        jnp.where(iota(square, 1) == 0, over, jnp.where(iota(square, 1) == 1, free, 0.0)).astype(BF16),
    )
    over_start, free_start = starts[:, 0:1], starts[:, 1:2]
    columns = jnp.zeros(square, F32)
    for i, column in enumerate([over_start, over, *unit_of[HALF:]]):
        columns = jnp.where(iota(square, 1) == i, column, columns)
    rows = columns.T
    balanced = []
    for slot in range(HALF):
        rank = free_start + (slot - count)
        filler = jnp.zeros((DEVS, 1), F32)
        for extra in range(HALF):
            match = (rows[0:1] + extra == rank) & (rows[1:2] > extra)
            filler += jnp.sum(jnp.where(match, rows[2 + extra : 3 + extra], 0.0), axis=1, keepdims=True)
        balanced.append(jnp.where(count > slot, unit_of[slot], filler))
    return balanced, unit_of[HALF:], count


def pack_kernel(
    mask_ref, px_ref, py_ref, owner_ref, est_hbm, meas_hbm, out_hbm, table_ref, count_ref,
    est_ref, meas_ref, wide, out_ref, est_sem, meas_sem, out_sem,
):
    est_copy = pltpu.make_async_copy(est_hbm, est_ref, est_sem)
    meas_copy = pltpu.make_async_copy(meas_hbm, meas_ref, meas_sem)
    est_copy.start()
    meas_copy.start()
    balanced, overflow, count = slot_tables(mask_ref, owner_ref)
    count_ref[...] = jnp.broadcast_to(count, (DEVS, TILE)).astype(I32)
    units = jnp.concatenate(balanced, axis=0).astype(I32)
    odd = units % 2 == 1
    slots = HALF * DEVS
    lane = iota((DEVS, slots), 1)
    along = jnp.zeros((DEVS, slots), F32)
    across = jnp.zeros((DEVS, slots), F32)
    for slot in range(HALF):
        mine = (lane // HALF == iota((DEVS, slots), 0)) & (lane % HALF == slot)
        along = jnp.where(mine, balanced[slot], along)
        mine = (lane % DEVS == iota((DEVS, slots), 0)) & (lane // DEVS == slot)
        across = jnp.where(mine, balanced[slot], across)
    table_ref[...] = jnp.broadcast_to(jnp.sum(along, axis=0, keepdims=True), (8, slots)).astype(I32)
    across = jnp.sum(across, axis=0, keepdims=True)
    past = jnp.concatenate(
        [jnp.where(count > HALF + i, overflow[i], -1.0) for i in range(HALF)], axis=0
    )
    again = one_hot(past == across)

    half_xy = TAPS_XY // 2
    matrix_x = band(placed_taps(lambda m: px_ref[0, m], TAPS_XY, NX, lambda m: m - half_xy), NX, half_xy)
    matrix_y = band(placed_taps(lambda m: py_ref[0, m], TAPS_XY, NY, lambda m: m - half_xy), NY, half_xy)
    pick = one_hot(units // 2 == iota((slots, NX), 1))
    picked_x = dot(pick, matrix_x).astype(BF16)
    est_copy.wait()
    narrow = []
    for plane in range(SLAB):
        along_x = dot(picked_x, est_ref[plane]).astype(BF16)
        blurred = dot(along_x, matrix_y, ((1,), (1,)))
        blurred = jnp.where(odd, blurred[:, TILE:], blurred[:, :TILE])
        narrow.append(blurred.astype(BF16))
        for slot in range(HALF):
            row = plane * HALF + slot
            wide[pl.ds(row, DEVS, stride=MSG), :] = blurred[slot * DEVS : (slot + 1) * DEVS]
    blurred = dot(again, jnp.concatenate(narrow, axis=1))
    for plane in range(SLAB):
        for slot in range(HALF):
            row = (SLAB + plane) * HALF + slot
            wide[pl.ds(row, DEVS, stride=MSG), :] = blurred[
                slot * DEVS : (slot + 1) * DEVS, plane * TILE : (plane + 1) * TILE
            ]
    meas_copy.wait()
    for plane in range(SLAB):
        seen = dot(pick, meas_ref[0, plane])
        seen = jnp.where(odd, seen[:, TILE:], seen[:, :TILE])
        for slot in range(HALF):
            row = (2 * SLAB + plane) * HALF + slot
            wide[pl.ds(row, DEVS, stride=MSG), :] = seen[slot * DEVS : (slot + 1) * DEVS]
    part = DEVS // OUT_PARTS
    copies = []
    for i in range(OUT_PARTS):
        here = pl.ds(i * part, part)
        out_ref[here] = wide[pl.ds(i * part * MSG, part * MSG), :].astype(BF16).reshape(part, MSG, TILE)
        copies.append(pltpu.make_async_copy(out_ref.at[here], out_hbm.at[here], out_sem.at[i]))
        copies[-1].start()
    for copy in copies:
        copy.wait()


def prep_kernel(pz_ref, taps_ref, table_ref, forward_ref, adjoint_ref, spread_ref, x_ref, y_ref):
    group = SLAB * HALF
    edge = ZB // 2
    half_z = TAPS_Z // 2
    near = edge - HALF * half_z
    far = edge + HALF * half_z
    forward_ref[...] = rolled(
        placed_taps(lambda m: pz_ref[0, m], TAPS_Z, 2 * ZB, lambda m: near + HALF * m), ZB
    ).astype(BF16)
    adjoint = rolled(
        placed_taps(lambda m: pz_ref[0, m], TAPS_Z, 2 * ZB, lambda m: far - HALF * m), ZB
    ).astype(BF16)
    r = iota((ZB, ZB), 0)
    part = ZB // SLAB
    source = r % part // HALF * group + r // part * HALF + r % HALF
    adjoint_ref[...] = dot(one_hot(iota((ZB, ZB), 1) == source), adjoint).astype(BF16)

    units = table_ref[0:1, :]
    here = units // 2 == iota((NX, units.shape[1]), 0)
    for t in range(2):
        spread_ref[t] = one_hot(here & (units % 2 == t))
    half_xy = TAPS_XY // 2
    for view in range(VIEWS):
        x_ref[:, view * NX : (view + 1) * NX] = band(
            placed_taps(lambda m: taps_ref[view, m], TAPS_XY, NX, lambda m: half_xy - m), NX, half_xy
        )
        y_ref[view] = band(
            placed_taps(lambda m: taps_ref[view, TAPS_XY + m], TAPS_XY, NY, lambda m: m - half_xy), NY, half_xy
        )


def z_kernel(forward_ref, adjoint_ref, in_ref, back_ref, padded, ratio):
    group = SLAB * HALF
    rows = DEVS * group
    edge = ZB // 2
    for ref in (padded, ratio):
        ref[0:edge, :] = jnp.zeros((edge, TILE), BF16)
        ref[edge + rows :, :] = jnp.zeros((edge, TILE), BF16)
    padded[edge : edge + rows, :] = in_ref[:, 0:group, :].reshape(rows, TILE)
    for block in range(rows // ZB):
        own = dot(forward_ref[...], padded[block * ZB : block * ZB + 2 * ZB, :])
        seen = in_ref[block * ZB // group : (block + 1) * ZB // group, 2 * group :, :].reshape(ZB, TILE)
        ratio[edge + block * ZB : edge + (block + 1) * ZB, :] = (seen.astype(F32) / own).astype(BF16)
    part = ZB // SLAB
    for block in range(rows // ZB):
        values = dot(adjoint_ref[...], ratio[block * ZB : block * ZB + 2 * ZB, :]).astype(BF16)
        for plane in range(SLAB):
            back_ref[plane, block * part : (block + 1) * part, :] = values[plane * part : (plane + 1) * part]


def column_kernel(me_ref, forward_ref, count_ref, in_ref, column_ref, padded):
    group = SLAB * HALF
    rows = DEVS * group
    edge = ZB // 2
    padded[0:edge, :] = jnp.zeros((edge, 2 * TILE), BF16)
    padded[edge + rows :, :] = jnp.zeros((edge, 2 * TILE), BF16)
    padded[edge : edge + rows, 0:TILE] = in_ref[:, 0:group, :].reshape(rows, TILE)
    padded[edge : edge + rows, TILE:] = in_ref[:, group : 2 * group, :].reshape(rows, TILE)
    count = count_ref[pl.ds(me_ref[0], 1), :].reshape(1, 1, TILE)
    planes = ZB // HALF
    pairs = planes // 2
    sub = iota((pairs, 8, TILE), 1)
    live = sub < count
    for block in range(rows // ZB):
        values = dot(forward_ref[...], padded[block * ZB : block * ZB + 2 * ZB, :])
        own = values[:, :TILE].reshape(pairs, 8, TILE)
        more = values[:, TILE:].reshape(pairs, 8, TILE)
        first = jnp.where(sub < HALF, own, pltpu.roll(more, HALF, 1))
        second = jnp.where(sub < HALF, pltpu.roll(own, HALF, 1), more)
        both = jnp.stack([jnp.where(live, first, 0.0), jnp.where(live, second, 0.0)], axis=1)
        column_ref[block * planes : (block + 1) * planes] = both.reshape(planes, 8, TILE).astype(BF16)


def back_kernel(me_ref, mask_ref, spread_ref, x_ref, y_ref, est_ref, in_ref, out_ref, stacked):
    cols = jnp.concatenate([in_ref[view] for view in range(VIEWS)], axis=1)
    tile_row = iota((NX, 1), 0) // TILE
    back_z = []
    for t in range(2):
        found = dot(spread_ref[t], cols)
        tissue = jnp.zeros((NX, 1), I32)
        for i in range(NX // TILE):
            tissue = jnp.where(tile_row == i, mask_ref[2 * i + t], tissue)
        back_z.append(jnp.where(tissue > 0, found, 1.0).astype(BF16))
    for view in range(VIEWS):
        lanes = slice(view * TILE, (view + 1) * TILE)
        one_view = jnp.concatenate([back_z[0][:, lanes], back_z[1][:, lanes]], axis=1)
        stacked[view * NX : (view + 1) * NX, :] = dot(one_view, y_ref[view]).astype(BF16)
    summed = dot(x_ref[...], stacked[...])
    updated = (est_ref[0].astype(F32) * summed / VIEWS).astype(BF16)
    for view in range(VIEWS):
        out_ref[view] = updated


def call(kernel, name, out_shape, in_specs, scratch, limit, flops=0, moved=0):
    return pl.pallas_call(
        kernel,
        out_shape=out_shape,
        in_specs=in_specs,
        out_specs=jax.tree.map(lambda s: ANY if name == "pack" and s.shape == (DEVS, MSG, TILE) else VMEM, out_shape),
        scratch_shapes=scratch,
        compiler_params=pltpu.CompilerParams(vmem_limit_bytes=limit * 1024 * 1024),
        cost_estimate=pl.CostEstimate(flops=flops, bytes_accessed=moved, transcendentals=0),
        name=name,
    )


def pack(estimate, measured, psf_x, psf_y, tissue_mask, column_owner):
    return call(
        pack_kernel,
        "pack",
        (shape(DEVS, MSG, TILE), shape(8, HALF * DEVS, dtype=I32), shape(DEVS, TILE, dtype=I32)),
        [SMEM, SMEM, SMEM, VMEM, ANY, ANY],
        [
            pltpu.VMEM((SLAB, NX, NY), BF16),
            pltpu.VMEM((1, SLAB, NX, NY), BF16),
            pltpu.VMEM((DEVS * MSG, TILE), F32),
            pltpu.VMEM((DEVS, MSG, TILE), BF16),
            pltpu.SemaphoreType.DMA,
            pltpu.SemaphoreType.DMA,
            pltpu.SemaphoreType.DMA((OUT_PARTS,)),
        ],
        PACK_LIMIT,
        flops=2_000_000_000,
        moved=4_000_000,
    )(tissue_mask, psf_x, psf_y, column_owner.reshape(1, UNITS), estimate, measured)


def prep(psf_z, taps, table):
    return call(
        prep_kernel,
        "prep",
        (
            shape(ZB, 2 * ZB),
            shape(ZB, 2 * ZB),
            shape(2, NX, HALF * DEVS),
            shape(NX, VIEWS * NX),
            shape(VIEWS, NY, NY),
        ),
        [SMEM, SMEM, VMEM],
        [],
        LIMIT,
        flops=1_000_000_000,
        moved=4_000_000,
    )(psf_z, taps, table)


def z_pair(forward, adjoint, arrived):
    rows = DEVS * SLAB * HALF
    return call(
        z_kernel,
        "zpair",
        shape(VIEWS, HALF * DEVS, TILE),
        [VMEM, VMEM, VMEM],
        [pltpu.VMEM((rows + ZB, TILE), BF16), pltpu.VMEM((rows + ZB, TILE), BF16)],
        LIMIT,
        flops=540_000_000,
        moved=3_000_000,
    )(forward, adjoint, arrived)


def column(space_index, forward, count, arrived):
    rows = DEVS * SLAB * HALF
    return call(
        column_kernel,
        "column",
        shape(SLAB * DEVS, 2 * HALF, TILE),
        [SMEM, VMEM, VMEM, VMEM],
        [pltpu.VMEM((rows + ZB, 2 * TILE), BF16)],
        LIMIT,
        flops=540_000_000,
        moved=3_000_000,
    )(space_index, forward, count, arrived)


def back(view_index, tissue_mask, spread, matrix_x, matrix_y, estimate, returned):
    whole = lambda *dims: pl.BlockSpec(dims, lambda i, me: (0,) * len(dims))
    return pl.pallas_call(
        back_kernel,
        grid_spec=pltpu.PrefetchScalarGridSpec(
            num_scalar_prefetch=1,
            grid=(1,),
            in_specs=[
                SMEM,
                whole(2, NX, HALF * DEVS),
                whole(NX, VIEWS * NX),
                whole(VIEWS, NY, NY),
                pl.BlockSpec((1, NX, NY), lambda i, me: (me[0], 0, 0)),
                whole(VIEWS, HALF * DEVS, TILE),
            ],
            out_specs=whole(VIEWS, NX, NY),
            scratch_shapes=[pltpu.VMEM((VIEWS * NX, NY), BF16)],
        ),
        out_shape=shape(VIEWS, NX, NY),
        compiler_params=pltpu.CompilerParams(vmem_limit_bytes=LIMIT * 1024 * 1024),
        cost_estimate=pl.CostEstimate(flops=1_400_000_000, bytes_accessed=5_000_000, transcendentals=0),
        name="back",
    )(view_index, tissue_mask, spread, matrix_x, matrix_y, estimate, returned)


def shards(estimate, measured, psf_x, psf_y, psf_z, tissue_mask, column_owner):
    message, table, count = pack(estimate, measured, psf_x, psf_y, tissue_mask, column_owner)
    arrived = lax.all_to_all(message, "space", split_axis=0, concat_axis=0, tiled=True)
    taps = lax.all_gather(jnp.concatenate([psf_x, psf_y], axis=1), "view", axis=0, tiled=True)
    forward, adjoint, spread, matrix_x, matrix_y = prep(psf_z, taps, table)
    space_index = lax.axis_index("space").astype(I32).reshape(1)
    view_index = lax.axis_index("view").astype(I32).reshape(1)
    sent = z_pair(forward, adjoint, arrived)
    returned = lax.all_to_all(
        sent.reshape(VIEWS * DEVS, HALF, TILE),
        ("view", "space"),
        split_axis=0,
        concat_axis=0,
        tiled=True,
    ).reshape(VIEWS, HALF * DEVS, TILE)
    column_blur = column(space_index, forward, count, arrived)
    updated = back(view_index, tissue_mask, spread, matrix_x, matrix_y, estimate, returned)
    updated = lax.all_to_all(updated, "view", split_axis=0, concat_axis=0, tiled=True)
    return updated, column_blur[None]


def solution(mesh):
    placed = (
        P("space", None, None),
        P("view", "space", None, None),
        P("view", None),
        P("view", None),
        P("view", None),
        P(),
        P(),
    )
    return jax.shard_map(
        shards,
        mesh=mesh,
        in_specs=placed,
        out_specs=(P("space", None, None), P("view", None, "space", None)),
        check_vma=False,
    )
```

```python
import jax
import jax.numpy as jnp
from jax import lax
from jax.experimental import pallas as pl
from jax.experimental.pallas import tpu as pltpu
from jax.sharding import PartitionSpec as P

F32 = jnp.float32
BF16 = jnp.bfloat16
I32 = jnp.int32

VIEWS, DEVS = 4, 128
SLAB, NX, NY, TILE = 4, 512, 256, 128
UNITS = 1024
HALF = 4
MSG = 3 * SLAB * HALF
TAPS_XY, TAPS_Z = 31, 63
ZB = 256
XB = 128
WIDE_LIMIT, LIMIT = 60, 24
OUT_PARTS = 4

SMEM = pl.BlockSpec(memory_space=pltpu.SMEM)
VMEM = pl.BlockSpec(memory_space=pltpu.VMEM)
ANY = pl.BlockSpec(memory_space=pl.ANY)
HBM = pl.BlockSpec(memory_space=pltpu.HBM)


def shape(*dims, dtype=BF16):
    return jax.ShapeDtypeStruct(dims, dtype)


def iota(shape, dim):
    return lax.broadcasted_iota(I32, shape, dim)


def placed_taps(read, count, lanes, place):
    lane = iota((1, lanes), 1)
    total = read(0)
    for m in range(1, count):
        total = total + read(m)
    row = jnp.zeros((1, lanes), F32)
    for m in range(count):
        row = jnp.where(lane == place(m) % lanes, read(m), row)
    return (row / jnp.full((1, lanes), total, F32)).astype(BF16).astype(F32)


def rolled(row, rows):
    return pltpu.roll(
        jnp.broadcast_to(row, (rows, row.shape[1])), 0, 1, stride=1, stride_axis=0
    )


def band(row, n, half):
    distance = jnp.abs(iota((n, n), 1) - iota((n, n), 0))
    return jnp.where(distance <= half, rolled(row, n), 0.0).astype(BF16)


def dot(a, b, dims=((1,), (0,))):
    return lax.dot_general(a, b, (dims, ((), ())), preferred_element_type=F32)


def one_hot(condition):
    return jnp.where(condition, 1.0, 0.0).astype(BF16)


def slot_tables(mask_ref, owner_ref):
    device = iota((DEVS, ZB), 0)
    lane = iota((DEVS, ZB), 1)
    before_tri = one_hot(iota((ZB, ZB), 0) < iota((ZB, ZB), 1))
    count = jnp.zeros((DEVS, 1), F32)
    unit_of = [jnp.zeros((DEVS, 1), F32) for _ in range(2 * HALF)]
    for block in range(UNITS // ZB):
        tissue = jnp.where(lane % 2 == 0, mask_ref[2 * block], mask_ref[2 * block + 1])
        owner = owner_ref[0:1, block * ZB : (block + 1) * ZB]
        member = (owner == device) & (tissue > 0)
        before = dot(one_hot(member), before_tri) + count
        unit = (lane + block * ZB).astype(F32)
        for slot in range(2 * HALF):
            here = member & (before == float(slot))
            unit_of[slot] += jnp.sum(jnp.where(here, unit, 0.0), axis=1, keepdims=True)
        count += jnp.sum(jnp.where(member, 1.0, 0.0), axis=1, keepdims=True)
    over = jnp.maximum(count - HALF, 0.0)
    free = jnp.maximum(HALF - count, 0.0)
    lower = one_hot(iota((DEVS, DEVS), 1) < iota((DEVS, DEVS), 0))
    square = (DEVS, DEVS)
    starts = dot(
        lower,
        jnp.where(iota(square, 1) == 0, over, jnp.where(iota(square, 1) == 1, free, 0.0)).astype(BF16),
    )
    over_start, free_start = starts[:, 0:1], starts[:, 1:2]
    columns = jnp.zeros(square, F32)
    for i, column in enumerate([over_start, over, *unit_of[HALF:]]):
        columns = jnp.where(iota(square, 1) == i, column, columns)
    rows = columns.T
    balanced = []
    for slot in range(HALF):
        rank = free_start + (slot - count)
        filler = jnp.zeros((DEVS, 1), F32)
        for extra in range(HALF):
            match = (rows[0:1] + extra == rank) & (rows[1:2] > extra)
            filler += jnp.sum(jnp.where(match, rows[2 + extra : 3 + extra], 0.0), axis=1, keepdims=True)
        balanced.append(jnp.where(count > slot, unit_of[slot], filler))
    return balanced, unit_of[HALF:], count


def pack_kernel(
    mask_ref, px_ref, py_ref, owner_ref, est_hbm, meas_hbm, out_hbm, table_ref, count_ref,
    est_ref, meas_ref, wide, out_ref, est_sem, meas_sem, out_sem,
):
    est_copy = pltpu.make_async_copy(est_hbm, est_ref, est_sem)
    meas_copy = pltpu.make_async_copy(meas_hbm, meas_ref, meas_sem)
    est_copy.start()
    meas_copy.start()
    balanced, overflow, count = slot_tables(mask_ref, owner_ref)
    count_ref[...] = jnp.broadcast_to(count, (DEVS, TILE)).astype(I32)
    units = jnp.concatenate(balanced, axis=0).astype(I32)
    odd = units % 2 == 1
    slots = HALF * DEVS
    lane = iota((DEVS, slots), 1)
    along = jnp.zeros((DEVS, slots), F32)
    across = jnp.zeros((DEVS, slots), F32)
    for slot in range(HALF):
        mine = (lane // HALF == iota((DEVS, slots), 0)) & (lane % HALF == slot)
        along = jnp.where(mine, balanced[slot], along)
        mine = (lane % DEVS == iota((DEVS, slots), 0)) & (lane // DEVS == slot)
        across = jnp.where(mine, balanced[slot], across)
    table_ref[...] = jnp.broadcast_to(jnp.sum(along, axis=0, keepdims=True), (8, slots)).astype(I32)
    across = jnp.sum(across, axis=0, keepdims=True)
    past = jnp.concatenate(
        [jnp.where(count > HALF + i, overflow[i], -1.0) for i in range(HALF)], axis=0
    )
    again = one_hot(past == across)

    half_xy = TAPS_XY // 2
    matrix_x = band(placed_taps(lambda m: px_ref[0, m], TAPS_XY, NX, lambda m: m - half_xy), NX, half_xy)
    matrix_y = band(placed_taps(lambda m: py_ref[0, m], TAPS_XY, NY, lambda m: m - half_xy), NY, half_xy)
    pick = one_hot(units // 2 == iota((slots, NX), 1))
    picked_x = dot(pick, matrix_x).astype(BF16)
    est_copy.wait()
    narrow = []
    for plane in range(SLAB):
        along_x = dot(picked_x, est_ref[plane]).astype(BF16)
        blurred = dot(along_x, matrix_y, ((1,), (1,)))
        blurred = jnp.where(odd, blurred[:, TILE:], blurred[:, :TILE])
        narrow.append(blurred.astype(BF16))
        for slot in range(HALF):
            row = plane * HALF + slot
            wide[pl.ds(row, DEVS, stride=MSG), :] = blurred[slot * DEVS : (slot + 1) * DEVS]
    blurred = dot(again, jnp.concatenate(narrow, axis=1))
    for plane in range(SLAB):
        for slot in range(HALF):
            row = (SLAB + plane) * HALF + slot
            wide[pl.ds(row, DEVS, stride=MSG), :] = blurred[
                slot * DEVS : (slot + 1) * DEVS, plane * TILE : (plane + 1) * TILE
            ]
    meas_copy.wait()
    for plane in range(SLAB):
        seen = dot(pick, meas_ref[0, plane])
        seen = jnp.where(odd, seen[:, TILE:], seen[:, :TILE])
        for slot in range(HALF):
            row = (2 * SLAB + plane) * HALF + slot
            wide[pl.ds(row, DEVS, stride=MSG), :] = seen[slot * DEVS : (slot + 1) * DEVS]
    part = DEVS // OUT_PARTS
    copies = []
    for i in range(OUT_PARTS):
        here = pl.ds(i * part, part)
        out_ref[here] = wide[pl.ds(i * part * MSG, part * MSG), :].astype(BF16).reshape(part, MSG, TILE)
        copies.append(pltpu.make_async_copy(out_ref.at[here], out_hbm.at[here], out_sem.at[i]))
        copies[-1].start()
    for copy in copies:
        copy.wait()


def prep_kernel(pz_ref, px_ref, py_ref, forward_ref, adjoint_ref, rows_ref):
    group = SLAB * HALF
    edge = ZB // 2
    half_z = TAPS_Z // 2
    near = edge - HALF * half_z
    far = edge + HALF * half_z
    forward_ref[...] = rolled(
        placed_taps(lambda m: pz_ref[0, m], TAPS_Z, 2 * ZB, lambda m: near + HALF * m), ZB
    ).astype(BF16)
    adjoint = rolled(
        placed_taps(lambda m: pz_ref[0, m], TAPS_Z, 2 * ZB, lambda m: far - HALF * m), ZB
    ).astype(BF16)
    r = iota((ZB, ZB), 0)
    part = ZB // SLAB
    source = r % part // HALF * group + r // part * HALF + r % HALF
    adjoint_ref[...] = dot(one_hot(iota((ZB, ZB), 1) == source), adjoint).astype(BF16)
    half_xy = TAPS_XY // 2
    for view in range(VIEWS):
        rows_ref[view : view + 1, :] = placed_taps(
            lambda m: px_ref[view, m], TAPS_XY, 2 * XB, lambda m: XB // 2 + half_xy - m
        )
        rows_ref[VIEWS + view : VIEWS + view + 1, :] = placed_taps(
            lambda m: py_ref[view, m], TAPS_XY, NY, lambda m: m - half_xy
        )


def z_kernel(forward_hbm, adjoint_hbm, in_ref, back_ref, forward_ref, adjoint_ref, padded, ratio, sems):
    forward_copy = pltpu.make_async_copy(forward_hbm, forward_ref, sems.at[0])
    adjoint_copy = pltpu.make_async_copy(adjoint_hbm, adjoint_ref, sems.at[1])
    forward_copy.start()
    adjoint_copy.start()
    group = SLAB * HALF
    rows = DEVS * group
    edge = ZB // 2
    for ref in (padded, ratio):
        ref[0:edge, :] = jnp.zeros((edge, TILE), BF16)
        ref[edge + rows :, :] = jnp.zeros((edge, TILE), BF16)
    padded[edge : edge + rows, :] = in_ref[:, 0:group, :].reshape(rows, TILE)
    forward_copy.wait()
    for block in range(rows // ZB):
        own = dot(forward_ref[...], padded[block * ZB : block * ZB + 2 * ZB, :])
        seen = in_ref[block * ZB // group : (block + 1) * ZB // group, 2 * group :, :].reshape(ZB, TILE)
        ratio[edge + block * ZB : edge + (block + 1) * ZB, :] = (seen.astype(F32) / own).astype(BF16)
    part = ZB // SLAB
    adjoint_copy.wait()
    for block in range(rows // ZB):
        values = dot(adjoint_ref[...], ratio[block * ZB : block * ZB + 2 * ZB, :]).astype(BF16)
        for plane in range(SLAB):
            back_ref[plane, block * part : (block + 1) * part, :] = values[plane * part : (plane + 1) * part]


def column_kernel(me_ref, forward_ref, count_ref, in_ref, column_ref, padded):
    group = SLAB * HALF
    rows = DEVS * group
    edge = ZB // 2
    padded[0:edge, :] = jnp.zeros((edge, 2 * TILE), BF16)
    padded[edge + rows :, :] = jnp.zeros((edge, 2 * TILE), BF16)
    padded[edge : edge + rows, 0:TILE] = in_ref[:, 0:group, :].reshape(rows, TILE)
    padded[edge : edge + rows, TILE:] = in_ref[:, group : 2 * group, :].reshape(rows, TILE)
    count = count_ref[pl.ds(me_ref[0], 1), :].reshape(1, 1, TILE)
    planes = ZB // HALF
    pairs = planes // 2
    sub = iota((pairs, 8, TILE), 1)
    live = sub < count
    for block in range(rows // ZB):
        values = dot(forward_ref[...], padded[block * ZB : block * ZB + 2 * ZB, :])
        own = values[:, :TILE].reshape(pairs, 8, TILE)
        more = values[:, TILE:].reshape(pairs, 8, TILE)
        first = jnp.where(sub < HALF, own, pltpu.roll(more, HALF, 1))
        second = jnp.where(sub < HALF, pltpu.roll(own, HALF, 1), more)
        both = jnp.stack([jnp.where(live, first, 0.0), jnp.where(live, second, 0.0)], axis=1)
        column_ref[block * planes : (block + 1) * planes] = both.reshape(planes, 8, TILE).astype(BF16)


def back_kernel(
    me_ref, mask_ref, table_ref, rows_ref, in_ref, est_hbm, out_hbm,
    est_ref, padded, out_ref, est_sem, out_sems,
):
    est_copy = pltpu.make_async_copy(est_hbm.at[me_ref[0]], est_ref, est_sem)
    est_copy.start()
    edge = XB // 2
    cols = jnp.concatenate([in_ref[view] for view in range(VIEWS)], axis=1)
    units = table_ref[0:1, :]
    here = units // 2 == iota((NX, HALF * DEVS), 0)
    tile_row = iota((NX, 1), 0) // TILE
    back_z = []
    for t in range(2):
        found = dot(one_hot(here & (units % 2 == t)), cols)
        tissue = jnp.zeros((NX, 1), I32)
        for i in range(NX // TILE):
            tissue = jnp.where(tile_row == i, mask_ref[2 * i + t], tissue)
        back_z.append(jnp.where(tissue > 0, found, 1.0).astype(BF16))
    bands = []
    for view in range(VIEWS):
        bands.append(rolled(rows_ref[view : view + 1, :], XB).astype(BF16))
        matrix_y = band(rows_ref[VIEWS + view : VIEWS + view + 1, :], NY, TAPS_XY // 2)
        lanes = slice(view * TILE, (view + 1) * TILE)
        one_view = jnp.concatenate([back_z[0][:, lanes], back_z[1][:, lanes]], axis=1)
        padded[view, 0:edge, :] = jnp.zeros((edge, NY), BF16)
        padded[view, edge + NX :, :] = jnp.zeros((edge, NY), BF16)
        padded[view, edge : edge + NX, :] = dot(one_view, matrix_y).astype(BF16)
    est_copy.wait()
    writes = []
    for block in range(NX // XB):
        here = pl.ds(block * XB, XB)
        summed = jnp.zeros((XB, NY), F32)
        for view in range(VIEWS):
            summed += dot(bands[view], padded[view, block * XB : block * XB + 2 * XB, :])
        out_ref[here, :] = (est_ref[here, :].astype(F32) * summed / VIEWS).astype(BF16)
        for view in range(VIEWS):
            writes.append(
                pltpu.make_async_copy(out_ref.at[here, :], out_hbm.at[view, here, :], out_sems.at[block, view])
            )
            writes[-1].start()
    for write in writes:
        write.wait()


def call(kernel, name, out_shape, in_specs, out_specs, scratch, limit, flops, moved):
    return pl.pallas_call(
        kernel,
        out_shape=out_shape,
        in_specs=in_specs,
        out_specs=out_specs,
        scratch_shapes=scratch,
        compiler_params=pltpu.CompilerParams(vmem_limit_bytes=limit * 1024 * 1024),
        cost_estimate=pl.CostEstimate(flops=flops, bytes_accessed=moved, transcendentals=0),
        name=name,
    )


def pack(estimate, measured, psf_x, psf_y, tissue_mask, column_owner):
    return call(
        pack_kernel,
        "pack",
        (shape(DEVS, MSG, TILE), shape(8, HALF * DEVS, dtype=I32), shape(DEVS, TILE, dtype=I32)),
        [SMEM, SMEM, SMEM, VMEM, ANY, ANY],
        (ANY, VMEM, VMEM),
        [
            pltpu.VMEM((SLAB, NX, NY), BF16),
            pltpu.VMEM((1, SLAB, NX, NY), BF16),
            pltpu.VMEM((DEVS * MSG, TILE), F32),
            pltpu.VMEM((DEVS, MSG, TILE), BF16),
            pltpu.SemaphoreType.DMA,
            pltpu.SemaphoreType.DMA,
            pltpu.SemaphoreType.DMA((OUT_PARTS,)),
        ],
        WIDE_LIMIT,
        flops=2_000_000_000,
        moved=4_000_000,
    )(tissue_mask, psf_x, psf_y, column_owner.reshape(1, UNITS), estimate, measured)


def prep(psf_z, taps_x, taps_y):
    return call(
        prep_kernel,
        "prep",
        (shape(ZB, 2 * ZB), shape(ZB, 2 * ZB), shape(2 * VIEWS, NY, dtype=F32)),
        [SMEM, SMEM, SMEM],
        (VMEM, VMEM, VMEM),
        [],
        LIMIT,
        flops=1_000_000_000,
        moved=4_000_000,
    )(psf_z, taps_x, taps_y)


def z_pair(forward, adjoint, arrived):
    rows = DEVS * SLAB * HALF
    return call(
        z_kernel,
        "zpair",
        shape(VIEWS, HALF * DEVS, TILE),
        [HBM, HBM, VMEM],
        VMEM,
        [
            pltpu.VMEM((ZB, 2 * ZB), BF16),
            pltpu.VMEM((ZB, 2 * ZB), BF16),
            pltpu.VMEM((rows + ZB, TILE), BF16),
            pltpu.VMEM((rows + ZB, TILE), BF16),
            pltpu.SemaphoreType.DMA((2,)),
        ],
        LIMIT,
        flops=540_000_000,
        moved=3_000_000,
    )(forward, adjoint, arrived)


def column(space_index, forward, count, arrived):
    rows = DEVS * SLAB * HALF
    return call(
        column_kernel,
        "column",
        shape(SLAB * DEVS, 2 * HALF, TILE),
        [SMEM, VMEM, VMEM, VMEM],
        VMEM,
        [pltpu.VMEM((rows + ZB, 2 * TILE), BF16)],
        WIDE_LIMIT,
        flops=540_000_000,
        moved=3_000_000,
    )(space_index, forward, count, arrived)


def back(view_index, tissue_mask, table, rows, returned, estimate):
    return call(
        back_kernel,
        "back",
        shape(VIEWS, NX, NY),
        [SMEM, SMEM, VMEM, VMEM, VMEM, HBM],
        HBM,
        [
            pltpu.VMEM((NX, NY), BF16),
            pltpu.VMEM((VIEWS, NX + XB, NY), BF16),
            pltpu.VMEM((NX, NY), BF16),
            pltpu.SemaphoreType.DMA,
            pltpu.SemaphoreType.DMA((NX // XB, VIEWS)),
        ],
        LIMIT,
        flops=1_400_000_000,
        moved=5_000_000,
    )(view_index, tissue_mask, table, rows, returned, estimate)


def shards(estimate, measured, psf_x, psf_y, psf_z, tissue_mask, column_owner):
    message, table, count = pack(estimate, measured, psf_x, psf_y, tissue_mask, column_owner)
    arrived = lax.all_to_all(message, "space", split_axis=0, concat_axis=0, tiled=True)
    taps = lax.all_gather(jnp.concatenate([psf_x, psf_y], axis=1), "view", axis=0, tiled=True)
    forward, adjoint, rows = prep(psf_z, taps[:, :TAPS_XY], taps[:, TAPS_XY:])
    space_index = lax.axis_index("space").astype(I32).reshape(1)
    view_index = lax.axis_index("view").astype(I32).reshape(1)
    sent = z_pair(forward, adjoint, arrived)
    returned = lax.all_to_all(
        sent.reshape(VIEWS * DEVS, HALF, TILE),
        ("view", "space"),
        split_axis=0,
        concat_axis=0,
        tiled=True,
    ).reshape(VIEWS, HALF * DEVS, TILE)
    column_blur = column(space_index, forward, count, arrived)
    updated = back(view_index, tissue_mask, table, rows, returned, estimate)
    updated = lax.all_to_all(updated, "view", split_axis=0, concat_axis=0, tiled=True)
    return updated, column_blur[None]


def solution(mesh):
    placed = (
        P("space", None, None),
        P("view", "space", None, None),
        P("view", None),
        P("view", None),
        P("view", None),
        P(),
        P(),
    )
    return jax.shard_map(
        shards,
        mesh=mesh,
        in_specs=placed,
        out_specs=(P("space", None, None), P("view", None, "space", None)),
        check_vma=False,
    )
```

```python
import jax
import jax.numpy as jnp
from jax import lax
from jax.experimental import pallas as pl
from jax.experimental.pallas import tpu as pltpu
from jax.sharding import PartitionSpec as P

F32 = jnp.float32
BF16 = jnp.bfloat16
I32 = jnp.int32

VIEWS, DEVS = 4, 128
SLAB, NX, NY, TILE = 4, 512, 256, 128
UNITS = 1024
HALF = 4
MSG = 3 * SLAB * HALF
TAPS_XY, TAPS_Z = 31, 63
ZB = 256
XB = 128
WIDE_LIMIT, LIMIT = 60, 24

SMEM = pl.BlockSpec(memory_space=pltpu.SMEM)
VMEM = pl.BlockSpec(memory_space=pltpu.VMEM)
ANY = pl.BlockSpec(memory_space=pl.ANY)
HBM = pl.BlockSpec(memory_space=pltpu.HBM)


def shape(*dims, dtype=BF16):
    return jax.ShapeDtypeStruct(dims, dtype)


def iota(shape, dim):
    return lax.broadcasted_iota(I32, shape, dim)


def placed_taps(read, count, lanes, place):
    lane = iota((1, lanes), 1)
    total = read(0)
    for m in range(1, count):
        total = total + read(m)
    row = jnp.zeros((1, lanes), F32)
    for m in range(count):
        row = jnp.where(lane == place(m) % lanes, read(m), row)
    return (row / jnp.full((1, lanes), total, F32)).astype(BF16).astype(F32)


def rolled(row, rows):
    return pltpu.roll(
        jnp.broadcast_to(row, (rows, row.shape[1])), 0, 1, stride=1, stride_axis=0
    )


def band(row, n, half):
    distance = jnp.abs(iota((n, n), 1) - iota((n, n), 0))
    return jnp.where(distance <= half, rolled(row, n), 0.0).astype(BF16)


def dot(a, b, dims=((1,), (0,))):
    return lax.dot_general(a, b, (dims, ((), ())), preferred_element_type=F32)


def one_hot(condition):
    return jnp.where(condition, 1.0, 0.0).astype(BF16)


def slot_rows(mask_ref, owner_ref):
    pairs = UNITS // ZB
    square = (DEVS, TILE)
    device = iota(square, 0).astype(F32)
    w = iota((ZB, ZB), 1)
    unit = 2 * (w % TILE) + w // TILE
    deal = one_hot(iota((ZB, ZB), 0) == unit)
    owners = jnp.concatenate([owner_ref[0:1, i * ZB : (i + 1) * ZB] for i in range(pairs)] * 2, axis=0)
    owners = dot(owners.astype(F32).astype(BF16), deal)
    row = iota((ZB, ZB), 0)
    earlier = one_hot(2 * (row % TILE) + row // TILE < unit)
    sums = jnp.concatenate([earlier, jnp.ones((ZB, TILE), BF16)], axis=1)
    count = jnp.zeros(square, F32)
    owner, member, before = [], [], []
    for pair in range(pairs):
        for t in range(2):
            here = owners[pair : pair + 1, t * TILE : (t + 1) * TILE]
            owner.append(jnp.where(mask_ref[2 * pair + t] > 0, here, -1.0))
            member.append(device == owner[-1])
        found = dot(jnp.concatenate([one_hot(m) for m in member[-2:]], axis=1), sums)
        before.append(found[:, :TILE] + count)
        before.append(found[:, TILE:ZB] + count)
        count += found[:, ZB:]
    over = jnp.maximum(count - HALF, 0.0)
    free = jnp.maximum(HALF - count, 0.0)
    lower = one_hot(iota((DEVS, DEVS), 1) < iota((DEVS, DEVS), 0))
    starts = dot(lower, jnp.concatenate([over, free], axis=1).astype(BF16))
    over_start, free_start = starts[:, :TILE], starts[:, TILE:]
    free_end = free_start + free
    place = (count - free_start) * DEVS + device
    balanced, overflow = [], []
    for mine, inside, ahead in zip(owner, member, before):
        position = jnp.sum(jnp.where(inside, ahead, 0.0), axis=0, keepdims=True)
        start = jnp.sum(jnp.where(inside, over_start, 0.0), axis=0, keepdims=True)
        rank = start + position - HALF
        found = jnp.where((free_start <= rank) & (rank < free_end), place + rank * DEVS, 0.0)
        filled = jnp.sum(found, axis=0, keepdims=True)
        own = position * DEVS + mine
        balanced.append(jnp.where(mine < 0, -1.0, jnp.where(position < HALF, own, filled)))
        overflow.append(jnp.where((mine >= 0) & (position >= HALF), own - HALF * DEVS, -1.0))
    return balanced, overflow, count


def tissue_tiles(mask_ref):
    tiles = UNITS // TILE
    found = jnp.int32(0)
    chosen = [jnp.int32(0)] * (tiles // 2)
    for tile in range(tiles):
        here = mask_ref[tile] > 0
        chosen = [jnp.where(here & (found == i), tile, old) for i, old in enumerate(chosen)]
        found += here.astype(I32)
    return chosen


def pack_kernel(
    mask_ref, px_ref, py_ref, owner_ref, est_hbm, meas_hbm, out_hbm, table_ref, count_ref,
    est_ref, meas_ref, along, places, matrix_y, out_ref, est_sem, meas_sem, out_sem,
):
    est_copy = pltpu.make_async_copy(est_hbm, est_ref, est_sem)
    meas_copy = pltpu.make_async_copy(meas_hbm, meas_ref, meas_sem)
    meas_copy.start()
    est_copy.start()
    slots = HALF * DEVS
    group = SLAB * HALF
    tiles = UNITS // TILE
    balanced, overflow, count = slot_rows(mask_ref, owner_ref)
    count_ref[...] = count.astype(I32)
    table_ref[...] = jnp.concatenate(balanced, axis=0).astype(I32)
    places[...] = jnp.concatenate(balanced + overflow, axis=0)
    chosen = tissue_tiles(mask_ref)
    row_of = [pl.multiple_of(tile // 2 * TILE, TILE) for tile in chosen]
    lane_of = [pl.multiple_of(tile % 2 * TILE, TILE) for tile in chosen]
    index = iota((slots, TILE), 0).astype(F32)
    pick, pick_more = [
        jnp.concatenate([one_hot(index == places[pl.ds(first + tile, 1), :]) for tile in chosen], axis=1)
        for first in (0, tiles)
    ]
    half_xy = TAPS_XY // 2
    matrix_x = band(placed_taps(lambda m: px_ref[0, m], TAPS_XY, NX, lambda m: m - half_xy), NX, half_xy)
    matrix_y[...] = band(placed_taps(lambda m: py_ref[0, m], TAPS_XY, NY, lambda m: half_xy - m), NY, half_xy)

    block = ZB // group
    r = iota((ZB, ZB), 0)
    turn = one_hot(iota((ZB, ZB), 1) == r % group * block + r // group)
    copies = []

    def rows_of(values, i):
        return jnp.concatenate(
            [
                values[slot * DEVS + i * block : slot * DEVS + (i + 1) * block, plane * TILE : (plane + 1) * TILE]
                for plane in range(SLAB)
                for slot in range(HALF)
            ],
            axis=0,
        )

    meas_copy.wait()
    seen = jnp.concatenate(
        [
            jnp.concatenate(
                [meas_ref[0, plane, pl.ds(row, TILE), pl.ds(lane, TILE)] for plane in range(SLAB)], axis=1
            )
            for row, lane in zip(row_of, lane_of)
        ],
        axis=0,
    )
    seen = dot(pick, seen).astype(BF16)
    est_copy.wait()
    for plane in range(SLAB):
        along[plane] = dot(matrix_x, est_ref[plane]).astype(BF16)
    blurred = []
    for row, lane in zip(row_of, lane_of):
        rows = jnp.concatenate([along[plane, pl.ds(row, TILE), :] for plane in range(SLAB)], axis=0)
        tile = dot(rows, matrix_y[:, pl.ds(lane, TILE)]).astype(BF16)
        blurred.append(
            jnp.concatenate([tile[plane * TILE : (plane + 1) * TILE] for plane in range(SLAB)], axis=1)
        )
    blurred = jnp.concatenate(blurred, axis=0)
    parts = [dot(pick, blurred).astype(BF16), dot(pick_more, blurred).astype(BF16), seen]
    for i in range(DEVS // block):
        turned = dot(turn, jnp.concatenate([rows_of(part, i) for part in parts], axis=1)).astype(BF16)
        for k in range(len(parts)):
            out_ref[i * block : (i + 1) * block, k * group : (k + 1) * group, :] = turned[
                :, k * TILE : (k + 1) * TILE
            ].reshape(block, group, TILE)
        here = pl.ds(i * block, block)
        copies.append(pltpu.make_async_copy(out_ref.at[here], out_hbm.at[here], out_sem.at[i]))
        copies[-1].start()
    for copy in copies:
        copy.wait()


def prep_kernel(pz_ref, px_ref, py_ref, table_ref, forward_ref, adjoint_ref, rows_ref, units_ref):
    group = SLAB * HALF
    edge = ZB // 2
    half_z = TAPS_Z // 2
    near = edge - HALF * half_z
    far = edge + HALF * half_z
    forward_ref[...] = rolled(
        placed_taps(lambda m: pz_ref[0, m], TAPS_Z, 2 * ZB, lambda m: near + HALF * m), ZB
    ).astype(BF16)
    adjoint = rolled(
        placed_taps(lambda m: pz_ref[0, m], TAPS_Z, 2 * ZB, lambda m: far - HALF * m), ZB
    ).astype(BF16)
    r = iota((ZB, ZB), 0)
    part = ZB // SLAB
    source = r % part // HALF * group + r // part * HALF + r % HALF
    adjoint_ref[...] = dot(one_hot(iota((ZB, ZB), 1) == source), adjoint).astype(BF16)
    half_xy = TAPS_XY // 2
    for view in range(VIEWS):
        rows_ref[view : view + 1, :] = placed_taps(
            lambda m: px_ref[view, m], TAPS_XY, 2 * XB, lambda m: XB // 2 + half_xy - m
        )
        rows_ref[VIEWS + view : VIEWS + view + 1, :] = placed_taps(
            lambda m: py_ref[view, m], TAPS_XY, NY, lambda m: m - half_xy
        )
    slots = HALF * DEVS
    tiles = UNITS // TILE
    table = table_ref[...].astype(F32)
    table = jnp.concatenate([table] * (TILE // tiles), axis=0).T.astype(I32)
    total = jnp.zeros((1, slots), I32)
    for tile in range(tiles):
        place = table[:, tile : tile + 1]
        place = jnp.where(place < 0, -1, place % DEVS * HALF + place // DEVS)
        unit = 2 * (tile // 2 * TILE + iota((TILE, slots), 0)) + tile % 2
        total += jnp.sum(jnp.where(place == iota((TILE, slots), 1), unit, 0), axis=0, keepdims=True)
    units_ref[...] = jnp.broadcast_to(total, (8, slots))


def z_kernel(forward_ref, adjoint_ref, in_ref, back_hbm, ratio, back_ref, sems):
    group = SLAB * HALF
    rows = DEVS * group
    blocks = rows // ZB
    edge = ZB // 2
    block = ZB // group
    none = jnp.zeros((edge, TILE), BF16)

    def window(block_at):
        first, last = block_at * block - block // 2, (block_at + 1) * block + block // 2
        inner = in_ref[max(first, 0) : min(last, DEVS), 0:group, :]
        inner = inner.reshape(inner.shape[0] * group, TILE)
        return jnp.concatenate([none] * (first < 0) + [inner] + [none] * (last > DEVS), axis=0)

    ratio[0:edge, :] = none
    ratio[edge + rows :, :] = none
    for i in range(blocks // 2):
        pair = (i, i + blocks // 2)
        both = dot(forward_ref[...], jnp.concatenate([window(j) for j in pair], axis=1))
        for half, j in enumerate(pair):
            seen = in_ref[j * block : (j + 1) * block, 2 * group :, :].reshape(ZB, TILE)
            ratio[edge + j * ZB : edge + (j + 1) * ZB, :] = (
                seen.astype(F32) / both[:, half * TILE : (half + 1) * TILE]
            ).astype(BF16)
    part = ZB // SLAB
    copies = []
    for i in range(blocks // 2):
        pair = (i, i + blocks // 2)
        both = dot(
            adjoint_ref[...], jnp.concatenate([ratio[j * ZB : j * ZB + 2 * ZB, :] for j in pair], axis=1)
        ).astype(BF16)
        for half, j in enumerate(pair):
            for plane in range(SLAB):
                back_ref[plane, j * part : (j + 1) * part, :] = both[
                    plane * part : (plane + 1) * part, half * TILE : (half + 1) * TILE
                ]
        if i % 2:
            for half, j in enumerate(pair):
                here = pl.ds((j - 1) * part, 2 * part)
                copies.append(
                    pltpu.make_async_copy(back_ref.at[:, here, :], back_hbm.at[:, here, :], sems.at[i // 2, half])
                )
                copies[-1].start()
    for copy in copies:
        copy.wait()


def column_kernel(me_ref, forward_ref, count_ref, in_ref, column_ref, padded):
    group = SLAB * HALF
    rows = DEVS * group
    edge = ZB // 2
    padded[0:edge, :] = jnp.zeros((edge, 2 * TILE), BF16)
    padded[edge + rows :, :] = jnp.zeros((edge, 2 * TILE), BF16)
    padded[edge : edge + rows, 0:TILE] = in_ref[:, 0:group, :].reshape(rows, TILE)
    padded[edge : edge + rows, TILE:] = in_ref[:, group : 2 * group, :].reshape(rows, TILE)
    count = count_ref[pl.ds(me_ref[0], 1), :].reshape(1, 1, TILE)
    planes = ZB // HALF
    pairs = planes // 2
    sub = iota((pairs, 8, TILE), 1)
    live = sub < count
    for block in range(rows // ZB):
        values = dot(forward_ref[...], padded[block * ZB : block * ZB + 2 * ZB, :])
        own = values[:, :TILE].reshape(pairs, 8, TILE)
        more = values[:, TILE:].reshape(pairs, 8, TILE)
        first = jnp.where(sub < HALF, own, pltpu.roll(more, HALF, 1))
        second = jnp.where(sub < HALF, pltpu.roll(own, HALF, 1), more)
        both = jnp.stack([jnp.where(live, first, 0.0), jnp.where(live, second, 0.0)], axis=1)
        column_ref[block * planes : (block + 1) * planes] = both.reshape(planes, 8, TILE).astype(BF16)


def back_kernel(
    me_ref, mask_ref, units_ref, rows_ref, in_ref, est_hbm, out_hbm,
    est_ref, back_z, padded, out_ref, est_sem, out_sems,
):
    est_copy = pltpu.make_async_copy(est_hbm.at[me_ref[0]], est_ref, est_sem)
    est_copy.start()
    edge = XB // 2
    cols = jnp.concatenate([in_ref[view] for view in range(VIEWS)], axis=1)
    units = units_ref[0:1, :]
    slots = HALF * DEVS
    chosen = tissue_tiles(mask_ref)
    here = [units == 2 * (tile // 2 * TILE + iota((TILE, slots), 0)) + tile % 2 for tile in chosen]
    found = dot(jnp.concatenate([one_hot(h) for h in here], axis=0), cols).astype(BF16)
    back_z[...] = jnp.ones((VIEWS, NX, NY), BF16)
    for i, tile in enumerate(chosen):
        row = pl.multiple_of(tile // 2 * TILE, TILE)
        lane = pl.multiple_of(tile % 2 * TILE, TILE)
        for view in range(VIEWS):
            back_z[view, pl.ds(row, TILE), pl.ds(lane, TILE)] = found[
                i * TILE : (i + 1) * TILE, view * TILE : (view + 1) * TILE
            ]
    bands = []
    for view in range(VIEWS):
        bands.append(rolled(rows_ref[view : view + 1, :], XB).astype(BF16))
        matrix_y = band(rows_ref[VIEWS + view : VIEWS + view + 1, :], NY, TAPS_XY // 2)
        padded[view, 0:edge, :] = jnp.zeros((edge, NY), BF16)
        padded[view, edge + NX :, :] = jnp.zeros((edge, NY), BF16)
        padded[view, edge : edge + NX, :] = dot(back_z[view], matrix_y).astype(BF16)
    est_copy.wait()
    writes = []
    for block in range(NX // XB):
        here = pl.ds(block * XB, XB)
        summed = jnp.zeros((XB, NY), F32)
        for view in range(VIEWS):
            summed += dot(bands[view], padded[view, block * XB : block * XB + 2 * XB, :])
        out_ref[here, :] = (est_ref[here, :].astype(F32) * summed / VIEWS).astype(BF16)
        for view in range(VIEWS):
            writes.append(
                pltpu.make_async_copy(out_ref.at[here, :], out_hbm.at[view, here, :], out_sems.at[block, view])
            )
            writes[-1].start()
    for write in writes:
        write.wait()


def call(kernel, name, out_shape, in_specs, out_specs, scratch, limit, flops, moved):
    return pl.pallas_call(
        kernel,
        out_shape=out_shape,
        in_specs=in_specs,
        out_specs=out_specs,
        scratch_shapes=scratch,
        compiler_params=pltpu.CompilerParams(vmem_limit_bytes=limit * 1024 * 1024),
        cost_estimate=pl.CostEstimate(flops=flops, bytes_accessed=moved, transcendentals=0),
        name=name,
    )


def pack(estimate, measured, psf_x, psf_y, tissue_mask, column_owner):
    return call(
        pack_kernel,
        "pack",
        (shape(DEVS, MSG, TILE), shape(UNITS // TILE, TILE, dtype=I32), shape(DEVS, TILE, dtype=I32)),
        [SMEM, SMEM, SMEM, VMEM, ANY, ANY],
        (ANY, VMEM, VMEM),
        [
            pltpu.VMEM((SLAB, NX, NY), BF16),
            pltpu.VMEM((1, SLAB, NX, NY), BF16),
            pltpu.VMEM((SLAB, NX, NY), BF16),
            pltpu.VMEM((2 * UNITS // TILE, TILE), F32),
            pltpu.VMEM((NY, NY), BF16),
            pltpu.VMEM((DEVS, MSG, TILE), BF16),
            pltpu.SemaphoreType.DMA,
            pltpu.SemaphoreType.DMA,
            pltpu.SemaphoreType.DMA((DEVS * SLAB * HALF // ZB,)),
        ],
        WIDE_LIMIT,
        flops=2_000_000_000,
        moved=4_000_000,
    )(tissue_mask, psf_x, psf_y, column_owner.reshape(1, UNITS), estimate, measured)


def prep(psf_z, taps_x, taps_y, table):
    return call(
        prep_kernel,
        "prep",
        (
            shape(ZB, 2 * ZB),
            shape(ZB, 2 * ZB),
            shape(2 * VIEWS, NY, dtype=F32),
            shape(8, HALF * DEVS, dtype=I32),
        ),
        [SMEM, SMEM, SMEM, VMEM],
        (VMEM,) * 4,
        [],
        LIMIT,
        flops=1_000_000_000,
        moved=4_000_000,
    )(psf_z, taps_x, taps_y, table)


def z_pair(forward, adjoint, arrived):
    rows = DEVS * SLAB * HALF
    return call(
        z_kernel,
        "zpair",
        shape(VIEWS, HALF * DEVS, TILE),
        [VMEM, VMEM, VMEM],
        ANY,
        [
            pltpu.VMEM((rows + ZB, TILE), BF16),
            pltpu.VMEM((VIEWS, HALF * DEVS, TILE), BF16),
            pltpu.SemaphoreType.DMA((rows // ZB // 4, 2)),
        ],
        LIMIT,
        flops=540_000_000,
        moved=3_000_000,
    )(forward, adjoint, arrived)


def column(space_index, forward, count, arrived):
    rows = DEVS * SLAB * HALF
    return call(
        column_kernel,
        "column",
        shape(SLAB * DEVS, 2 * HALF, TILE),
        [SMEM, VMEM, VMEM, VMEM],
        VMEM,
        [pltpu.VMEM((rows + ZB, 2 * TILE), BF16)],
        WIDE_LIMIT,
        flops=540_000_000,
        moved=3_000_000,
    )(space_index, forward, count, arrived)


def back(view_index, tissue_mask, units, rows, returned, estimate):
    return call(
        back_kernel,
        "back",
        shape(VIEWS, NX, NY),
        [SMEM, SMEM, VMEM, VMEM, VMEM, HBM],
        HBM,
        [
            pltpu.VMEM((NX, NY), BF16),
            pltpu.VMEM((VIEWS, NX, NY), BF16),
            pltpu.VMEM((VIEWS, NX + XB, NY), BF16),
            pltpu.VMEM((NX, NY), BF16),
            pltpu.SemaphoreType.DMA,
            pltpu.SemaphoreType.DMA((NX // XB, VIEWS)),
        ],
        LIMIT,
        flops=1_400_000_000,
        moved=5_000_000,
    )(view_index, tissue_mask, units, rows, returned, estimate)


def shards(estimate, measured, psf_x, psf_y, psf_z, tissue_mask, column_owner):
    message, table, count = pack(estimate, measured, psf_x, psf_y, tissue_mask, column_owner)
    arrived = lax.all_to_all(message, "space", split_axis=0, concat_axis=0, tiled=True)
    taps = lax.all_gather(jnp.concatenate([psf_x, psf_y], axis=1), "view", axis=0, tiled=True)
    forward, adjoint, rows, units = prep(psf_z, taps[:, :TAPS_XY], taps[:, TAPS_XY:], table)
    space_index = lax.axis_index("space").astype(I32).reshape(1)
    view_index = lax.axis_index("view").astype(I32).reshape(1)
    sent = z_pair(forward, adjoint, arrived)
    returned = lax.all_to_all(
        sent.reshape(VIEWS * DEVS, HALF, TILE),
        ("view", "space"),
        split_axis=0,
        concat_axis=0,
        tiled=True,
    ).reshape(VIEWS, HALF * DEVS, TILE)
    column_blur = column(space_index, forward, count, arrived)
    updated = back(view_index, tissue_mask, units, rows, returned, estimate)
    updated = lax.all_to_all(updated, "view", split_axis=0, concat_axis=0, tiled=True)
    return updated, column_blur[None]


def solution(mesh):
    placed = (
        P("space", None, None),
        P("view", "space", None, None),
        P("view", None),
        P("view", None),
        P("view", None),
        P(),
        P(),
    )
    return jax.shard_map(
        shards,
        mesh=mesh,
        in_specs=placed,
        out_specs=(P("space", None, None), P("view", None, "space", None)),
        check_vma=False,
    )
```

```python
import jax
import jax.numpy as jnp
from jax import lax
from jax.experimental import pallas as pl
from jax.experimental.pallas import tpu as pltpu
from jax.sharding import PartitionSpec as P

F32 = jnp.float32
BF16 = jnp.bfloat16
I32 = jnp.int32

VIEWS, DEVS = 4, 128
SLAB, NX, NY, TILE = 4, 512, 256, 128
UNITS = 1024
HALF = 4
MSG = 3 * SLAB * HALF
TAPS_XY, TAPS_Z = 31, 63
ZB = 256
XB = 128
WIDE_LIMIT, LIMIT = 60, 24

SMEM = pl.BlockSpec(memory_space=pltpu.SMEM)
VMEM = pl.BlockSpec(memory_space=pltpu.VMEM)
ANY = pl.BlockSpec(memory_space=pl.ANY)
HBM = pl.BlockSpec(memory_space=pltpu.HBM)


def shape(*dims, dtype=BF16):
    return jax.ShapeDtypeStruct(dims, dtype)


def iota(shape, dim):
    return lax.broadcasted_iota(I32, shape, dim)


def placed_taps(read, count, lanes, place):
    lane = iota((1, lanes), 1)
    total = read(0)
    for m in range(1, count):
        total = total + read(m)
    row = jnp.zeros((1, lanes), F32)
    for m in range(count):
        row = jnp.where(lane == place(m) % lanes, read(m), row)
    return (row / jnp.full((1, lanes), total, F32)).astype(BF16).astype(F32)


def rolled(row, rows):
    return pltpu.roll(
        jnp.broadcast_to(row, (rows, row.shape[1])), 0, 1, stride=1, stride_axis=0
    )


def band(row, n, half):
    distance = jnp.abs(iota((n, n), 1) - iota((n, n), 0))
    return jnp.where(distance <= half, rolled(row, n), 0.0).astype(BF16)


def dot(a, b, dims=((1,), (0,))):
    return lax.dot_general(a, b, (dims, ((), ())), preferred_element_type=F32)


def one_hot(condition):
    return jnp.where(condition, 1.0, 0.0).astype(BF16)


def slot_rows(mask_ref, owner_ref):
    pairs = UNITS // ZB
    square = (DEVS, TILE)
    device = iota(square, 0).astype(F32)
    w = iota((ZB, ZB), 1)
    unit = 2 * (w % TILE) + w // TILE
    deal = one_hot(iota((ZB, ZB), 0) == unit)
    owners = jnp.concatenate([owner_ref[0:1, i * ZB : (i + 1) * ZB] for i in range(pairs)] * 2, axis=0)
    owners = dot(owners.astype(F32).astype(BF16), deal)
    row = iota((ZB, ZB), 0)
    earlier = one_hot(2 * (row % TILE) + row // TILE < unit)
    sums = jnp.concatenate([earlier, jnp.ones((ZB, TILE), BF16)], axis=1)
    count = jnp.zeros(square, F32)
    owner, member, before = [], [], []
    for pair in range(pairs):
        for t in range(2):
            here = owners[pair : pair + 1, t * TILE : (t + 1) * TILE]
            owner.append(jnp.where(mask_ref[2 * pair + t] > 0, here, -1.0))
            member.append(device == owner[-1])
        found = dot(jnp.concatenate([one_hot(m) for m in member[-2:]], axis=1), sums)
        before.append(found[:, :TILE] + count)
        before.append(found[:, TILE:ZB] + count)
        count += found[:, ZB:]
    over = jnp.maximum(count - HALF, 0.0)
    free = jnp.maximum(HALF - count, 0.0)
    lower = one_hot(iota((DEVS, DEVS), 1) < iota((DEVS, DEVS), 0))
    starts = dot(lower, jnp.concatenate([over, free], axis=1).astype(BF16))
    over_start, free_start = starts[:, :TILE], starts[:, TILE:]
    free_end = free_start + free
    place = (count - free_start) * DEVS + device
    balanced, overflow = [], []
    for mine, inside, ahead in zip(owner, member, before):
        position = jnp.sum(jnp.where(inside, ahead, 0.0), axis=0, keepdims=True)
        start = jnp.sum(jnp.where(inside, over_start, 0.0), axis=0, keepdims=True)
        rank = start + position - HALF
        found = jnp.where((free_start <= rank) & (rank < free_end), place + rank * DEVS, 0.0)
        filled = jnp.sum(found, axis=0, keepdims=True)
        own = position * DEVS + mine
        balanced.append(jnp.where(mine < 0, -1.0, jnp.where(position < HALF, own, filled)))
        overflow.append(jnp.where((mine >= 0) & (position >= HALF), own - HALF * DEVS, -1.0))
    return balanced, overflow, count


def tissue_tiles(mask_ref):
    tiles = UNITS // TILE
    found = jnp.int32(0)
    chosen = [jnp.int32(0)] * (tiles // 2)
    for tile in range(tiles):
        here = mask_ref[tile] > 0
        chosen = [jnp.where(here & (found == i), tile, old) for i, old in enumerate(chosen)]
        found += here.astype(I32)
    return chosen


def pack_kernel(
    mask_hbm, px_hbm, py_hbm, owner_hbm, est_hbm, meas_hbm, out_hbm, table_hbm, count_hbm,
    mask_ref, px_ref, py_ref, owner_ref, est_ref, meas_ref, along, places, matrix_y,
    out_ref, table_ref, count_ref, sems, out_sem,
):
    reads = [
        pltpu.make_async_copy(source, target, sems.at[i])
        for i, (source, target) in enumerate(
            zip(
                (mask_hbm, owner_hbm, px_hbm, py_hbm, meas_hbm, est_hbm),
                (mask_ref, owner_ref, px_ref, py_ref, meas_ref, est_ref),
            )
        )
    ]
    for copy in reads:
        copy.start()
    meas_copy, est_copy = reads[4:]
    for copy in reads[:2]:
        copy.wait()
    slots = HALF * DEVS
    group = SLAB * HALF
    tiles = UNITS // TILE
    balanced, overflow, count = slot_rows(mask_ref, owner_ref)
    count_ref[...] = count.astype(I32)
    table_ref[...] = jnp.concatenate(balanced, axis=0).astype(I32)
    copies = [
        pltpu.make_async_copy(table_ref, table_hbm, sems.at[6]),
        pltpu.make_async_copy(count_ref, count_hbm, sems.at[7]),
    ]
    for copy in copies:
        copy.start()
    places[...] = jnp.concatenate(balanced + overflow, axis=0)
    chosen = tissue_tiles(mask_ref)
    row_of = [pl.multiple_of(tile // 2 * TILE, TILE) for tile in chosen]
    lane_of = [pl.multiple_of(tile % 2 * TILE, TILE) for tile in chosen]
    index = iota((slots, TILE), 0).astype(F32)
    pick, pick_more = [
        jnp.concatenate([one_hot(index == places[pl.ds(first + tile, 1), :]) for tile in chosen], axis=1)
        for first in (0, tiles)
    ]
    for copy in reads[2:4]:
        copy.wait()
    half_xy = TAPS_XY // 2
    matrix_x = band(placed_taps(lambda m: px_ref[0, m], TAPS_XY, NX, lambda m: m - half_xy), NX, half_xy)
    matrix_y[...] = band(placed_taps(lambda m: py_ref[0, m], TAPS_XY, NY, lambda m: half_xy - m), NY, half_xy)

    block = ZB // group
    r = iota((ZB, ZB), 0)
    turn = one_hot(iota((ZB, ZB), 1) == r % group * block + r // group)

    def rows_of(values, i):
        return jnp.concatenate(
            [
                values[slot * DEVS + i * block : slot * DEVS + (i + 1) * block, plane * TILE : (plane + 1) * TILE]
                for plane in range(SLAB)
                for slot in range(HALF)
            ],
            axis=0,
        )

    meas_copy.wait()
    seen = jnp.concatenate(
        [
            jnp.concatenate(
                [meas_ref[0, plane, pl.ds(row, TILE), pl.ds(lane, TILE)] for plane in range(SLAB)], axis=1
            )
            for row, lane in zip(row_of, lane_of)
        ],
        axis=0,
    )
    seen = dot(pick, seen).astype(BF16)
    est_copy.wait()
    for plane in range(SLAB):
        along[plane] = dot(matrix_x, est_ref[plane]).astype(BF16)
    blurred = []
    for row, lane in zip(row_of, lane_of):
        rows = jnp.concatenate([along[plane, pl.ds(row, TILE), :] for plane in range(SLAB)], axis=0)
        tile = dot(rows, matrix_y[:, pl.ds(lane, TILE)]).astype(BF16)
        blurred.append(
            jnp.concatenate([tile[plane * TILE : (plane + 1) * TILE] for plane in range(SLAB)], axis=1)
        )
    blurred = jnp.concatenate(blurred, axis=0)
    parts = [dot(pick, blurred).astype(BF16), dot(pick_more, blurred).astype(BF16), seen]
    for i in range(DEVS // block):
        turned = dot(turn, jnp.concatenate([rows_of(part, i) for part in parts], axis=1)).astype(BF16)
        for k in range(len(parts)):
            out_ref[i * block : (i + 1) * block, k * group : (k + 1) * group, :] = turned[
                :, k * TILE : (k + 1) * TILE
            ].reshape(block, group, TILE)
        here = pl.ds(i * block, block)
        copies.append(pltpu.make_async_copy(out_ref.at[here], out_hbm.at[here], out_sem.at[i]))
        copies[-1].start()
    for copy in copies:
        copy.wait()


def prep_kernel(pz_ref, px_ref, py_ref, table_ref, forward_ref, adjoint_ref, rows_ref, units_ref):
    group = SLAB * HALF
    edge = ZB // 2
    half_z = TAPS_Z // 2
    near = edge - HALF * half_z
    far = edge + HALF * half_z
    forward_ref[...] = rolled(
        placed_taps(lambda m: pz_ref[0, m], TAPS_Z, 2 * ZB, lambda m: near + HALF * m), ZB
    ).astype(BF16)
    adjoint = rolled(
        placed_taps(lambda m: pz_ref[0, m], TAPS_Z, 2 * ZB, lambda m: far - HALF * m), ZB
    ).astype(BF16)
    r = iota((ZB, ZB), 0)
    part = ZB // SLAB
    source = r % part // HALF * group + r // part * HALF + r % HALF
    adjoint_ref[...] = dot(one_hot(iota((ZB, ZB), 1) == source), adjoint).astype(BF16)
    half_xy = TAPS_XY // 2
    for view in range(VIEWS):
        rows_ref[view : view + 1, :] = placed_taps(
            lambda m: px_ref[view, m], TAPS_XY, 2 * XB, lambda m: XB // 2 + half_xy - m
        )
        rows_ref[VIEWS + view : VIEWS + view + 1, :] = placed_taps(
            lambda m: py_ref[view, m], TAPS_XY, NY, lambda m: m - half_xy
        )
    slots = HALF * DEVS
    tiles = UNITS // TILE
    table = table_ref[...].astype(F32)
    table = jnp.concatenate([table] * (TILE // tiles), axis=0).T.astype(I32)
    total = jnp.zeros((1, slots), I32)
    for tile in range(tiles):
        place = table[:, tile : tile + 1]
        place = jnp.where(place < 0, -1, place % DEVS * HALF + place // DEVS)
        unit = 2 * (tile // 2 * TILE + iota((TILE, slots), 0)) + tile % 2
        total += jnp.sum(jnp.where(place == iota((TILE, slots), 1), unit, 0), axis=0, keepdims=True)
    units_ref[...] = jnp.broadcast_to(total, (8, slots))


def z_kernel(forward_ref, adjoint_ref, in_ref, back_hbm, ratio, back_ref, sems):
    group = SLAB * HALF
    rows = DEVS * group
    blocks = rows // ZB
    edge = ZB // 2
    block = ZB // group
    none = jnp.zeros((edge, TILE), BF16)

    def window(block_at):
        first, last = block_at * block - block // 2, (block_at + 1) * block + block // 2
        inner = in_ref[max(first, 0) : min(last, DEVS), 0:group, :]
        inner = inner.reshape(inner.shape[0] * group, TILE)
        return jnp.concatenate([none] * (first < 0) + [inner] + [none] * (last > DEVS), axis=0)

    ratio[0:edge, :] = none
    ratio[edge + rows :, :] = none
    for i in range(blocks // 2):
        pair = (i, i + blocks // 2)
        both = dot(forward_ref[...], jnp.concatenate([window(j) for j in pair], axis=1))
        for half, j in enumerate(pair):
            seen = in_ref[j * block : (j + 1) * block, 2 * group :, :].reshape(ZB, TILE)
            ratio[edge + j * ZB : edge + (j + 1) * ZB, :] = (
                seen.astype(F32) / both[:, half * TILE : (half + 1) * TILE]
            ).astype(BF16)
    part = ZB // SLAB
    copies = []
    for i in range(blocks // 2):
        pair = (i, i + blocks // 2)
        both = dot(
            adjoint_ref[...], jnp.concatenate([ratio[j * ZB : j * ZB + 2 * ZB, :] for j in pair], axis=1)
        ).astype(BF16)
        for half, j in enumerate(pair):
            for plane in range(SLAB):
                back_ref[plane, j * part : (j + 1) * part, :] = both[
                    plane * part : (plane + 1) * part, half * TILE : (half + 1) * TILE
                ]
        if i % 2:
            for half, j in enumerate(pair):
                here = pl.ds((j - 1) * part, 2 * part)
                copies.append(
                    pltpu.make_async_copy(back_ref.at[:, here, :], back_hbm.at[:, here, :], sems.at[i // 2, half])
                )
                copies[-1].start()
    for copy in copies:
        copy.wait()


def column_kernel(forward_ref, count_ref, in_ref, column_ref, padded):
    group = SLAB * HALF
    rows = DEVS * group
    edge = ZB // 2
    padded[0:edge, :] = jnp.zeros((edge, 2 * TILE), BF16)
    padded[edge + rows :, :] = jnp.zeros((edge, 2 * TILE), BF16)
    padded[edge : edge + rows, 0:TILE] = in_ref[:, 0:group, :].reshape(rows, TILE)
    padded[edge : edge + rows, TILE:] = in_ref[:, group : 2 * group, :].reshape(rows, TILE)
    count = count_ref[pl.ds(lax.axis_index("space"), 1), :].reshape(1, 1, TILE)
    planes = ZB // HALF
    pairs = planes // 2
    sub = iota((pairs, 8, TILE), 1)
    live = sub < count
    for block in range(rows // ZB):
        values = dot(forward_ref[...], padded[block * ZB : block * ZB + 2 * ZB, :])
        own = values[:, :TILE].reshape(pairs, 8, TILE)
        more = values[:, TILE:].reshape(pairs, 8, TILE)
        first = jnp.where(sub < HALF, own, pltpu.roll(more, HALF, 1))
        second = jnp.where(sub < HALF, pltpu.roll(own, HALF, 1), more)
        both = jnp.stack([jnp.where(live, first, 0.0), jnp.where(live, second, 0.0)], axis=1)
        column_ref[block * planes : (block + 1) * planes] = both.reshape(planes, 8, TILE).astype(BF16)


def back_kernel(
    mask_hbm, units_ref, rows_ref, in_ref, est_hbm, out_hbm,
    mask_ref, est_ref, back_z, padded, out_ref, mask_sem, est_sem, out_sems,
):
    mask_copy = pltpu.make_async_copy(mask_hbm, mask_ref, mask_sem)
    est_copy = pltpu.make_async_copy(est_hbm.at[lax.axis_index("view")], est_ref, est_sem)
    mask_copy.start()
    est_copy.start()
    edge = XB // 2
    back_z[...] = jnp.ones((VIEWS, NX, NY), BF16)
    bands, matrix_y = [], []
    for view in range(VIEWS):
        bands.append(rolled(rows_ref[view : view + 1, :], XB).astype(BF16))
        matrix_y.append(band(rows_ref[VIEWS + view : VIEWS + view + 1, :], NY, TAPS_XY // 2))
        padded[view, 0:edge, :] = jnp.zeros((edge, NY), BF16)
        padded[view, edge + NX :, :] = jnp.zeros((edge, NY), BF16)
    cols = jnp.concatenate([in_ref[view] for view in range(VIEWS)], axis=1)
    units = units_ref[0:1, :]
    slots = HALF * DEVS
    mask_copy.wait()
    chosen = tissue_tiles(mask_ref)
    here = [units == 2 * (tile // 2 * TILE + iota((TILE, slots), 0)) + tile % 2 for tile in chosen]
    found = dot(jnp.concatenate([one_hot(h) for h in here], axis=0), cols).astype(BF16)
    for i, tile in enumerate(chosen):
        row = pl.multiple_of(tile // 2 * TILE, TILE)
        lane = pl.multiple_of(tile % 2 * TILE, TILE)
        for view in range(VIEWS):
            back_z[view, pl.ds(row, TILE), pl.ds(lane, TILE)] = found[
                i * TILE : (i + 1) * TILE, view * TILE : (view + 1) * TILE
            ]
    for view in range(VIEWS):
        padded[view, edge : edge + NX, :] = dot(back_z[view], matrix_y[view]).astype(BF16)
    est_copy.wait()
    writes = []
    for block in range(NX // XB):
        here = pl.ds(block * XB, XB)
        summed = jnp.zeros((XB, NY), F32)
        for view in range(VIEWS):
            summed += dot(bands[view], padded[view, block * XB : block * XB + 2 * XB, :])
        out_ref[here, :] = (est_ref[here, :].astype(F32) * summed / VIEWS).astype(BF16)
        for view in range(VIEWS):
            writes.append(
                pltpu.make_async_copy(out_ref.at[here, :], out_hbm.at[view, here, :], out_sems.at[block, view])
            )
            writes[-1].start()
    for write in writes:
        write.wait()


def call(kernel, name, out_shape, in_specs, out_specs, scratch, limit, flops, moved):
    return pl.pallas_call(
        kernel,
        out_shape=out_shape,
        in_specs=in_specs,
        out_specs=out_specs,
        scratch_shapes=scratch,
        compiler_params=pltpu.CompilerParams(vmem_limit_bytes=limit * 1024 * 1024),
        cost_estimate=pl.CostEstimate(flops=flops, bytes_accessed=moved, transcendentals=0),
        name=name,
    )


def pack(estimate, measured, psf_x, psf_y, tissue_mask, column_owner):
    return call(
        pack_kernel,
        "pack",
        (shape(DEVS, MSG, TILE), shape(UNITS // TILE, TILE, dtype=I32), shape(DEVS, TILE, dtype=I32)),
        [ANY] * 6,
        (ANY, ANY, ANY),
        [
            pltpu.SMEM((UNITS // TILE,), I32),
            pltpu.SMEM((1, TAPS_XY), F32),
            pltpu.SMEM((1, TAPS_XY), F32),
            pltpu.VMEM((1, UNITS), I32),
            pltpu.VMEM((SLAB, NX, NY), BF16),
            pltpu.VMEM((1, SLAB, NX, NY), BF16),
            pltpu.VMEM((SLAB, NX, NY), BF16),
            pltpu.VMEM((2 * UNITS // TILE, TILE), F32),
            pltpu.VMEM((NY, NY), BF16),
            pltpu.VMEM((DEVS, MSG, TILE), BF16),
            pltpu.VMEM((UNITS // TILE, TILE), I32),
            pltpu.VMEM((DEVS, TILE), I32),
            pltpu.SemaphoreType.DMA((8,)),
            pltpu.SemaphoreType.DMA((DEVS * SLAB * HALF // ZB,)),
        ],
        WIDE_LIMIT,
        flops=2_000_000_000,
        moved=4_000_000,
    )(tissue_mask, psf_x, psf_y, column_owner.reshape(1, UNITS), estimate, measured)


def prep(psf_z, taps_x, taps_y, table):
    return call(
        prep_kernel,
        "prep",
        (
            shape(ZB, 2 * ZB),
            shape(ZB, 2 * ZB),
            shape(2 * VIEWS, NY, dtype=F32),
            shape(8, HALF * DEVS, dtype=I32),
        ),
        [SMEM, SMEM, SMEM, VMEM],
        (VMEM,) * 4,
        [],
        LIMIT,
        flops=1_000_000_000,
        moved=4_000_000,
    )(psf_z, taps_x, taps_y, table)


def z_pair(forward, adjoint, arrived):
    rows = DEVS * SLAB * HALF
    return call(
        z_kernel,
        "zpair",
        shape(VIEWS, HALF * DEVS, TILE),
        [VMEM, VMEM, VMEM],
        ANY,
        [
            pltpu.VMEM((rows + ZB, TILE), BF16),
            pltpu.VMEM((VIEWS, HALF * DEVS, TILE), BF16),
            pltpu.SemaphoreType.DMA((rows // ZB // 4, 2)),
        ],
        LIMIT,
        flops=540_000_000,
        moved=3_000_000,
    )(forward, adjoint, arrived)


def column(forward, count, arrived):
    rows = DEVS * SLAB * HALF
    return call(
        column_kernel,
        "column",
        shape(SLAB * DEVS, 2 * HALF, TILE),
        [VMEM, VMEM, VMEM],
        VMEM,
        [pltpu.VMEM((rows + ZB, 2 * TILE), BF16)],
        WIDE_LIMIT,
        flops=540_000_000,
        moved=3_000_000,
    )(forward, count, arrived)


def back(tissue_mask, units, rows, returned, estimate):
    return call(
        back_kernel,
        "back",
        shape(VIEWS, NX, NY),
        [ANY, VMEM, VMEM, VMEM, HBM],
        HBM,
        [
            pltpu.SMEM((UNITS // TILE,), I32),
            pltpu.VMEM((NX, NY), BF16),
            pltpu.VMEM((VIEWS, NX, NY), BF16),
            pltpu.VMEM((VIEWS, NX + XB, NY), BF16),
            pltpu.VMEM((NX, NY), BF16),
            pltpu.SemaphoreType.DMA,
            pltpu.SemaphoreType.DMA,
            pltpu.SemaphoreType.DMA((NX // XB, VIEWS)),
        ],
        LIMIT,
        flops=1_400_000_000,
        moved=5_000_000,
    )(tissue_mask, units, rows, returned, estimate)


def shards(estimate, measured, psf_x, psf_y, psf_z, tissue_mask, column_owner):
    message, table, count = pack(estimate, measured, psf_x, psf_y, tissue_mask, column_owner)
    arrived = lax.all_to_all(message, "space", split_axis=0, concat_axis=0, tiled=True)
    taps = lax.all_gather(jnp.concatenate([psf_x, psf_y], axis=1), "view", axis=0, tiled=True)
    forward, adjoint, rows, units = prep(psf_z, taps[:, :TAPS_XY], taps[:, TAPS_XY:], table)
    sent = z_pair(forward, adjoint, arrived)
    returned = lax.all_to_all(
        sent.reshape(VIEWS * DEVS, HALF, TILE),
        ("view", "space"),
        split_axis=0,
        concat_axis=0,
        tiled=True,
    ).reshape(VIEWS, HALF * DEVS, TILE)
    column_blur = column(forward, count, arrived)
    updated = back(tissue_mask, units, rows, returned, estimate)
    updated = lax.all_to_all(updated, "view", split_axis=0, concat_axis=0, tiled=True)
    return updated, column_blur[None]


def solution(mesh):
    placed = (
        P("space", None, None),
        P("view", "space", None, None),
        P("view", None),
        P("view", None),
        P("view", None),
        P(),
        P(),
    )
    return jax.shard_map(
        shards,
        mesh=mesh,
        in_specs=placed,
        out_specs=(P("space", None, None), P("view", None, "space", None)),
        check_vma=False,
    )
```

```python
import jax
import jax.numpy as jnp
from jax import lax
from jax.experimental import pallas as pl
from jax.experimental.pallas import tpu as pltpu
from jax.sharding import PartitionSpec as P

F32 = jnp.float32
BF16 = jnp.bfloat16
I32 = jnp.int32

VIEWS, DEVS = 4, 128
SLAB, NX, NY, TILE = 4, 512, 256, 128
UNITS = 1024
HALF = 4
MSG = 3 * SLAB * HALF
TAPS_XY, TAPS_Z = 31, 63
ZB = 256
XB = 128
WIDE_LIMIT, LIMIT = 60, 24

SMEM = pl.BlockSpec(memory_space=pltpu.SMEM)
VMEM = pl.BlockSpec(memory_space=pltpu.VMEM)
ANY = pl.BlockSpec(memory_space=pl.ANY)
HBM = pl.BlockSpec(memory_space=pltpu.HBM)


def shape(*dims, dtype=BF16):
    return jax.ShapeDtypeStruct(dims, dtype)


def iota(shape, dim):
    return lax.broadcasted_iota(I32, shape, dim)


def placed_taps(read, count, lanes, place):
    lane = iota((1, lanes), 1)
    total = read(0)
    for m in range(1, count):
        total = total + read(m)
    row = jnp.zeros((1, lanes), F32)
    for m in range(count):
        row = jnp.where(lane == place(m) % lanes, read(m), row)
    return (row / jnp.full((1, lanes), total, F32)).astype(BF16).astype(F32)


def rolled(row, rows):
    return pltpu.roll(
        jnp.broadcast_to(row, (rows, row.shape[1])), 0, 1, stride=1, stride_axis=0
    )


def band(row, n, half):
    distance = jnp.abs(iota((n, n), 1) - iota((n, n), 0))
    return jnp.where(distance <= half, rolled(row, n), 0.0).astype(BF16)


def dot(a, b, dims=((1,), (0,))):
    return lax.dot_general(a, b, (dims, ((), ())), preferred_element_type=F32)


def one_hot(condition):
    return jnp.where(condition, 1.0, 0.0).astype(BF16)


def slot_rows(mask_ref, owner_ref):
    pairs = UNITS // ZB
    square = (DEVS, TILE)
    device = iota(square, 0).astype(F32)
    w = iota((ZB, ZB), 1)
    unit = 2 * (w % TILE) + w // TILE
    deal = one_hot(iota((ZB, ZB), 0) == unit)
    owners = jnp.concatenate([owner_ref[0:1, i * ZB : (i + 1) * ZB] for i in range(pairs)] * 2, axis=0)
    owners = dot(owners.astype(F32).astype(BF16), deal)
    row = iota((ZB, ZB), 0)
    earlier = one_hot(2 * (row % TILE) + row // TILE < unit)
    sums = jnp.concatenate([earlier, jnp.ones((ZB, TILE), BF16)], axis=1)
    count = jnp.zeros(square, F32)
    owner, member, before = [], [], []
    for pair in range(pairs):
        for t in range(2):
            here = owners[pair : pair + 1, t * TILE : (t + 1) * TILE]
            owner.append(jnp.where(mask_ref[2 * pair + t] > 0, here, -1.0))
            member.append(device == owner[-1])
        found = dot(jnp.concatenate([one_hot(m) for m in member[-2:]], axis=1), sums)
        before.append(found[:, :TILE] + count)
        before.append(found[:, TILE:ZB] + count)
        count += found[:, ZB:]
    over = jnp.maximum(count - HALF, 0.0)
    free = jnp.maximum(HALF - count, 0.0)
    lower = one_hot(iota((DEVS, DEVS), 1) < iota((DEVS, DEVS), 0))
    starts = dot(lower, jnp.concatenate([over, free], axis=1).astype(BF16))
    over_start, free_start = starts[:, :TILE], starts[:, TILE:]
    free_end = free_start + free
    place = (count - free_start) * DEVS + device
    balanced, overflow = [], []
    for mine, inside, ahead in zip(owner, member, before):
        position = jnp.sum(jnp.where(inside, ahead, 0.0), axis=0, keepdims=True)
        start = jnp.sum(jnp.where(inside, over_start, 0.0), axis=0, keepdims=True)
        rank = start + position - HALF
        found = jnp.where((free_start <= rank) & (rank < free_end), place + rank * DEVS, 0.0)
        filled = jnp.sum(found, axis=0, keepdims=True)
        own = position * DEVS + mine
        balanced.append(jnp.where(mine < 0, -1.0, jnp.where(position < HALF, own, filled)))
        overflow.append(jnp.where((mine >= 0) & (position >= HALF), own - HALF * DEVS, -1.0))
    return balanced, overflow, count


def tissue_tiles(mask_ref):
    tiles = UNITS // TILE
    found = jnp.int32(0)
    chosen = [jnp.int32(0)] * (tiles // 2)
    for tile in range(tiles):
        here = mask_ref[tile] > 0
        chosen = [jnp.where(here & (found == i), tile, old) for i, old in enumerate(chosen)]
        found += here.astype(I32)
    return chosen


def pack_kernel(
    mask_hbm, px_hbm, py_hbm, owner_hbm, est_hbm, meas_hbm, out_hbm, table_hbm, count_hbm,
    mask_ref, px_ref, py_ref, owner_ref, est_ref, meas_ref, along, places, matrix_y,
    out_ref, table_ref, count_ref, sems, out_sem,
):
    reads = [
        pltpu.make_async_copy(source, target, sems.at[i])
        for i, (source, target) in enumerate(
            zip(
                (mask_hbm, owner_hbm, px_hbm, py_hbm, est_hbm, meas_hbm),
                (mask_ref, owner_ref, px_ref, py_ref, est_ref, meas_ref),
            )
        )
    ]
    for copy in reads:
        copy.start()
    est_copy, meas_copy = reads[4:]
    for copy in reads[:2]:
        copy.wait()
    slots = HALF * DEVS
    group = SLAB * HALF
    tiles = UNITS // TILE
    balanced, overflow, count = slot_rows(mask_ref, owner_ref)
    count_ref[...] = count.astype(I32)
    table_ref[...] = jnp.concatenate(balanced, axis=0).astype(I32)
    copies = [
        pltpu.make_async_copy(table_ref, table_hbm, sems.at[6]),
        pltpu.make_async_copy(count_ref, count_hbm, sems.at[7]),
    ]
    for copy in copies:
        copy.start()
    places[...] = jnp.concatenate(balanced + overflow, axis=0)
    for copy in reads[2:4]:
        copy.wait()
    half_xy = TAPS_XY // 2
    matrix_x = band(placed_taps(lambda m: px_ref[0, m], TAPS_XY, NX, lambda m: m - half_xy), NX, half_xy)
    matrix_y[...] = band(placed_taps(lambda m: py_ref[0, m], TAPS_XY, NY, lambda m: half_xy - m), NY, half_xy)

    est_copy.wait()
    for plane in range(SLAB):
        along[plane] = dot(matrix_x, est_ref[plane]).astype(BF16)
    chosen = tissue_tiles(mask_ref)
    row_of = [pl.multiple_of(tile // 2 * TILE, TILE) for tile in chosen]
    lane_of = [pl.multiple_of(tile % 2 * TILE, TILE) for tile in chosen]
    index = iota((slots, TILE), 0).astype(F32)
    pick, pick_more = [
        jnp.concatenate([one_hot(index == places[pl.ds(first + tile, 1), :]) for tile in chosen], axis=1)
        for first in (0, tiles)
    ]
    block = ZB // group
    r = iota((ZB, ZB), 0)
    turn = one_hot(iota((ZB, ZB), 1) == r % group * block + r // group)

    def rows_of(values, i):
        return jnp.concatenate(
            [
                values[slot * DEVS + i * block : slot * DEVS + (i + 1) * block, plane * TILE : (plane + 1) * TILE]
                for plane in range(SLAB)
                for slot in range(HALF)
            ],
            axis=0,
        )

    meas_copy.wait()
    seen = jnp.concatenate(
        [
            jnp.concatenate(
                [meas_ref[0, plane, pl.ds(row, TILE), pl.ds(lane, TILE)] for plane in range(SLAB)], axis=1
            )
            for row, lane in zip(row_of, lane_of)
        ],
        axis=0,
    )
    seen = dot(pick, seen).astype(BF16)
    blurred = []
    for row, lane in zip(row_of, lane_of):
        rows = jnp.concatenate([along[plane, pl.ds(row, TILE), :] for plane in range(SLAB)], axis=0)
        tile = dot(rows, matrix_y[:, pl.ds(lane, TILE)]).astype(BF16)
        blurred.append(
            jnp.concatenate([tile[plane * TILE : (plane + 1) * TILE] for plane in range(SLAB)], axis=1)
        )
    blurred = jnp.concatenate(blurred, axis=0)
    parts = [dot(pick, blurred).astype(BF16), dot(pick_more, blurred).astype(BF16), seen]
    for i in range(DEVS // block):
        turned = dot(turn, jnp.concatenate([rows_of(part, i) for part in parts], axis=1)).astype(BF16)
        for k in range(len(parts)):
            out_ref[i * block : (i + 1) * block, k * group : (k + 1) * group, :] = turned[
                :, k * TILE : (k + 1) * TILE
            ].reshape(block, group, TILE)
        here = pl.ds(i * block, block)
        copies.append(pltpu.make_async_copy(out_ref.at[here], out_hbm.at[here], out_sem.at[i]))
        copies[-1].start()
    for copy in copies:
        copy.wait()


def prep_kernel(pz_ref, px_ref, py_ref, table_ref, forward_ref, adjoint_ref, rows_ref, units_ref):
    group = SLAB * HALF
    edge = ZB // 2
    half_z = TAPS_Z // 2
    near = edge - HALF * half_z
    far = edge + HALF * half_z
    forward_ref[...] = rolled(
        placed_taps(lambda m: pz_ref[0, m], TAPS_Z, 2 * ZB, lambda m: near + HALF * m), ZB
    ).astype(BF16)
    adjoint = rolled(
        placed_taps(lambda m: pz_ref[0, m], TAPS_Z, 2 * ZB, lambda m: far - HALF * m), ZB
    ).astype(BF16)
    r = iota((ZB, ZB), 0)
    part = ZB // SLAB
    source = r % part // HALF * group + r // part * HALF + r % HALF
    adjoint_ref[...] = dot(one_hot(iota((ZB, ZB), 1) == source), adjoint).astype(BF16)
    half_xy = TAPS_XY // 2
    for view in range(VIEWS):
        rows_ref[view : view + 1, :] = placed_taps(
            lambda m: px_ref[view, m], TAPS_XY, 2 * XB, lambda m: XB // 2 + half_xy - m
        )
        rows_ref[VIEWS + view : VIEWS + view + 1, :] = placed_taps(
            lambda m: py_ref[view, m], TAPS_XY, NY, lambda m: m - half_xy
        )
    slots = HALF * DEVS
    tiles = UNITS // TILE
    table = table_ref[...].astype(F32)
    table = jnp.concatenate([table] * (TILE // tiles), axis=0).T.astype(I32)
    total = jnp.zeros((1, slots), I32)
    for tile in range(tiles):
        place = table[:, tile : tile + 1]
        place = jnp.where(place < 0, -1, place % DEVS * HALF + place // DEVS)
        unit = 2 * (tile // 2 * TILE + iota((TILE, slots), 0)) + tile % 2
        total += jnp.sum(jnp.where(place == iota((TILE, slots), 1), unit, 0), axis=0, keepdims=True)
    units_ref[...] = jnp.broadcast_to(total, (8, slots))


def z_kernel(forward_ref, adjoint_ref, in_ref, back_hbm, ratio, back_ref, sems):
    group = SLAB * HALF
    rows = DEVS * group
    blocks = rows // ZB
    edge = ZB // 2
    block = ZB // group
    none = jnp.zeros((edge, TILE), BF16)

    def window(block_at):
        first, last = block_at * block - block // 2, (block_at + 1) * block + block // 2
        inner = in_ref[max(first, 0) : min(last, DEVS), 0:group, :]
        inner = inner.reshape(inner.shape[0] * group, TILE)
        return jnp.concatenate([none] * (first < 0) + [inner] + [none] * (last > DEVS), axis=0)

    ratio[0:edge, :] = none
    ratio[edge + rows :, :] = none
    for i in range(blocks // 2):
        pair = (i, i + blocks // 2)
        both = dot(forward_ref[...], jnp.concatenate([window(j) for j in pair], axis=1))
        for half, j in enumerate(pair):
            seen = in_ref[j * block : (j + 1) * block, 2 * group :, :].reshape(ZB, TILE)
            ratio[edge + j * ZB : edge + (j + 1) * ZB, :] = (
                seen.astype(F32) / both[:, half * TILE : (half + 1) * TILE]
            ).astype(BF16)
    part = ZB // SLAB
    copies = []
    for i in range(blocks // 2):
        pair = (i, i + blocks // 2)
        both = dot(
            adjoint_ref[...], jnp.concatenate([ratio[j * ZB : j * ZB + 2 * ZB, :] for j in pair], axis=1)
        ).astype(BF16)
        for half, j in enumerate(pair):
            for plane in range(SLAB):
                back_ref[plane, j * part : (j + 1) * part, :] = both[
                    plane * part : (plane + 1) * part, half * TILE : (half + 1) * TILE
                ]
        if i % 2:
            for half, j in enumerate(pair):
                here = pl.ds((j - 1) * part, 2 * part)
                copies.append(
                    pltpu.make_async_copy(back_ref.at[:, here, :], back_hbm.at[:, here, :], sems.at[i // 2, half])
                )
                copies[-1].start()
    for copy in copies:
        copy.wait()


def column_kernel(forward_ref, count_ref, in_ref, column_ref, padded):
    group = SLAB * HALF
    rows = DEVS * group
    edge = ZB // 2
    padded[0:edge, :] = jnp.zeros((edge, 2 * TILE), BF16)
    padded[edge + rows :, :] = jnp.zeros((edge, 2 * TILE), BF16)
    padded[edge : edge + rows, 0:TILE] = in_ref[:, 0:group, :].reshape(rows, TILE)
    padded[edge : edge + rows, TILE:] = in_ref[:, group : 2 * group, :].reshape(rows, TILE)
    count = count_ref[pl.ds(lax.axis_index("space"), 1), :].reshape(1, 1, TILE)
    planes = ZB // HALF
    pairs = planes // 2
    sub = iota((pairs, 8, TILE), 1)
    live = sub < count
    for block in range(rows // ZB):
        values = dot(forward_ref[...], padded[block * ZB : block * ZB + 2 * ZB, :])
        own = values[:, :TILE].reshape(pairs, 8, TILE)
        more = values[:, TILE:].reshape(pairs, 8, TILE)
        first = jnp.where(sub < HALF, own, pltpu.roll(more, HALF, 1))
        second = jnp.where(sub < HALF, pltpu.roll(own, HALF, 1), more)
        both = jnp.stack([jnp.where(live, first, 0.0), jnp.where(live, second, 0.0)], axis=1)
        column_ref[block * planes : (block + 1) * planes] = both.reshape(planes, 8, TILE).astype(BF16)


def back_kernel(
    mask_hbm, units_ref, rows_ref, in_ref, est_hbm, out_ref,
    mask_ref, est_ref, back_z, padded, mask_sem, est_sem,
):
    mask_copy = pltpu.make_async_copy(mask_hbm, mask_ref, mask_sem)
    est_copy = pltpu.make_async_copy(est_hbm.at[lax.axis_index("view")], est_ref, est_sem)
    mask_copy.start()
    est_copy.start()
    edge = XB // 2
    back_z[...] = jnp.ones((VIEWS, NX, NY), BF16)
    bands, matrix_y = [], []
    for view in range(VIEWS):
        bands.append(rolled(rows_ref[view : view + 1, :], XB).astype(BF16))
        matrix_y.append(band(rows_ref[VIEWS + view : VIEWS + view + 1, :], NY, TAPS_XY // 2))
        padded[view, 0:edge, :] = jnp.zeros((edge, NY), BF16)
        padded[view, edge + NX :, :] = jnp.zeros((edge, NY), BF16)
    cols = jnp.concatenate([in_ref[view] for view in range(VIEWS)], axis=1)
    units = units_ref[0:1, :]
    slots = HALF * DEVS
    mask_copy.wait()
    chosen = tissue_tiles(mask_ref)
    here = [units == 2 * (tile // 2 * TILE + iota((TILE, slots), 0)) + tile % 2 for tile in chosen]
    found = dot(jnp.concatenate([one_hot(h) for h in here], axis=0), cols).astype(BF16)
    for i, tile in enumerate(chosen):
        row = pl.multiple_of(tile // 2 * TILE, TILE)
        lane = pl.multiple_of(tile % 2 * TILE, TILE)
        for view in range(VIEWS):
            back_z[view, pl.ds(row, TILE), pl.ds(lane, TILE)] = found[
                i * TILE : (i + 1) * TILE, view * TILE : (view + 1) * TILE
            ]
    for view in range(VIEWS):
        padded[view, edge : edge + NX, :] = dot(back_z[view], matrix_y[view]).astype(BF16)
    est_copy.wait()
    for block in range(NX // XB):
        here = pl.ds(block * XB, XB)
        summed = jnp.zeros((XB, NY), F32)
        for view in range(VIEWS):
            summed += dot(bands[view], padded[view, block * XB : block * XB + 2 * XB, :])
        updated = (est_ref[here, :].astype(F32) * summed / VIEWS).astype(BF16)
        for view in range(VIEWS):
            out_ref[view, here, :] = updated


def call(kernel, name, out_shape, in_specs, out_specs, scratch, limit, flops, moved):
    return pl.pallas_call(
        kernel,
        out_shape=out_shape,
        in_specs=in_specs,
        out_specs=out_specs,
        scratch_shapes=scratch,
        compiler_params=pltpu.CompilerParams(vmem_limit_bytes=limit * 1024 * 1024),
        cost_estimate=pl.CostEstimate(flops=flops, bytes_accessed=moved, transcendentals=0),
        name=name,
    )


def pack(estimate, measured, psf_x, psf_y, tissue_mask, column_owner):
    return call(
        pack_kernel,
        "pack",
        (shape(DEVS, MSG, TILE), shape(UNITS // TILE, TILE, dtype=I32), shape(DEVS, TILE, dtype=I32)),
        [ANY] * 6,
        (ANY, ANY, ANY),
        [
            pltpu.SMEM((UNITS // TILE,), I32),
            pltpu.SMEM((1, TAPS_XY), F32),
            pltpu.SMEM((1, TAPS_XY), F32),
            pltpu.VMEM((1, UNITS), I32),
            pltpu.VMEM((SLAB, NX, NY), BF16),
            pltpu.VMEM((1, SLAB, NX, NY), BF16),
            pltpu.VMEM((SLAB, NX, NY), BF16),
            pltpu.VMEM((2 * UNITS // TILE, TILE), F32),
            pltpu.VMEM((NY, NY), BF16),
            pltpu.VMEM((DEVS, MSG, TILE), BF16),
            pltpu.VMEM((UNITS // TILE, TILE), I32),
            pltpu.VMEM((DEVS, TILE), I32),
            pltpu.SemaphoreType.DMA((8,)),
            pltpu.SemaphoreType.DMA((DEVS * SLAB * HALF // ZB,)),
        ],
        WIDE_LIMIT,
        flops=2_000_000_000,
        moved=4_000_000,
    )(tissue_mask, psf_x, psf_y, column_owner.reshape(1, UNITS), estimate, measured)


def prep(psf_z, taps_x, taps_y, table):
    return call(
        prep_kernel,
        "prep",
        (
            shape(ZB, 2 * ZB),
            shape(ZB, 2 * ZB),
            shape(2 * VIEWS, NY, dtype=F32),
            shape(8, HALF * DEVS, dtype=I32),
        ),
        [SMEM, SMEM, SMEM, VMEM],
        (VMEM,) * 4,
        [],
        LIMIT,
        flops=1_000_000_000,
        moved=4_000_000,
    )(psf_z, taps_x, taps_y, table)


def z_pair(forward, adjoint, arrived):
    rows = DEVS * SLAB * HALF
    return call(
        z_kernel,
        "zpair",
        shape(VIEWS, HALF * DEVS, TILE),
        [VMEM, VMEM, VMEM],
        ANY,
        [
            pltpu.VMEM((rows + ZB, TILE), BF16),
            pltpu.VMEM((VIEWS, HALF * DEVS, TILE), BF16),
            pltpu.SemaphoreType.DMA((rows // ZB // 4, 2)),
        ],
        LIMIT,
        flops=540_000_000,
        moved=3_000_000,
    )(forward, adjoint, arrived)


def column(forward, count, arrived):
    rows = DEVS * SLAB * HALF
    return call(
        column_kernel,
        "column",
        shape(SLAB * DEVS, 2 * HALF, TILE),
        [VMEM, VMEM, VMEM],
        VMEM,
        [pltpu.VMEM((rows + ZB, 2 * TILE), BF16)],
        WIDE_LIMIT,
        flops=540_000_000,
        moved=3_000_000,
    )(forward, count, arrived)


def back(tissue_mask, units, rows, returned, estimate):
    return call(
        back_kernel,
        "back",
        shape(VIEWS, NX, NY),
        [ANY, VMEM, VMEM, VMEM, HBM],
        VMEM,
        [
            pltpu.SMEM((UNITS // TILE,), I32),
            pltpu.VMEM((NX, NY), BF16),
            pltpu.VMEM((VIEWS, NX, NY), BF16),
            pltpu.VMEM((VIEWS, NX + XB, NY), BF16),
            pltpu.SemaphoreType.DMA,
            pltpu.SemaphoreType.DMA,
        ],
        LIMIT,
        flops=1_400_000_000,
        moved=5_000_000,
    )(tissue_mask, units, rows, returned, estimate)


def shards(estimate, measured, psf_x, psf_y, psf_z, tissue_mask, column_owner):
    message, table, count = pack(estimate, measured, psf_x, psf_y, tissue_mask, column_owner)
    arrived = lax.all_to_all(message, "space", split_axis=0, concat_axis=0, tiled=True)
    taps = lax.all_gather(jnp.concatenate([psf_x, psf_y], axis=1), "view", axis=0, tiled=True)
    forward, adjoint, rows, units = prep(psf_z, taps[:, :TAPS_XY], taps[:, TAPS_XY:], table)
    sent = z_pair(forward, adjoint, arrived)
    returned = lax.all_to_all(
        sent.reshape(VIEWS * DEVS, HALF, TILE),
        ("view", "space"),
        split_axis=0,
        concat_axis=0,
        tiled=True,
    ).reshape(VIEWS, HALF * DEVS, TILE)
    column_blur = column(forward, count, arrived)
    updated = back(tissue_mask, units, rows, returned, estimate)
    updated = lax.all_to_all(updated, "view", split_axis=0, concat_axis=0, tiled=True)
    return updated, column_blur[None]


def solution(mesh):
    placed = (
        P("space", None, None),
        P("view", "space", None, None),
        P("view", None),
        P("view", None),
        P("view", None),
        P(),
        P(),
    )
    return jax.shard_map(
        shards,
        mesh=mesh,
        in_specs=placed,
        out_specs=(P("space", None, None), P("view", None, "space", None)),
        check_vma=False,
    )
```

```python
import jax
import jax.numpy as jnp
from jax import lax
from jax.experimental import pallas as pl
from jax.experimental.pallas import tpu as pltpu
from jax.sharding import PartitionSpec as P

F32 = jnp.float32
BF16 = jnp.bfloat16
I32 = jnp.int32

VIEWS, DEVS = 4, 128
SLAB, NX, NY, TILE = 4, 512, 256, 128
UNITS = 1024
HALF = 4
MSG = 3 * SLAB * HALF
TAPS_XY, TAPS_Z = 31, 63
ZB = 256
XB = 128
WIDE_LIMIT, LIMIT = 60, 24

SMEM = pl.BlockSpec(memory_space=pltpu.SMEM)
VMEM = pl.BlockSpec(memory_space=pltpu.VMEM)
ANY = pl.BlockSpec(memory_space=pl.ANY)
HBM = pl.BlockSpec(memory_space=pltpu.HBM)


def shape(*dims, dtype=BF16):
    return jax.ShapeDtypeStruct(dims, dtype)


def iota(shape, dim):
    return lax.broadcasted_iota(I32, shape, dim)


def placed_taps(read, count, lanes, place):
    lane = iota((1, lanes), 1)
    total = read(0)
    for m in range(1, count):
        total = total + read(m)
    row = jnp.zeros((1, lanes), F32)
    for m in range(count):
        row = jnp.where(lane == place(m) % lanes, read(m), row)
    return (row / jnp.full((1, lanes), total, F32)).astype(BF16).astype(F32)


def rolled(row, rows):
    return pltpu.roll(
        jnp.broadcast_to(row, (rows, row.shape[1])), 0, 1, stride=1, stride_axis=0
    )


def band(row, n, half):
    distance = jnp.abs(iota((n, n), 1) - iota((n, n), 0))
    return jnp.where(distance <= half, rolled(row, n), 0.0).astype(BF16)


def dot(a, b, dims=((1,), (0,))):
    return lax.dot_general(a, b, (dims, ((), ())), preferred_element_type=F32)


def one_hot(condition):
    return jnp.where(condition, 1.0, 0.0).astype(BF16)


def slot_rows(mask_ref, owner_ref):
    pairs = UNITS // ZB
    square = (DEVS, TILE)
    device = iota(square, 0).astype(F32)
    w = iota((ZB, ZB), 1)
    unit = 2 * (w % TILE) + w // TILE
    deal = one_hot(iota((ZB, ZB), 0) == unit)
    owners = jnp.concatenate([owner_ref[0:1, i * ZB : (i + 1) * ZB] for i in range(pairs)] * 2, axis=0)
    owners = dot(owners.astype(F32).astype(BF16), deal)
    row = iota((ZB, ZB), 0)
    earlier = one_hot(2 * (row % TILE) + row // TILE < unit)
    sums = jnp.concatenate([earlier, jnp.ones((ZB, TILE), BF16)], axis=1)
    count = jnp.zeros(square, F32)
    owner, member, before = [], [], []
    for pair in range(pairs):
        for t in range(2):
            here = owners[pair : pair + 1, t * TILE : (t + 1) * TILE]
            owner.append(jnp.where(mask_ref[2 * pair + t] > 0, here, -1.0))
            member.append(device == owner[-1])
        found = dot(jnp.concatenate([one_hot(m) for m in member[-2:]], axis=1), sums)
        before.append(found[:, :TILE] + count)
        before.append(found[:, TILE:ZB] + count)
        count += found[:, ZB:]
    over = jnp.maximum(count - HALF, 0.0)
    free = jnp.maximum(HALF - count, 0.0)
    lower = one_hot(iota((DEVS, DEVS), 1) < iota((DEVS, DEVS), 0))
    starts = dot(lower, jnp.concatenate([over, free], axis=1).astype(BF16))
    over_start, free_start = starts[:, :TILE], starts[:, TILE:]
    free_end = free_start + free
    place = (count - free_start) * DEVS + device
    balanced, overflow = [], []
    for mine, inside, ahead in zip(owner, member, before):
        position = jnp.sum(jnp.where(inside, ahead, 0.0), axis=0, keepdims=True)
        start = jnp.sum(jnp.where(inside, over_start, 0.0), axis=0, keepdims=True)
        rank = start + position - HALF
        found = jnp.where((free_start <= rank) & (rank < free_end), place + rank * DEVS, 0.0)
        filled = jnp.sum(found, axis=0, keepdims=True)
        own = position * DEVS + mine
        balanced.append(jnp.where(mine < 0, -1.0, jnp.where(position < HALF, own, filled)))
        overflow.append(jnp.where((mine >= 0) & (position >= HALF), own - HALF * DEVS, -1.0))
    return balanced, overflow, count


def tissue_tiles(mask_ref):
    tiles = UNITS // TILE
    found = jnp.int32(0)
    chosen = [jnp.int32(0)] * (tiles // 2)
    for tile in range(tiles):
        here = mask_ref[tile] > 0
        chosen = [jnp.where(here & (found == i), tile, old) for i, old in enumerate(chosen)]
        found += here.astype(I32)
    return chosen


def pack_kernel(
    mask_hbm, px_hbm, py_hbm, owner_hbm, est_hbm, meas_hbm, out_hbm, table_hbm, count_hbm,
    mask_ref, px_ref, py_ref, owner_ref, est_ref, meas_ref, along, places, matrix_y,
    out_ref, table_ref, count_ref, sems, out_sem,
):
    reads = [
        pltpu.make_async_copy(source, target, sems.at[i])
        for i, (source, target) in enumerate(
            zip(
                (mask_hbm, owner_hbm, px_hbm, py_hbm, est_hbm, meas_hbm),
                (mask_ref, owner_ref, px_ref, py_ref, est_ref, meas_ref),
            )
        )
    ]
    for copy in reads:
        copy.start()
    est_copy, meas_copy = reads[4:]
    for copy in reads[:2]:
        copy.wait()
    slots = HALF * DEVS
    group = SLAB * HALF
    tiles = UNITS // TILE
    balanced, overflow, count = slot_rows(mask_ref, owner_ref)
    count_ref[...] = count.astype(I32)
    table_ref[...] = jnp.concatenate(balanced, axis=0).astype(I32)
    copies = [
        pltpu.make_async_copy(table_ref, table_hbm, sems.at[6]),
        pltpu.make_async_copy(count_ref, count_hbm, sems.at[7]),
    ]
    for copy in copies:
        copy.start()
    places[...] = jnp.concatenate(balanced + overflow, axis=0)
    for copy in reads[2:4]:
        copy.wait()
    half_xy = TAPS_XY // 2
    matrix_x = band(placed_taps(lambda m: px_ref[0, m], TAPS_XY, NX, lambda m: m - half_xy), NX, half_xy)
    matrix_y[...] = band(placed_taps(lambda m: py_ref[0, m], TAPS_XY, NY, lambda m: half_xy - m), NY, half_xy)

    est_copy.wait()
    for plane in range(SLAB):
        along[plane] = dot(matrix_x, est_ref[plane]).astype(BF16)
    chosen = tissue_tiles(mask_ref)
    row_of = [pl.multiple_of(tile // 2 * TILE, TILE) for tile in chosen]
    lane_of = [pl.multiple_of(tile % 2 * TILE, TILE) for tile in chosen]
    index = iota((slots, TILE), 0).astype(F32)
    pick, pick_more = [
        jnp.concatenate([one_hot(index == places[pl.ds(first + tile, 1), :]) for tile in chosen], axis=1)
        for first in (0, tiles)
    ]
    block = ZB // group
    r = iota((ZB, ZB), 0)
    turn = one_hot(iota((ZB, ZB), 1) == r % group * block + r // group)

    def rows_of(values, i):
        return jnp.concatenate(
            [
                values[slot * DEVS + i * block : slot * DEVS + (i + 1) * block, plane * TILE : (plane + 1) * TILE]
                for plane in range(SLAB)
                for slot in range(HALF)
            ],
            axis=0,
        )

    meas_copy.wait()
    seen = jnp.concatenate(
        [
            jnp.concatenate(
                [meas_ref[0, plane, pl.ds(row, TILE), pl.ds(lane, TILE)] for plane in range(SLAB)], axis=1
            )
            for row, lane in zip(row_of, lane_of)
        ],
        axis=0,
    )
    seen = dot(pick, seen).astype(BF16)
    blurred = []
    for row, lane in zip(row_of, lane_of):
        rows = jnp.concatenate([along[plane, pl.ds(row, TILE), :] for plane in range(SLAB)], axis=0)
        tile = dot(rows, matrix_y[:, pl.ds(lane, TILE)]).astype(BF16)
        blurred.append(
            jnp.concatenate([tile[plane * TILE : (plane + 1) * TILE] for plane in range(SLAB)], axis=1)
        )
    blurred = jnp.concatenate(blurred, axis=0)
    parts = [dot(pick, blurred).astype(BF16), dot(pick_more, blurred).astype(BF16), seen]
    for i in range(DEVS // block):
        turned = dot(turn, jnp.concatenate([rows_of(part, i) for part in parts], axis=1)).astype(BF16)
        for k in range(len(parts)):
            out_ref[i * block : (i + 1) * block, k * group : (k + 1) * group, :] = turned[
                :, k * TILE : (k + 1) * TILE
            ].reshape(block, group, TILE)
        here = pl.ds(i * block, block)
        copies.append(pltpu.make_async_copy(out_ref.at[here], out_hbm.at[here], out_sem.at[i]))
        copies[-1].start()
    for copy in copies:
        copy.wait()


def prep_kernel(pz_ref, px_ref, py_ref, table_ref, forward_ref, adjoint_ref, rows_ref, units_ref):
    group = SLAB * HALF
    edge = ZB // 2
    half_z = TAPS_Z // 2
    near = edge - HALF * half_z
    far = edge + HALF * half_z
    forward_ref[...] = rolled(
        placed_taps(lambda m: pz_ref[0, m], TAPS_Z, 2 * ZB, lambda m: near + HALF * m), ZB
    ).astype(BF16)
    adjoint = rolled(
        placed_taps(lambda m: pz_ref[0, m], TAPS_Z, 2 * ZB, lambda m: far - HALF * m), ZB
    ).astype(BF16)
    r = iota((ZB, ZB), 0)
    part = ZB // SLAB
    source = r % part // HALF * group + r // part * HALF + r % HALF
    adjoint_ref[...] = dot(one_hot(iota((ZB, ZB), 1) == source), adjoint).astype(BF16)
    half_xy = TAPS_XY // 2
    for view in range(VIEWS):
        rows_ref[view : view + 1, :] = placed_taps(
            lambda m: px_ref[view, m], TAPS_XY, 2 * XB, lambda m: XB // 2 + half_xy - m
        )
        rows_ref[VIEWS + view : VIEWS + view + 1, :] = placed_taps(
            lambda m: py_ref[view, m], TAPS_XY, NY, lambda m: m - half_xy
        )
    slots = HALF * DEVS
    tiles = UNITS // TILE
    table = table_ref[...].astype(F32)
    table = jnp.concatenate([table] * (TILE // tiles), axis=0).T.astype(I32)
    total = jnp.zeros((1, slots), I32)
    for tile in range(tiles):
        place = table[:, tile : tile + 1]
        place = jnp.where(place < 0, -1, place % DEVS * HALF + place // DEVS)
        unit = 2 * (tile // 2 * TILE + iota((TILE, slots), 0)) + tile % 2
        total += jnp.sum(jnp.where(place == iota((TILE, slots), 1), unit, 0), axis=0, keepdims=True)
    units_ref[...] = jnp.broadcast_to(total, (8, slots))


def z_kernel(forward_ref, adjoint_ref, in_ref, back_hbm, ratio, back_ref, sems):
    group = SLAB * HALF
    rows = DEVS * group
    blocks = rows // ZB
    edge = ZB // 2
    block = ZB // group
    none = jnp.zeros((edge, TILE), BF16)

    def window(block_at):
        first, last = block_at * block - block // 2, (block_at + 1) * block + block // 2
        inner = in_ref[max(first, 0) : min(last, DEVS), 0:group, :]
        inner = inner.reshape(inner.shape[0] * group, TILE)
        return jnp.concatenate([none] * (first < 0) + [inner] + [none] * (last > DEVS), axis=0)

    ratio[0:edge, :] = none
    ratio[edge + rows :, :] = none
    for i in range(blocks // 2):
        pair = (i, i + blocks // 2)
        both = dot(forward_ref[...], jnp.concatenate([window(j) for j in pair], axis=1))
        for half, j in enumerate(pair):
            seen = in_ref[j * block : (j + 1) * block, 2 * group :, :].reshape(ZB, TILE)
            ratio[edge + j * ZB : edge + (j + 1) * ZB, :] = (
                seen.astype(F32) / both[:, half * TILE : (half + 1) * TILE]
            ).astype(BF16)
    part = ZB // SLAB
    copies = []
    for i in range(blocks // 2):
        pair = (i, i + blocks // 2)
        both = dot(
            adjoint_ref[...], jnp.concatenate([ratio[j * ZB : j * ZB + 2 * ZB, :] for j in pair], axis=1)
        ).astype(BF16)
        for half, j in enumerate(pair):
            for plane in range(SLAB):
                back_ref[plane, j * part : (j + 1) * part, :] = both[
                    plane * part : (plane + 1) * part, half * TILE : (half + 1) * TILE
                ]
        if i % 2:
            for half, j in enumerate(pair):
                here = pl.ds((j - 1) * part, 2 * part)
                copies.append(
                    pltpu.make_async_copy(back_ref.at[:, here, :], back_hbm.at[:, here, :], sems.at[i // 2, half])
                )
                copies[-1].start()
    for copy in copies:
        copy.wait()


def column_kernel(forward_ref, count_ref, in_ref, column_ref, padded):
    group = SLAB * HALF
    rows = DEVS * group
    edge = ZB // 2
    padded[0:edge, :] = jnp.zeros((edge, 2 * TILE), BF16)
    padded[edge + rows :, :] = jnp.zeros((edge, 2 * TILE), BF16)
    padded[edge : edge + rows, 0:TILE] = in_ref[:, 0:group, :].reshape(rows, TILE)
    padded[edge : edge + rows, TILE:] = in_ref[:, group : 2 * group, :].reshape(rows, TILE)
    count = count_ref[pl.ds(lax.axis_index("space"), 1), :].reshape(1, 1, TILE)
    planes = ZB // HALF
    pairs = planes // 2
    sub = iota((pairs, 8, TILE), 1)
    live = sub < count
    for block in range(rows // ZB):
        values = dot(forward_ref[...], padded[block * ZB : block * ZB + 2 * ZB, :])
        own = values[:, :TILE].reshape(pairs, 8, TILE)
        more = values[:, TILE:].reshape(pairs, 8, TILE)
        first = jnp.where(sub < HALF, own, pltpu.roll(more, HALF, 1))
        second = jnp.where(sub < HALF, pltpu.roll(own, HALF, 1), more)
        both = jnp.stack([jnp.where(live, first, 0.0), jnp.where(live, second, 0.0)], axis=1)
        column_ref[block * planes : (block + 1) * planes] = both.reshape(planes, 8, TILE).astype(BF16)


def back_kernel(
    mask_hbm, units_ref, rows_ref, in_ref, est_hbm, out_ref,
    mask_ref, est_ref, back_z, padded, mask_sem, est_sem,
):
    mask_copy = pltpu.make_async_copy(mask_hbm, mask_ref, mask_sem)
    est_copy = pltpu.make_async_copy(est_hbm.at[lax.axis_index("view")], est_ref, est_sem)
    mask_copy.start()
    est_copy.start()
    edge = XB // 2
    back_z[...] = jnp.ones((VIEWS, NX, NY), BF16)
    bands, matrix_y = [], []
    for view in range(VIEWS):
        bands.append(rolled(rows_ref[view : view + 1, :], XB).astype(BF16))
        matrix_y.append(band(rows_ref[VIEWS + view : VIEWS + view + 1, :], NY, TAPS_XY // 2))
        padded[view, 0:edge, :] = jnp.zeros((edge, NY), BF16)
        padded[view, edge + NX :, :] = jnp.zeros((edge, NY), BF16)
    cols = jnp.concatenate([in_ref[view] for view in range(VIEWS)], axis=1)
    units = units_ref[0:1, :]
    slots = HALF * DEVS
    mask_copy.wait()
    chosen = tissue_tiles(mask_ref)
    here = [units == 2 * (tile // 2 * TILE + iota((TILE, slots), 0)) + tile % 2 for tile in chosen]
    found = dot(jnp.concatenate([one_hot(h) for h in here], axis=0), cols).astype(BF16)
    for i, tile in enumerate(chosen):
        row = pl.multiple_of(tile // 2 * TILE, TILE)
        lane = pl.multiple_of(tile % 2 * TILE, TILE)
        for view in range(VIEWS):
            back_z[view, pl.ds(row, TILE), pl.ds(lane, TILE)] = found[
                i * TILE : (i + 1) * TILE, view * TILE : (view + 1) * TILE
            ]
    for view in range(VIEWS):
        padded[view, edge : edge + NX, :] = dot(back_z[view], matrix_y[view]).astype(BF16)
    est_copy.wait()
    for block in range(NX // XB):
        here = pl.ds(block * XB, XB)
        summed = jnp.zeros((XB, NY), F32)
        for view in range(VIEWS):
            summed += dot(bands[view], padded[view, block * XB : block * XB + 2 * XB, :])
        updated = (est_ref[here, :].astype(F32) * summed / VIEWS).astype(BF16)
        for view in range(VIEWS):
            out_ref[view, here, :] = updated


def call(kernel, name, out_shape, in_specs, out_specs, scratch, limit, flops, moved):
    return pl.pallas_call(
        kernel,
        out_shape=out_shape,
        in_specs=in_specs,
        out_specs=out_specs,
        scratch_shapes=scratch,
        compiler_params=pltpu.CompilerParams(vmem_limit_bytes=limit * 1024 * 1024),
        cost_estimate=pl.CostEstimate(flops=flops, bytes_accessed=moved, transcendentals=0),
        name=name,
    )


def pack(estimate, measured, psf_x, psf_y, tissue_mask, column_owner):
    return call(
        pack_kernel,
        "pack",
        (shape(DEVS, MSG, TILE), shape(UNITS // TILE, TILE, dtype=I32), shape(DEVS, TILE, dtype=I32)),
        [ANY] * 6,
        (ANY, ANY, ANY),
        [
            pltpu.SMEM((UNITS // TILE,), I32),
            pltpu.SMEM((1, TAPS_XY), F32),
            pltpu.SMEM((1, TAPS_XY), F32),
            pltpu.VMEM((1, UNITS), I32),
            pltpu.VMEM((SLAB, NX, NY), BF16),
            pltpu.VMEM((1, SLAB, NX, NY), BF16),
            pltpu.VMEM((SLAB, NX, NY), BF16),
            pltpu.VMEM((2 * UNITS // TILE, TILE), F32),
            pltpu.VMEM((NY, NY), BF16),
            pltpu.VMEM((DEVS, MSG, TILE), BF16),
            pltpu.VMEM((UNITS // TILE, TILE), I32),
            pltpu.VMEM((DEVS, TILE), I32),
            pltpu.SemaphoreType.DMA((8,)),
            pltpu.SemaphoreType.DMA((DEVS * SLAB * HALF // ZB,)),
        ],
        WIDE_LIMIT,
        flops=2_000_000_000,
        moved=4_000_000,
    )(tissue_mask, psf_x, psf_y, column_owner.reshape(1, UNITS), estimate, measured)


def prep(psf_z, taps_x, taps_y, table):
    return call(
        prep_kernel,
        "prep",
        (
            shape(ZB, 2 * ZB),
            shape(ZB, 2 * ZB),
            shape(2 * VIEWS, NY, dtype=F32),
            shape(8, HALF * DEVS, dtype=I32),
        ),
        [SMEM, SMEM, SMEM, VMEM],
        (VMEM,) * 4,
        [],
        LIMIT,
        flops=1_000_000_000,
        moved=4_000_000,
    )(psf_z, taps_x, taps_y, table)


def z_pair(forward, adjoint, arrived):
    rows = DEVS * SLAB * HALF
    return call(
        z_kernel,
        "zpair",
        shape(VIEWS, HALF * DEVS, TILE),
        [VMEM, VMEM, VMEM],
        ANY,
        [
            pltpu.VMEM((rows + ZB, TILE), BF16),
            pltpu.VMEM((VIEWS, HALF * DEVS, TILE), BF16),
            pltpu.SemaphoreType.DMA((rows // ZB // 4, 2)),
        ],
        LIMIT,
        flops=540_000_000,
        moved=3_000_000,
    )(forward, adjoint, arrived)


def column(forward, count, arrived):
    rows = DEVS * SLAB * HALF
    return call(
        column_kernel,
        "column",
        shape(SLAB * DEVS, 2 * HALF, TILE),
        [VMEM, VMEM, VMEM],
        VMEM,
        [pltpu.VMEM((rows + ZB, 2 * TILE), BF16)],
        LIMIT,
        flops=540_000_000,
        moved=3_000_000,
    )(forward, count, arrived)


def back(tissue_mask, units, rows, returned, estimate):
    return call(
        back_kernel,
        "back",
        shape(VIEWS, NX, NY),
        [ANY, VMEM, VMEM, VMEM, HBM],
        VMEM,
        [
            pltpu.SMEM((UNITS // TILE,), I32),
            pltpu.VMEM((NX, NY), BF16),
            pltpu.VMEM((VIEWS, NX, NY), BF16),
            pltpu.VMEM((VIEWS, NX + XB, NY), BF16),
            pltpu.SemaphoreType.DMA,
            pltpu.SemaphoreType.DMA,
        ],
        LIMIT,
        flops=1_400_000_000,
        moved=5_000_000,
    )(tissue_mask, units, rows, returned, estimate)


def shards(estimate, measured, psf_x, psf_y, psf_z, tissue_mask, column_owner):
    message, table, count = pack(estimate, measured, psf_x, psf_y, tissue_mask, column_owner)
    arrived = lax.all_to_all(message, "space", split_axis=0, concat_axis=0, tiled=True)
    taps = lax.all_gather(jnp.concatenate([psf_x, psf_y], axis=1), "view", axis=0, tiled=True)
    forward, adjoint, rows, units = prep(psf_z, taps[:, :TAPS_XY], taps[:, TAPS_XY:], table)
    sent = z_pair(forward, adjoint, arrived)
    returned = lax.all_to_all(
        sent.reshape(VIEWS * DEVS, HALF, TILE),
        ("view", "space"),
        split_axis=0,
        concat_axis=0,
        tiled=True,
    ).reshape(VIEWS, HALF * DEVS, TILE)
    returned, column_blur = lax.optimization_barrier((returned, column(forward, count, arrived)))
    updated = back(tissue_mask, units, rows, returned, estimate)
    updated = lax.all_to_all(updated, "view", split_axis=0, concat_axis=0, tiled=True)
    return updated, column_blur[None]


def solution(mesh):
    placed = (
        P("space", None, None),
        P("view", "space", None, None),
        P("view", None),
        P("view", None),
        P("view", None),
        P(),
        P(),
    )
    return jax.shard_map(
        shards,
        mesh=mesh,
        in_specs=placed,
        out_specs=(P("space", None, None), P("view", None, "space", None)),
        check_vma=False,
    )
```

```python
import jax
import jax.numpy as jnp
from jax import lax
from jax.experimental import pallas as pl
from jax.experimental.pallas import tpu as pltpu
from jax.sharding import PartitionSpec as P

F32 = jnp.float32
BF16 = jnp.bfloat16
I32 = jnp.int32

VIEWS, DEVS = 4, 128
SLAB, NX, NY, TILE = 4, 512, 256, 128
UNITS = 1024
HALF = 4
MSG = 3 * SLAB * HALF
TAPS_XY, TAPS_Z = 31, 63
ZB = 256
XB = 128
WIDE_LIMIT, LIMIT = 60, 24

SMEM = pl.BlockSpec(memory_space=pltpu.SMEM)
VMEM = pl.BlockSpec(memory_space=pltpu.VMEM)
ANY = pl.BlockSpec(memory_space=pl.ANY)


def shape(*dims, dtype=BF16):
    return jax.ShapeDtypeStruct(dims, dtype)


def iota(shape, dim):
    return lax.broadcasted_iota(I32, shape, dim)


def placed_taps(read, count, lanes, place):
    lane = iota((1, lanes), 1)
    total = read(0)
    for m in range(1, count):
        total = total + read(m)
    row = jnp.zeros((1, lanes), F32)
    for m in range(count):
        row = jnp.where(lane == place(m) % lanes, read(m), row)
    return (row / jnp.full((1, lanes), total, F32)).astype(BF16).astype(F32)


def rolled(row, rows):
    return pltpu.roll(
        jnp.broadcast_to(row, (rows, row.shape[1])), 0, 1, stride=1, stride_axis=0
    )


def band(row, n, half):
    distance = jnp.abs(iota((n, n), 1) - iota((n, n), 0))
    return jnp.where(distance <= half, rolled(row, n), 0.0).astype(BF16)


def dot(a, b, dims=((1,), (0,))):
    return lax.dot_general(a, b, (dims, ((), ())), preferred_element_type=F32)


def one_hot(condition):
    return jnp.where(condition, 1.0, 0.0).astype(BF16)


def slot_rows(mask_ref, owner_ref):
    pairs = UNITS // ZB
    square = (DEVS, TILE)
    device = iota(square, 0).astype(F32)
    w = iota((ZB, ZB), 1)
    unit = 2 * (w % TILE) + w // TILE
    deal = one_hot(iota((ZB, ZB), 0) == unit)
    owners = jnp.concatenate([owner_ref[0:1, i * ZB : (i + 1) * ZB] for i in range(pairs)] * 2, axis=0)
    owners = dot(owners.astype(F32).astype(BF16), deal)
    row = iota((ZB, ZB), 0)
    earlier = one_hot(2 * (row % TILE) + row // TILE < unit)
    sums = jnp.concatenate([earlier, jnp.ones((ZB, TILE), BF16)], axis=1)
    count = jnp.zeros(square, F32)
    owner, member, before = [], [], []
    for pair in range(pairs):
        for t in range(2):
            here = owners[pair : pair + 1, t * TILE : (t + 1) * TILE]
            owner.append(jnp.where(mask_ref[2 * pair + t] > 0, here, -1.0))
            member.append(device == owner[-1])
        found = dot(jnp.concatenate([one_hot(m) for m in member[-2:]], axis=1), sums)
        before.append(found[:, :TILE] + count)
        before.append(found[:, TILE:ZB] + count)
        count += found[:, ZB:]
    over = jnp.maximum(count - HALF, 0.0)
    free = jnp.maximum(HALF - count, 0.0)
    lower = one_hot(iota((DEVS, DEVS), 1) < iota((DEVS, DEVS), 0))
    starts = dot(lower, jnp.concatenate([over, free], axis=1).astype(BF16))
    over_start, free_start = starts[:, :TILE], starts[:, TILE:]
    free_end = free_start + free
    place = (count - free_start) * DEVS + device
    balanced, overflow = [], []
    for mine, inside, ahead in zip(owner, member, before):
        position = jnp.sum(jnp.where(inside, ahead, 0.0), axis=0, keepdims=True)
        start = jnp.sum(jnp.where(inside, over_start, 0.0), axis=0, keepdims=True)
        rank = start + position - HALF
        found = jnp.where((free_start <= rank) & (rank < free_end), place + rank * DEVS, 0.0)
        filled = jnp.sum(found, axis=0, keepdims=True)
        own = position * DEVS + mine
        balanced.append(jnp.where(mine < 0, -1.0, jnp.where(position < HALF, own, filled)))
        overflow.append(jnp.where((mine >= 0) & (position >= HALF), own - HALF * DEVS, -1.0))
    return balanced, overflow, count


def tissue_tiles(mask_ref):
    tiles = UNITS // TILE
    found = jnp.int32(0)
    chosen = [jnp.int32(0)] * (tiles // 2)
    for tile in range(tiles):
        here = mask_ref[tile] > 0
        chosen = [jnp.where(here & (found == i), tile, old) for i, old in enumerate(chosen)]
        found += here.astype(I32)
    return chosen


def pack_kernel(
    mask_hbm, px_hbm, py_hbm, pz_hbm, owner_hbm, est_hbm, meas_hbm, out_hbm, table_hbm, count_hbm, rows_hbm,
    mask_ref, px_ref, py_ref, pz_ref, owner_ref, est_ref, meas_ref, along, places, matrix_y,
    out_ref, table_ref, count_ref, rows_ref, sems, out_sem,
):
    reads = [
        pltpu.make_async_copy(source, target, sems.at[i])
        for i, (source, target) in enumerate(
            zip(
                (mask_hbm, owner_hbm, px_hbm, py_hbm, pz_hbm, est_hbm, meas_hbm),
                (mask_ref, owner_ref, px_ref, py_ref, pz_ref, est_ref, meas_ref),
            )
        )
    ]
    for copy in reads:
        copy.start()
    est_copy, meas_copy = reads[5:]
    for copy in reads[:2]:
        copy.wait()
    slots = HALF * DEVS
    group = SLAB * HALF
    tiles = UNITS // TILE
    balanced, overflow, count = slot_rows(mask_ref, owner_ref)
    count_ref[...] = count.astype(I32)
    table_ref[...] = jnp.concatenate(balanced, axis=0).astype(I32)
    places[...] = jnp.concatenate(balanced + overflow, axis=0)
    for copy in reads[2:5]:
        copy.wait()
    half_z = TAPS_Z // 2
    near = ZB // 2 - HALF * half_z
    far = ZB // 2 + HALF * half_z
    ahead = placed_taps(lambda m: pz_ref[0, m], TAPS_Z, 2 * ZB, lambda m: near + HALF * m)
    behind = placed_taps(lambda m: pz_ref[0, m], TAPS_Z, 2 * ZB, lambda m: far - HALF * m)
    rows_ref[...] = jnp.concatenate([ahead, behind] * 4, axis=0)
    copies = [
        pltpu.make_async_copy(source, target, sems.at[len(reads) + i])
        for i, (source, target) in enumerate(
            zip((table_ref, count_ref, rows_ref), (table_hbm, count_hbm, rows_hbm))
        )
    ]
    for copy in copies:
        copy.start()
    half_xy = TAPS_XY // 2
    matrix_x = band(placed_taps(lambda m: px_ref[0, m], TAPS_XY, NX, lambda m: m - half_xy), NX, half_xy)
    matrix_y[...] = band(placed_taps(lambda m: py_ref[0, m], TAPS_XY, NY, lambda m: half_xy - m), NY, half_xy)

    est_copy.wait()
    for plane in range(SLAB):
        along[plane] = dot(matrix_x, est_ref[plane]).astype(BF16)
    chosen = tissue_tiles(mask_ref)
    row_of = [pl.multiple_of(tile // 2 * TILE, TILE) for tile in chosen]
    lane_of = [pl.multiple_of(tile % 2 * TILE, TILE) for tile in chosen]
    index = iota((slots, TILE), 0).astype(F32)
    pick, pick_more = [
        jnp.concatenate([one_hot(index == places[pl.ds(first + tile, 1), :]) for tile in chosen], axis=1)
        for first in (0, tiles)
    ]
    block = ZB // group
    r = iota((ZB, ZB), 0)
    turn = one_hot(iota((ZB, ZB), 1) == r % group * block + r // group)

    def rows_of(values, i):
        return jnp.concatenate(
            [
                values[slot * DEVS + i * block : slot * DEVS + (i + 1) * block, plane * TILE : (plane + 1) * TILE]
                for plane in range(SLAB)
                for slot in range(HALF)
            ],
            axis=0,
        )

    meas_copy.wait()
    seen = jnp.concatenate(
        [
            jnp.concatenate(
                [meas_ref[0, plane, pl.ds(row, TILE), pl.ds(lane, TILE)] for plane in range(SLAB)], axis=1
            )
            for row, lane in zip(row_of, lane_of)
        ],
        axis=0,
    )
    seen = dot(pick, seen).astype(BF16)
    blurred = []
    for row, lane in zip(row_of, lane_of):
        rows = jnp.concatenate([along[plane, pl.ds(row, TILE), :] for plane in range(SLAB)], axis=0)
        tile = dot(rows, matrix_y[:, pl.ds(lane, TILE)]).astype(BF16)
        blurred.append(
            jnp.concatenate([tile[plane * TILE : (plane + 1) * TILE] for plane in range(SLAB)], axis=1)
        )
    blurred = jnp.concatenate(blurred, axis=0)
    parts = [dot(pick, blurred).astype(BF16), dot(pick_more, blurred).astype(BF16), seen]
    for i in range(DEVS // block):
        turned = dot(turn, jnp.concatenate([rows_of(part, i) for part in parts], axis=1)).astype(BF16)
        for k in range(len(parts)):
            out_ref[i * block : (i + 1) * block, k * group : (k + 1) * group, :] = turned[
                :, k * TILE : (k + 1) * TILE
            ].reshape(block, group, TILE)
        here = pl.ds(i * block, block)
        copies.append(pltpu.make_async_copy(out_ref.at[here], out_hbm.at[here], out_sem.at[i]))
        copies[-1].start()
    for copy in copies:
        copy.wait()


def prep_kernel(px_ref, py_ref, table_ref, est_hbm, rows_ref, units_ref, plane_ref, sem):
    plane_copy = pltpu.make_async_copy(est_hbm.at[lax.axis_index("view")], plane_ref, sem)
    plane_copy.start()
    half_xy = TAPS_XY // 2
    for view in range(VIEWS):
        rows_ref[view : view + 1, :] = placed_taps(
            lambda m: px_ref[view, m], TAPS_XY, 2 * XB, lambda m: XB // 2 + half_xy - m
        )
        rows_ref[VIEWS + view : VIEWS + view + 1, :] = placed_taps(
            lambda m: py_ref[view, m], TAPS_XY, NY, lambda m: m - half_xy
        )
    slots = HALF * DEVS
    tiles = UNITS // TILE
    table = table_ref[...].astype(F32)
    table = jnp.concatenate([table] * (TILE // tiles), axis=0).T.astype(I32)
    total = jnp.zeros((1, slots), I32)
    for tile in range(tiles):
        place = table[:, tile : tile + 1]
        place = jnp.where(place < 0, -1, place % DEVS * HALF + place // DEVS)
        unit = 2 * (tile // 2 * TILE + iota((TILE, slots), 0)) + tile % 2
        total += jnp.sum(jnp.where(place == iota((TILE, slots), 1), unit, 0), axis=0, keepdims=True)
    units_ref[...] = jnp.broadcast_to(total, (8, slots))
    plane_copy.wait()


def z_kernel(rows_ref, in_ref, back_ref, ratio):
    group = SLAB * HALF
    rows = DEVS * group
    blocks = rows // ZB
    edge = ZB // 2
    block = ZB // group
    none = jnp.zeros((edge, TILE), BF16)
    part = ZB // SLAB
    forward = rolled(rows_ref[0:1, :], ZB).astype(BF16)
    r = iota((ZB, ZB), 0)
    source = r % part // HALF * group + r // part * HALF + r % HALF
    adjoint = rolled(rows_ref[1:2, :], ZB).astype(BF16)
    adjoint = dot(one_hot(iota((ZB, ZB), 1) == source), adjoint).astype(BF16)

    def window(block_at):
        first, last = block_at * block - block // 2, (block_at + 1) * block + block // 2
        inner = in_ref[max(first, 0) : min(last, DEVS), 0:group, :]
        inner = inner.reshape(inner.shape[0] * group, TILE)
        return jnp.concatenate([none] * (first < 0) + [inner] + [none] * (last > DEVS), axis=0)

    ratio[0:edge, :] = none
    ratio[edge + rows :, :] = none
    for i in range(blocks // 2):
        pair = (i, i + blocks // 2)
        both = dot(forward, jnp.concatenate([window(j) for j in pair], axis=1))
        for half, j in enumerate(pair):
            seen = in_ref[j * block : (j + 1) * block, 2 * group :, :].reshape(ZB, TILE)
            ratio[edge + j * ZB : edge + (j + 1) * ZB, :] = (
                seen.astype(F32) / both[:, half * TILE : (half + 1) * TILE]
            ).astype(BF16)
    for i in range(blocks // 2):
        pair = (i, i + blocks // 2)
        both = dot(
            adjoint, jnp.concatenate([ratio[j * ZB : j * ZB + 2 * ZB, :] for j in pair], axis=1)
        ).astype(BF16)
        for half, j in enumerate(pair):
            for plane in range(SLAB):
                back_ref[plane, j * part : (j + 1) * part, :] = both[
                    plane * part : (plane + 1) * part, half * TILE : (half + 1) * TILE
                ]


def column_kernel(rows_ref, count_ref, in_ref, column_ref, padded):
    group = SLAB * HALF
    rows = DEVS * group
    edge = ZB // 2
    padded[0:edge, :] = jnp.zeros((edge, 2 * TILE), BF16)
    padded[edge + rows :, :] = jnp.zeros((edge, 2 * TILE), BF16)
    padded[edge : edge + rows, 0:TILE] = in_ref[:, 0:group, :].reshape(rows, TILE)
    padded[edge : edge + rows, TILE:] = in_ref[:, group : 2 * group, :].reshape(rows, TILE)
    count = count_ref[pl.ds(lax.axis_index("space"), 1), :].reshape(1, 1, TILE)
    forward = rolled(rows_ref[0:1, :], ZB).astype(BF16)
    planes = ZB // HALF
    pairs = planes // 2
    sub = iota((pairs, 8, TILE), 1)
    live = sub < count
    for block in range(rows // ZB):
        values = dot(forward, padded[block * ZB : block * ZB + 2 * ZB, :])
        own = values[:, :TILE].reshape(pairs, 8, TILE)
        more = values[:, TILE:].reshape(pairs, 8, TILE)
        first = jnp.where(sub < HALF, own, pltpu.roll(more, HALF, 1))
        second = jnp.where(sub < HALF, pltpu.roll(own, HALF, 1), more)
        both = jnp.stack([jnp.where(live, first, 0.0), jnp.where(live, second, 0.0)], axis=1)
        column_ref[block * planes : (block + 1) * planes] = both.reshape(planes, 8, TILE).astype(BF16)


def back_kernel(
    mask_hbm, units_ref, rows_ref, in_ref, est_ref, out_ref, mask_ref, back_z, padded, mask_sem,
):
    mask_copy = pltpu.make_async_copy(mask_hbm, mask_ref, mask_sem)
    mask_copy.start()
    edge = XB // 2
    back_z[...] = jnp.ones((VIEWS, NX, NY), BF16)
    bands, matrix_y = [], []
    for view in range(VIEWS):
        bands.append(rolled(rows_ref[view : view + 1, :], XB).astype(BF16))
        matrix_y.append(band(rows_ref[VIEWS + view : VIEWS + view + 1, :], NY, TAPS_XY // 2))
        padded[view, 0:edge, :] = jnp.zeros((edge, NY), BF16)
        padded[view, edge + NX :, :] = jnp.zeros((edge, NY), BF16)
    cols = jnp.concatenate([in_ref[view] for view in range(VIEWS)], axis=1)
    units = units_ref[0:1, :]
    slots = HALF * DEVS
    mask_copy.wait()
    chosen = tissue_tiles(mask_ref)
    here = [units == 2 * (tile // 2 * TILE + iota((TILE, slots), 0)) + tile % 2 for tile in chosen]
    found = dot(jnp.concatenate([one_hot(h) for h in here], axis=0), cols).astype(BF16)
    for i, tile in enumerate(chosen):
        row = pl.multiple_of(tile // 2 * TILE, TILE)
        lane = pl.multiple_of(tile % 2 * TILE, TILE)
        for view in range(VIEWS):
            back_z[view, pl.ds(row, TILE), pl.ds(lane, TILE)] = found[
                i * TILE : (i + 1) * TILE, view * TILE : (view + 1) * TILE
            ]
    for view in range(VIEWS):
        padded[view, edge : edge + NX, :] = dot(back_z[view], matrix_y[view]).astype(BF16)
    for block in range(NX // XB):
        here = pl.ds(block * XB, XB)
        summed = jnp.zeros((XB, NY), F32)
        for view in range(VIEWS):
            summed += dot(bands[view], padded[view, block * XB : block * XB + 2 * XB, :])
        updated = (est_ref[here, :].astype(F32) * summed / VIEWS).astype(BF16)
        for view in range(VIEWS):
            out_ref[view, here, :] = updated


def call(kernel, name, out_shape, in_specs, out_specs, scratch, limit, flops, moved):
    return pl.pallas_call(
        kernel,
        out_shape=out_shape,
        in_specs=in_specs,
        out_specs=out_specs,
        scratch_shapes=scratch,
        compiler_params=pltpu.CompilerParams(vmem_limit_bytes=limit * 1024 * 1024),
        cost_estimate=pl.CostEstimate(flops=flops, bytes_accessed=moved, transcendentals=0),
        name=name,
    )


def pack(estimate, measured, psf_x, psf_y, psf_z, tissue_mask, column_owner):
    return call(
        pack_kernel,
        "pack",
        (
            shape(DEVS, MSG, TILE),
            shape(UNITS // TILE, TILE, dtype=I32),
            shape(DEVS, TILE, dtype=I32),
            shape(8, 2 * ZB, dtype=F32),
        ),
        [ANY] * 7,
        (ANY,) * 4,
        [
            pltpu.SMEM((UNITS // TILE,), I32),
            pltpu.SMEM((1, TAPS_XY), F32),
            pltpu.SMEM((1, TAPS_XY), F32),
            pltpu.SMEM((1, TAPS_Z), F32),
            pltpu.VMEM((1, UNITS), I32),
            pltpu.VMEM((SLAB, NX, NY), BF16),
            pltpu.VMEM((1, SLAB, NX, NY), BF16),
            pltpu.VMEM((SLAB, NX, NY), BF16),
            pltpu.VMEM((2 * UNITS // TILE, TILE), F32),
            pltpu.VMEM((NY, NY), BF16),
            pltpu.VMEM((DEVS, MSG, TILE), BF16),
            pltpu.VMEM((UNITS // TILE, TILE), I32),
            pltpu.VMEM((DEVS, TILE), I32),
            pltpu.VMEM((8, 2 * ZB), F32),
            pltpu.SemaphoreType.DMA((10,)),
            pltpu.SemaphoreType.DMA((DEVS * SLAB * HALF // ZB,)),
        ],
        WIDE_LIMIT,
        flops=2_000_000_000,
        moved=4_000_000,
    )(tissue_mask, psf_x, psf_y, psf_z, column_owner.reshape(1, UNITS), estimate, measured)


def prep(taps_x, taps_y, table, estimate):
    return call(
        prep_kernel,
        "prep",
        (shape(2 * VIEWS, NY, dtype=F32), shape(8, HALF * DEVS, dtype=I32), shape(NX, NY)),
        [SMEM, SMEM, VMEM, ANY],
        (VMEM,) * 3,
        [pltpu.SemaphoreType.DMA],
        LIMIT,
        flops=10_000_000,
        moved=1_000_000,
    )(taps_x, taps_y, table, estimate)


def z_pair(rows, arrived):
    depth = DEVS * SLAB * HALF
    return call(
        z_kernel,
        "zpair",
        shape(VIEWS, HALF * DEVS, TILE),
        [VMEM, VMEM],
        VMEM,
        [pltpu.VMEM((depth + ZB, TILE), BF16)],
        LIMIT,
        flops=540_000_000,
        moved=3_000_000,
    )(rows, arrived)


def column(rows, count, arrived):
    depth = DEVS * SLAB * HALF
    return call(
        column_kernel,
        "column",
        shape(SLAB * DEVS, 2 * HALF, TILE),
        [VMEM, VMEM, VMEM],
        VMEM,
        [pltpu.VMEM((depth + ZB, 2 * TILE), BF16)],
        LIMIT,
        flops=540_000_000,
        moved=3_000_000,
    )(rows, count, arrived)


def back(tissue_mask, units, rows, returned, plane):
    return call(
        back_kernel,
        "back",
        shape(VIEWS, NX, NY),
        [ANY, VMEM, VMEM, VMEM, VMEM],
        VMEM,
        [
            pltpu.SMEM((UNITS // TILE,), I32),
            pltpu.VMEM((VIEWS, NX, NY), BF16),
            pltpu.VMEM((VIEWS, NX + XB, NY), BF16),
            pltpu.SemaphoreType.DMA,
        ],
        LIMIT,
        flops=1_400_000_000,
        moved=5_000_000,
    )(tissue_mask, units, rows, returned, plane)


def shards(estimate, measured, psf_x, psf_y, psf_z, tissue_mask, column_owner):
    message, table, count, rows_z = pack(estimate, measured, psf_x, psf_y, psf_z, tissue_mask, column_owner)
    arrived = lax.all_to_all(message, "space", split_axis=0, concat_axis=0, tiled=True)
    arrived, psf_x, psf_y = lax.optimization_barrier((arrived, psf_x, psf_y))
    sent = z_pair(rows_z, arrived)
    returned = lax.all_to_all(
        sent.reshape(VIEWS * DEVS, HALF, TILE),
        ("view", "space"),
        split_axis=0,
        concat_axis=0,
        tiled=True,
    ).reshape(VIEWS, HALF * DEVS, TILE)
    taps = lax.all_gather(jnp.concatenate([psf_x, psf_y], axis=1), "view", axis=0, tiled=True)
    rows, units, plane = prep(taps[:, :TAPS_XY], taps[:, TAPS_XY:], table, estimate)
    returned, column_blur = lax.optimization_barrier((returned, column(rows_z, count, arrived)))
    updated = back(tissue_mask, units, rows, returned, plane)
    updated = lax.all_to_all(updated, "view", split_axis=0, concat_axis=0, tiled=True)
    return updated, column_blur[None]


def solution(mesh):
    placed = (
        P("space", None, None),
        P("view", "space", None, None),
        P("view", None),
        P("view", None),
        P("view", None),
        P(),
        P(),
    )
    return jax.shard_map(
        shards,
        mesh=mesh,
        in_specs=placed,
        out_specs=(P("space", None, None), P("view", None, "space", None)),
        check_vma=False,
    )
```

```python
import jax
import jax.numpy as jnp
from jax import lax
from jax.experimental import pallas as pl
from jax.experimental.pallas import tpu as pltpu
from jax.sharding import PartitionSpec as P

F32 = jnp.float32
BF16 = jnp.bfloat16
I32 = jnp.int32

VIEWS, DEVS = 4, 128
SLAB, NX, NY, TILE = 4, 512, 256, 128
UNITS = 1024
HALF = 4
MSG = 3 * SLAB * HALF
TAPS_XY, TAPS_Z = 31, 63
ZB = 256
XB = 128
WIDE_LIMIT, LIMIT = 60, 24

SMEM = pl.BlockSpec(memory_space=pltpu.SMEM)
VMEM = pl.BlockSpec(memory_space=pltpu.VMEM)
ANY = pl.BlockSpec(memory_space=pl.ANY)


def shape(*dims, dtype=BF16):
    return jax.ShapeDtypeStruct(dims, dtype)


def iota(shape, dim):
    return lax.broadcasted_iota(I32, shape, dim)


def placed_taps(read, count, lanes, place):
    lane = iota((1, lanes), 1)
    total = read(0)
    for m in range(1, count):
        total = total + read(m)
    row = jnp.zeros((1, lanes), F32)
    for m in range(count):
        row = jnp.where(lane == place(m) % lanes, read(m), row)
    return (row / jnp.full((1, lanes), total, F32)).astype(BF16).astype(F32)


def rolled(row, rows):
    return pltpu.roll(
        jnp.broadcast_to(row, (rows, row.shape[1])), 0, 1, stride=1, stride_axis=0
    )


def band(row, n, half):
    distance = jnp.abs(iota((n, n), 1) - iota((n, n), 0))
    return jnp.where(distance <= half, rolled(row, n), 0.0).astype(BF16)


def dot(a, b, dims=((1,), (0,))):
    return lax.dot_general(a, b, (dims, ((), ())), preferred_element_type=F32)


def one_hot(condition):
    return jnp.where(condition, 1.0, 0.0).astype(BF16)


def slot_rows(mask_ref, owner_ref):
    pairs = UNITS // ZB
    square = (DEVS, TILE)
    device = iota(square, 0).astype(F32)
    w = iota((ZB, ZB), 1)
    unit = 2 * (w % TILE) + w // TILE
    deal = one_hot(iota((ZB, ZB), 0) == unit)
    owners = jnp.concatenate([owner_ref[0:1, i * ZB : (i + 1) * ZB] for i in range(pairs)] * 2, axis=0)
    owners = dot(owners.astype(F32).astype(BF16), deal)
    row = iota((ZB, ZB), 0)
    earlier = one_hot(2 * (row % TILE) + row // TILE < unit)
    sums = jnp.concatenate([earlier, jnp.ones((ZB, TILE), BF16)], axis=1)
    count = jnp.zeros(square, F32)
    owner, member, before = [], [], []
    for pair in range(pairs):
        for t in range(2):
            here = owners[pair : pair + 1, t * TILE : (t + 1) * TILE]
            owner.append(jnp.where(mask_ref[2 * pair + t] > 0, here, -1.0))
            member.append(device == owner[-1])
        found = dot(jnp.concatenate([one_hot(m) for m in member[-2:]], axis=1), sums)
        before.append(found[:, :TILE] + count)
        before.append(found[:, TILE:ZB] + count)
        count += found[:, ZB:]
    over = jnp.maximum(count - HALF, 0.0)
    free = jnp.maximum(HALF - count, 0.0)
    lower = one_hot(iota((DEVS, DEVS), 1) < iota((DEVS, DEVS), 0))
    starts = dot(lower, jnp.concatenate([over, free], axis=1).astype(BF16))
    over_start, free_start = starts[:, :TILE], starts[:, TILE:]
    free_end = free_start + free
    place = (count - free_start) * DEVS + device
    balanced, overflow = [], []
    for mine, inside, ahead in zip(owner, member, before):
        position = jnp.sum(jnp.where(inside, ahead, 0.0), axis=0, keepdims=True)
        start = jnp.sum(jnp.where(inside, over_start, 0.0), axis=0, keepdims=True)
        rank = start + position - HALF
        found = jnp.where((free_start <= rank) & (rank < free_end), place + rank * DEVS, 0.0)
        filled = jnp.sum(found, axis=0, keepdims=True)
        own = position * DEVS + mine
        balanced.append(jnp.where(mine < 0, -1.0, jnp.where(position < HALF, own, filled)))
        overflow.append(jnp.where((mine >= 0) & (position >= HALF), own - HALF * DEVS, -1.0))
    return balanced, overflow, count


def tissue_tiles(mask_ref):
    tiles = UNITS // TILE
    found = jnp.int32(0)
    chosen = [jnp.int32(0)] * (tiles // 2)
    for tile in range(tiles):
        here = mask_ref[tile] > 0
        chosen = [jnp.where(here & (found == i), tile, old) for i, old in enumerate(chosen)]
        found += here.astype(I32)
    return chosen


def pack_kernel(
    mask_hbm, px_hbm, py_hbm, owner_hbm, est_hbm, meas_hbm, out_hbm, table_hbm, count_hbm,
    mask_ref, px_ref, py_ref, owner_ref, est_ref, meas_ref, along, places, matrix_y,
    out_ref, table_ref, count_ref, sems, out_sem,
):
    reads = [
        pltpu.make_async_copy(source, target, sems.at[i])
        for i, (source, target) in enumerate(
            zip(
                (mask_hbm, owner_hbm, px_hbm, py_hbm, est_hbm, meas_hbm),
                (mask_ref, owner_ref, px_ref, py_ref, est_ref, meas_ref),
            )
        )
    ]
    for copy in reads:
        copy.start()
    est_copy, meas_copy = reads[4:]
    for copy in reads[:2]:
        copy.wait()
    slots = HALF * DEVS
    group = SLAB * HALF
    tiles = UNITS // TILE
    balanced, overflow, count = slot_rows(mask_ref, owner_ref)
    count_ref[...] = count.astype(I32)
    table_ref[...] = jnp.concatenate(balanced, axis=0).astype(I32)
    copies = [
        pltpu.make_async_copy(table_ref, table_hbm, sems.at[6]),
        pltpu.make_async_copy(count_ref, count_hbm, sems.at[7]),
    ]
    for copy in copies:
        copy.start()
    places[...] = jnp.concatenate(balanced + overflow, axis=0)
    for copy in reads[2:4]:
        copy.wait()
    half_xy = TAPS_XY // 2
    matrix_x = band(placed_taps(lambda m: px_ref[0, m], TAPS_XY, NX, lambda m: m - half_xy), NX, half_xy)
    matrix_y[...] = band(placed_taps(lambda m: py_ref[0, m], TAPS_XY, NY, lambda m: half_xy - m), NY, half_xy)

    est_copy.wait()
    for plane in range(SLAB):
        along[plane] = dot(matrix_x, est_ref[plane]).astype(BF16)
    chosen = tissue_tiles(mask_ref)
    row_of = [pl.multiple_of(tile // 2 * TILE, TILE) for tile in chosen]
    lane_of = [pl.multiple_of(tile % 2 * TILE, TILE) for tile in chosen]
    index = iota((slots, TILE), 0).astype(F32)
    pick, pick_more = [
        jnp.concatenate([one_hot(index == places[pl.ds(first + tile, 1), :]) for tile in chosen], axis=1)
        for first in (0, tiles)
    ]
    block = ZB // group
    r = iota((ZB, ZB), 0)
    turn = one_hot(iota((ZB, ZB), 1) == r % group * block + r // group)

    def rows_of(values, i):
        return jnp.concatenate(
            [
                values[slot * DEVS + i * block : slot * DEVS + (i + 1) * block, plane * TILE : (plane + 1) * TILE]
                for plane in range(SLAB)
                for slot in range(HALF)
            ],
            axis=0,
        )

    meas_copy.wait()
    seen = jnp.concatenate(
        [
            jnp.concatenate(
                [meas_ref[0, plane, pl.ds(row, TILE), pl.ds(lane, TILE)] for plane in range(SLAB)], axis=1
            )
            for row, lane in zip(row_of, lane_of)
        ],
        axis=0,
    )
    seen = dot(pick, seen).astype(BF16)
    blurred = []
    for row, lane in zip(row_of, lane_of):
        rows = jnp.concatenate([along[plane, pl.ds(row, TILE), :] for plane in range(SLAB)], axis=0)
        tile = dot(rows, matrix_y[:, pl.ds(lane, TILE)]).astype(BF16)
        blurred.append(
            jnp.concatenate([tile[plane * TILE : (plane + 1) * TILE] for plane in range(SLAB)], axis=1)
        )
    blurred = jnp.concatenate(blurred, axis=0)
    parts = [dot(pick, blurred).astype(BF16), dot(pick_more, blurred).astype(BF16), seen]
    for i in range(DEVS // block):
        turned = dot(turn, jnp.concatenate([rows_of(part, i) for part in parts], axis=1)).astype(BF16)
        for k in range(len(parts)):
            out_ref[i * block : (i + 1) * block, k * group : (k + 1) * group, :] = turned[
                :, k * TILE : (k + 1) * TILE
            ].reshape(block, group, TILE)
        here = pl.ds(i * block, block)
        copies.append(pltpu.make_async_copy(out_ref.at[here], out_hbm.at[here], out_sem.at[i]))
        copies[-1].start()
    for copy in copies:
        copy.wait()


def bands_kernel(pz_ref, forward_ref, adjoint_ref):
    group = SLAB * HALF
    edge = ZB // 2
    half_z = TAPS_Z // 2
    near = edge - HALF * half_z
    far = edge + HALF * half_z
    forward_ref[...] = rolled(
        placed_taps(lambda m: pz_ref[0, m], TAPS_Z, 2 * ZB, lambda m: near + HALF * m), ZB
    ).astype(BF16)
    adjoint = rolled(
        placed_taps(lambda m: pz_ref[0, m], TAPS_Z, 2 * ZB, lambda m: far - HALF * m), ZB
    ).astype(BF16)
    r = iota((ZB, ZB), 0)
    part = ZB // SLAB
    source = r % part // HALF * group + r // part * HALF + r % HALF
    adjoint_ref[...] = dot(one_hot(iota((ZB, ZB), 1) == source), adjoint).astype(BF16)


def prep_kernel(px_ref, py_ref, table_ref, est_hbm, rows_ref, units_ref, plane_ref, sem):
    plane_copy = pltpu.make_async_copy(est_hbm.at[lax.axis_index("view")], plane_ref, sem)
    plane_copy.start()
    half_xy = TAPS_XY // 2
    for view in range(VIEWS):
        rows_ref[view : view + 1, :] = placed_taps(
            lambda m: px_ref[view, m], TAPS_XY, 2 * XB, lambda m: XB // 2 + half_xy - m
        )
        rows_ref[VIEWS + view : VIEWS + view + 1, :] = placed_taps(
            lambda m: py_ref[view, m], TAPS_XY, NY, lambda m: m - half_xy
        )
    slots = HALF * DEVS
    tiles = UNITS // TILE
    table = table_ref[...].astype(F32)
    table = jnp.concatenate([table] * (TILE // tiles), axis=0).T.astype(I32)
    total = jnp.zeros((1, slots), I32)
    for tile in range(tiles):
        place = table[:, tile : tile + 1]
        place = jnp.where(place < 0, -1, place % DEVS * HALF + place // DEVS)
        unit = 2 * (tile // 2 * TILE + iota((TILE, slots), 0)) + tile % 2
        total += jnp.sum(jnp.where(place == iota((TILE, slots), 1), unit, 0), axis=0, keepdims=True)
    units_ref[...] = jnp.broadcast_to(total, (8, slots))
    plane_copy.wait()


def z_kernel(forward_ref, adjoint_ref, in_ref, back_hbm, ratio, back_ref, sems):
    group = SLAB * HALF
    rows = DEVS * group
    blocks = rows // ZB
    edge = ZB // 2
    block = ZB // group
    none = jnp.zeros((edge, TILE), BF16)

    def window(block_at):
        first, last = block_at * block - block // 2, (block_at + 1) * block + block // 2
        inner = in_ref[max(first, 0) : min(last, DEVS), 0:group, :]
        inner = inner.reshape(inner.shape[0] * group, TILE)
        return jnp.concatenate([none] * (first < 0) + [inner] + [none] * (last > DEVS), axis=0)

    ratio[0:edge, :] = none
    ratio[edge + rows :, :] = none
    for i in range(blocks // 2):
        pair = (i, i + blocks // 2)
        both = dot(forward_ref[...], jnp.concatenate([window(j) for j in pair], axis=1))
        for half, j in enumerate(pair):
            seen = in_ref[j * block : (j + 1) * block, 2 * group :, :].reshape(ZB, TILE)
            ratio[edge + j * ZB : edge + (j + 1) * ZB, :] = (
                seen.astype(F32) / both[:, half * TILE : (half + 1) * TILE]
            ).astype(BF16)
    part = ZB // SLAB
    copies = []
    for i in range(blocks // 2):
        pair = (i, i + blocks // 2)
        both = dot(
            adjoint_ref[...], jnp.concatenate([ratio[j * ZB : j * ZB + 2 * ZB, :] for j in pair], axis=1)
        ).astype(BF16)
        for half, j in enumerate(pair):
            for plane in range(SLAB):
                back_ref[plane, j * part : (j + 1) * part, :] = both[
                    plane * part : (plane + 1) * part, half * TILE : (half + 1) * TILE
                ]
        if i % 2:
            for half, j in enumerate(pair):
                here = pl.ds((j - 1) * part, 2 * part)
                copies.append(
                    pltpu.make_async_copy(back_ref.at[:, here, :], back_hbm.at[:, here, :], sems.at[i // 2, half])
                )
                copies[-1].start()
    for copy in copies:
        copy.wait()


def column_kernel(forward_ref, count_ref, in_ref, column_ref, padded):
    group = SLAB * HALF
    rows = DEVS * group
    edge = ZB // 2
    padded[0:edge, :] = jnp.zeros((edge, 2 * TILE), BF16)
    padded[edge + rows :, :] = jnp.zeros((edge, 2 * TILE), BF16)
    padded[edge : edge + rows, 0:TILE] = in_ref[:, 0:group, :].reshape(rows, TILE)
    padded[edge : edge + rows, TILE:] = in_ref[:, group : 2 * group, :].reshape(rows, TILE)
    count = count_ref[pl.ds(lax.axis_index("space"), 1), :].reshape(1, 1, TILE)
    planes = ZB // HALF
    pairs = planes // 2
    sub = iota((pairs, 8, TILE), 1)
    live = sub < count
    for block in range(rows // ZB):
        values = dot(forward_ref[...], padded[block * ZB : block * ZB + 2 * ZB, :])
        own = values[:, :TILE].reshape(pairs, 8, TILE)
        more = values[:, TILE:].reshape(pairs, 8, TILE)
        first = jnp.where(sub < HALF, own, pltpu.roll(more, HALF, 1))
        second = jnp.where(sub < HALF, pltpu.roll(own, HALF, 1), more)
        both = jnp.stack([jnp.where(live, first, 0.0), jnp.where(live, second, 0.0)], axis=1)
        column_ref[block * planes : (block + 1) * planes] = both.reshape(planes, 8, TILE).astype(BF16)


def back_kernel(
    mask_hbm, units_ref, rows_ref, in_ref, est_ref, out_ref, mask_ref, back_z, padded, mask_sem,
):
    mask_copy = pltpu.make_async_copy(mask_hbm, mask_ref, mask_sem)
    mask_copy.start()
    edge = XB // 2
    back_z[...] = jnp.ones((VIEWS, NX, NY), BF16)
    bands, matrix_y = [], []
    for view in range(VIEWS):
        bands.append(rolled(rows_ref[view : view + 1, :], XB).astype(BF16))
        matrix_y.append(band(rows_ref[VIEWS + view : VIEWS + view + 1, :], NY, TAPS_XY // 2))
        padded[view, 0:edge, :] = jnp.zeros((edge, NY), BF16)
        padded[view, edge + NX :, :] = jnp.zeros((edge, NY), BF16)
    cols = jnp.concatenate([in_ref[view] for view in range(VIEWS)], axis=1)
    units = units_ref[0:1, :]
    slots = HALF * DEVS
    mask_copy.wait()
    chosen = tissue_tiles(mask_ref)
    here = [units == 2 * (tile // 2 * TILE + iota((TILE, slots), 0)) + tile % 2 for tile in chosen]
    found = dot(jnp.concatenate([one_hot(h) for h in here], axis=0), cols).astype(BF16)
    for i, tile in enumerate(chosen):
        row = pl.multiple_of(tile // 2 * TILE, TILE)
        lane = pl.multiple_of(tile % 2 * TILE, TILE)
        for view in range(VIEWS):
            back_z[view, pl.ds(row, TILE), pl.ds(lane, TILE)] = found[
                i * TILE : (i + 1) * TILE, view * TILE : (view + 1) * TILE
            ]
    for view in range(VIEWS):
        padded[view, edge : edge + NX, :] = dot(back_z[view], matrix_y[view]).astype(BF16)
    for block in range(NX // XB):
        here = pl.ds(block * XB, XB)
        summed = jnp.zeros((XB, NY), F32)
        for view in range(VIEWS):
            summed += dot(bands[view], padded[view, block * XB : block * XB + 2 * XB, :])
        updated = (est_ref[here, :].astype(F32) * summed / VIEWS).astype(BF16)
        for view in range(VIEWS):
            out_ref[view, here, :] = updated


def call(kernel, name, out_shape, in_specs, out_specs, scratch, limit, flops, moved):
    return pl.pallas_call(
        kernel,
        out_shape=out_shape,
        in_specs=in_specs,
        out_specs=out_specs,
        scratch_shapes=scratch,
        compiler_params=pltpu.CompilerParams(vmem_limit_bytes=limit * 1024 * 1024),
        cost_estimate=pl.CostEstimate(flops=flops, bytes_accessed=moved, transcendentals=0),
        name=name,
    )


def pack(estimate, measured, psf_x, psf_y, tissue_mask, column_owner):
    return call(
        pack_kernel,
        "pack",
        (shape(DEVS, MSG, TILE), shape(UNITS // TILE, TILE, dtype=I32), shape(DEVS, TILE, dtype=I32)),
        [ANY] * 6,
        (ANY, ANY, ANY),
        [
            pltpu.SMEM((UNITS // TILE,), I32),
            pltpu.SMEM((1, TAPS_XY), F32),
            pltpu.SMEM((1, TAPS_XY), F32),
            pltpu.VMEM((1, UNITS), I32),
            pltpu.VMEM((SLAB, NX, NY), BF16),
            pltpu.VMEM((1, SLAB, NX, NY), BF16),
            pltpu.VMEM((SLAB, NX, NY), BF16),
            pltpu.VMEM((2 * UNITS // TILE, TILE), F32),
            pltpu.VMEM((NY, NY), BF16),
            pltpu.VMEM((DEVS, MSG, TILE), BF16),
            pltpu.VMEM((UNITS // TILE, TILE), I32),
            pltpu.VMEM((DEVS, TILE), I32),
            pltpu.SemaphoreType.DMA((8,)),
            pltpu.SemaphoreType.DMA((DEVS * SLAB * HALF // ZB,)),
        ],
        WIDE_LIMIT,
        flops=2_000_000_000,
        moved=4_000_000,
    )(tissue_mask, psf_x, psf_y, column_owner.reshape(1, UNITS), estimate, measured)


def bands(psf_z):
    return call(
        bands_kernel,
        "bands",
        (shape(ZB, 2 * ZB), shape(ZB, 2 * ZB)),
        [SMEM],
        (VMEM, VMEM),
        [],
        LIMIT,
        flops=70_000_000,
        moved=500_000,
    )(psf_z)


def prep(taps_x, taps_y, table, estimate):
    return call(
        prep_kernel,
        "prep",
        (shape(2 * VIEWS, NY, dtype=F32), shape(8, HALF * DEVS, dtype=I32), shape(NX, NY)),
        [SMEM, SMEM, VMEM, ANY],
        (VMEM,) * 3,
        [pltpu.SemaphoreType.DMA],
        WIDE_LIMIT,
        flops=10_000_000,
        moved=1_000_000,
    )(taps_x, taps_y, table, estimate)


def z_pair(forward, adjoint, arrived):
    rows = DEVS * SLAB * HALF
    return call(
        z_kernel,
        "zpair",
        shape(VIEWS, HALF * DEVS, TILE),
        [VMEM, VMEM, VMEM],
        ANY,
        [
            pltpu.VMEM((rows + ZB, TILE), BF16),
            pltpu.VMEM((VIEWS, HALF * DEVS, TILE), BF16),
            pltpu.SemaphoreType.DMA((rows // ZB // 4, 2)),
        ],
        LIMIT,
        flops=540_000_000,
        moved=3_000_000,
    )(forward, adjoint, arrived)


def column(forward, count, arrived):
    rows = DEVS * SLAB * HALF
    return call(
        column_kernel,
        "column",
        shape(SLAB * DEVS, 2 * HALF, TILE),
        [VMEM, VMEM, VMEM],
        VMEM,
        [pltpu.VMEM((rows + ZB, 2 * TILE), BF16)],
        LIMIT,
        flops=540_000_000,
        moved=3_000_000,
    )(forward, count, arrived)


def back(tissue_mask, units, rows, returned, plane):
    return call(
        back_kernel,
        "back",
        shape(VIEWS, NX, NY),
        [ANY, VMEM, VMEM, VMEM, VMEM],
        VMEM,
        [
            pltpu.SMEM((UNITS // TILE,), I32),
            pltpu.VMEM((VIEWS, NX, NY), BF16),
            pltpu.VMEM((VIEWS, NX + XB, NY), BF16),
            pltpu.SemaphoreType.DMA,
        ],
        LIMIT,
        flops=1_400_000_000,
        moved=5_000_000,
    )(tissue_mask, units, rows, returned, plane)


def shards(estimate, measured, psf_x, psf_y, psf_z, tissue_mask, column_owner):
    message, table, count = pack(estimate, measured, psf_x, psf_y, tissue_mask, column_owner)
    message, psf_z = lax.optimization_barrier((message, psf_z))
    arrived = lax.all_to_all(message, "space", split_axis=0, concat_axis=0, tiled=True)
    forward, adjoint = bands(psf_z)
    arrived, psf_x, psf_y = lax.optimization_barrier((arrived, psf_x, psf_y))
    sent = z_pair(forward, adjoint, arrived)
    returned = lax.all_to_all(
        sent.reshape(VIEWS * DEVS, HALF, TILE),
        ("view", "space"),
        split_axis=0,
        concat_axis=0,
        tiled=True,
    ).reshape(VIEWS, HALF * DEVS, TILE)
    taps = lax.all_gather(jnp.concatenate([psf_x, psf_y], axis=1), "view", axis=0, tiled=True)
    rows, units, plane = prep(taps[:, :TAPS_XY], taps[:, TAPS_XY:], table, estimate)
    returned, column_blur = lax.optimization_barrier((returned, column(forward, count, arrived)))
    updated = back(tissue_mask, units, rows, returned, plane)
    updated = lax.all_to_all(updated, "view", split_axis=0, concat_axis=0, tiled=True)
    return updated, column_blur[None]


def solution(mesh):
    placed = (
        P("space", None, None),
        P("view", "space", None, None),
        P("view", None),
        P("view", None),
        P("view", None),
        P(),
        P(),
    )
    return jax.shard_map(
        shards,
        mesh=mesh,
        in_specs=placed,
        out_specs=(P("space", None, None), P("view", None, "space", None)),
        check_vma=False,
    )
```

```python
import jax
import jax.numpy as jnp
from jax import lax
from jax.experimental import pallas as pl
from jax.experimental.pallas import tpu as pltpu
from jax.sharding import PartitionSpec as P

F32 = jnp.float32
BF16 = jnp.bfloat16
I32 = jnp.int32

VIEWS, DEVS = 4, 128
SLAB, NX, NY, TILE = 4, 512, 256, 128
UNITS = 1024
HALF = 4
MSG = 3 * SLAB * HALF
TAPS_XY, TAPS_Z = 31, 63
ZB = 256
XB = 128
WIDE_LIMIT, LIMIT = 60, 24

SMEM = pl.BlockSpec(memory_space=pltpu.SMEM)
VMEM = pl.BlockSpec(memory_space=pltpu.VMEM)
ANY = pl.BlockSpec(memory_space=pl.ANY)


def shape(*dims, dtype=BF16):
    return jax.ShapeDtypeStruct(dims, dtype)


def iota(shape, dim):
    return lax.broadcasted_iota(I32, shape, dim)


def placed_taps(read, count, lanes, place):
    lane = iota((1, lanes), 1)
    total = read(0)
    for m in range(1, count):
        total = total + read(m)
    row = jnp.zeros((1, lanes), F32)
    for m in range(count):
        row = jnp.where(lane == place(m) % lanes, read(m), row)
    return (row / jnp.full((1, lanes), total, F32)).astype(BF16).astype(F32)


def rolled(row, rows):
    return pltpu.roll(
        jnp.broadcast_to(row, (rows, row.shape[1])), 0, 1, stride=1, stride_axis=0
    )


def band(row, n, half):
    distance = jnp.abs(iota((n, n), 1) - iota((n, n), 0))
    return jnp.where(distance <= half, rolled(row, n), 0.0).astype(BF16)


def dot(a, b, dims=((1,), (0,))):
    return lax.dot_general(a, b, (dims, ((), ())), preferred_element_type=F32)


def one_hot(condition):
    return jnp.where(condition, 1.0, 0.0).astype(BF16)


def slot_rows(mask_ref, owner_ref):
    pairs = UNITS // ZB
    square = (DEVS, TILE)
    device = iota(square, 0).astype(F32)
    w = iota((ZB, ZB), 1)
    unit = 2 * (w % TILE) + w // TILE
    deal = one_hot(iota((ZB, ZB), 0) == unit)
    owners = jnp.concatenate([owner_ref[0:1, i * ZB : (i + 1) * ZB] for i in range(pairs)] * 2, axis=0)
    owners = dot(owners.astype(F32).astype(BF16), deal)
    row = iota((ZB, ZB), 0)
    earlier = one_hot(2 * (row % TILE) + row // TILE < unit)
    sums = jnp.concatenate([earlier, jnp.ones((ZB, TILE), BF16)], axis=1)
    count = jnp.zeros(square, F32)
    owner, member, before = [], [], []
    for pair in range(pairs):
        for t in range(2):
            here = owners[pair : pair + 1, t * TILE : (t + 1) * TILE]
            owner.append(jnp.where(mask_ref[2 * pair + t] > 0, here, -1.0))
            member.append(device == owner[-1])
        found = dot(jnp.concatenate([one_hot(m) for m in member[-2:]], axis=1), sums)
        before.append(found[:, :TILE] + count)
        before.append(found[:, TILE:ZB] + count)
        count += found[:, ZB:]
    over = jnp.maximum(count - HALF, 0.0)
    free = jnp.maximum(HALF - count, 0.0)
    lower = one_hot(iota((DEVS, DEVS), 1) < iota((DEVS, DEVS), 0))
    starts = dot(lower, jnp.concatenate([over, free], axis=1).astype(BF16))
    over_start, free_start = starts[:, :TILE], starts[:, TILE:]
    free_end = free_start + free
    place = (count - free_start) * DEVS + device
    balanced, overflow = [], []
    for mine, inside, ahead in zip(owner, member, before):
        position = jnp.sum(jnp.where(inside, ahead, 0.0), axis=0, keepdims=True)
        start = jnp.sum(jnp.where(inside, over_start, 0.0), axis=0, keepdims=True)
        rank = start + position - HALF
        found = jnp.where((free_start <= rank) & (rank < free_end), place + rank * DEVS, 0.0)
        filled = jnp.sum(found, axis=0, keepdims=True)
        own = position * DEVS + mine
        balanced.append(jnp.where(mine < 0, -1.0, jnp.where(position < HALF, own, filled)))
        overflow.append(jnp.where((mine >= 0) & (position >= HALF), own - HALF * DEVS, -1.0))
    return balanced, overflow, count


def tissue_tiles(mask_ref):
    tiles = UNITS // TILE
    found = jnp.int32(0)
    chosen = [jnp.int32(0)] * (tiles // 2)
    for tile in range(tiles):
        here = mask_ref[tile] > 0
        chosen = [jnp.where(here & (found == i), tile, old) for i, old in enumerate(chosen)]
        found += here.astype(I32)
    return chosen


def pack_kernel(
    mask_hbm, px_hbm, py_hbm, owner_hbm, est_hbm, meas_hbm, out_hbm, table_hbm, count_hbm,
    mask_ref, px_ref, py_ref, owner_ref, est_ref, meas_ref, along, places, matrix_y,
    out_ref, table_ref, count_ref, sems, out_sem,
):
    reads = [
        pltpu.make_async_copy(source, target, sems.at[i])
        for i, (source, target) in enumerate(
            zip(
                (mask_hbm, owner_hbm, px_hbm, py_hbm, est_hbm, meas_hbm),
                (mask_ref, owner_ref, px_ref, py_ref, est_ref, meas_ref),
            )
        )
    ]
    for copy in reads:
        copy.start()
    est_copy, meas_copy = reads[4:]
    for copy in reads[:2]:
        copy.wait()
    slots = HALF * DEVS
    group = SLAB * HALF
    tiles = UNITS // TILE
    balanced, overflow, count = slot_rows(mask_ref, owner_ref)
    count_ref[...] = count.astype(I32)
    table_ref[...] = jnp.concatenate(balanced, axis=0).astype(I32)
    copies = [
        pltpu.make_async_copy(table_ref, table_hbm, sems.at[6]),
        pltpu.make_async_copy(count_ref, count_hbm, sems.at[7]),
    ]
    for copy in copies:
        copy.start()
    places[...] = jnp.concatenate(balanced + overflow, axis=0)
    for copy in reads[2:4]:
        copy.wait()
    half_xy = TAPS_XY // 2
    starts = [min(max(i * XB - XB // 2, 0), NX - 2 * XB) for i in range(NX // XB)]
    bands_x = {}
    for i, start in enumerate(starts):
        lead = i * XB - start
        if lead not in bands_x:
            row = placed_taps(lambda m: px_ref[0, m], TAPS_XY, 2 * XB, lambda m: lead + m - half_xy)
            distance = iota((XB, 2 * XB), 1) - iota((XB, 2 * XB), 0) - lead
            bands_x[lead] = jnp.where(jnp.abs(distance) <= half_xy, rolled(row, XB), 0.0).astype(BF16)
    matrix_y[...] = band(placed_taps(lambda m: py_ref[0, m], TAPS_XY, NY, lambda m: half_xy - m), NY, half_xy)

    est_copy.wait()
    for plane in range(SLAB):
        for i, start in enumerate(starts):
            along[plane, i * XB : (i + 1) * XB, :] = dot(
                bands_x[i * XB - start], est_ref[plane, start : start + 2 * XB, :]
            ).astype(BF16)
    chosen = tissue_tiles(mask_ref)
    row_of = [pl.multiple_of(tile // 2 * TILE, TILE) for tile in chosen]
    lane_of = [pl.multiple_of(tile % 2 * TILE, TILE) for tile in chosen]
    index = iota((slots, TILE), 0).astype(F32)
    pick, pick_more = [
        jnp.concatenate([one_hot(index == places[pl.ds(first + tile, 1), :]) for tile in chosen], axis=1)
        for first in (0, tiles)
    ]
    block = ZB // group
    r = iota((ZB, ZB), 0)
    turn = one_hot(iota((ZB, ZB), 1) == r % group * block + r // group)

    def rows_of(values, i):
        return jnp.concatenate(
            [
                values[slot * DEVS + i * block : slot * DEVS + (i + 1) * block, plane * TILE : (plane + 1) * TILE]
                for plane in range(SLAB)
                for slot in range(HALF)
            ],
            axis=0,
        )

    meas_copy.wait()
    seen = jnp.concatenate(
        [
            jnp.concatenate(
                [meas_ref[0, plane, pl.ds(row, TILE), pl.ds(lane, TILE)] for plane in range(SLAB)], axis=1
            )
            for row, lane in zip(row_of, lane_of)
        ],
        axis=0,
    )
    seen = dot(pick, seen).astype(BF16)
    blurred = []
    for row, lane in zip(row_of, lane_of):
        rows = jnp.concatenate([along[plane, pl.ds(row, TILE), :] for plane in range(SLAB)], axis=0)
        tile = dot(rows, matrix_y[:, pl.ds(lane, TILE)]).astype(BF16)
        blurred.append(
            jnp.concatenate([tile[plane * TILE : (plane + 1) * TILE] for plane in range(SLAB)], axis=1)
        )
    blurred = jnp.concatenate(blurred, axis=0)
    parts = [dot(pick, blurred).astype(BF16), dot(pick_more, blurred).astype(BF16), seen]
    for i in range(DEVS // block):
        turned = dot(turn, jnp.concatenate([rows_of(part, i) for part in parts], axis=1)).astype(BF16)
        for k in range(len(parts)):
            out_ref[i * block : (i + 1) * block, k * group : (k + 1) * group, :] = turned[
                :, k * TILE : (k + 1) * TILE
            ].reshape(block, group, TILE)
        here = pl.ds(i * block, block)
        copies.append(pltpu.make_async_copy(out_ref.at[here], out_hbm.at[here], out_sem.at[i]))
        copies[-1].start()
    for copy in copies:
        copy.wait()


def bands_kernel(pz_ref, forward_ref, adjoint_ref):
    group = SLAB * HALF
    edge = ZB // 2
    half_z = TAPS_Z // 2
    near = edge - HALF * half_z
    far = edge + HALF * half_z
    forward_ref[...] = rolled(
        placed_taps(lambda m: pz_ref[0, m], TAPS_Z, 2 * ZB, lambda m: near + HALF * m), ZB
    ).astype(BF16)
    adjoint = rolled(
        placed_taps(lambda m: pz_ref[0, m], TAPS_Z, 2 * ZB, lambda m: far - HALF * m), ZB
    ).astype(BF16)
    r = iota((ZB, ZB), 0)
    part = ZB // SLAB
    source = r % part // HALF * group + r // part * HALF + r % HALF
    adjoint_ref[...] = dot(one_hot(iota((ZB, ZB), 1) == source), adjoint).astype(BF16)


def prep_kernel(px_ref, py_ref, table_ref, est_hbm, rows_ref, units_ref, plane_ref, sem):
    plane_copy = pltpu.make_async_copy(est_hbm.at[lax.axis_index("view")], plane_ref, sem)
    plane_copy.start()
    half_xy = TAPS_XY // 2
    for view in range(VIEWS):
        rows_ref[view : view + 1, :] = placed_taps(
            lambda m: px_ref[view, m], TAPS_XY, 2 * XB, lambda m: XB // 2 + half_xy - m
        )
        rows_ref[VIEWS + view : VIEWS + view + 1, :] = placed_taps(
            lambda m: py_ref[view, m], TAPS_XY, NY, lambda m: m - half_xy
        )
    slots = HALF * DEVS
    tiles = UNITS // TILE
    table = table_ref[...].astype(F32)
    table = jnp.concatenate([table] * (TILE // tiles), axis=0).T.astype(I32)
    total = jnp.zeros((1, slots), I32)
    for tile in range(tiles):
        place = table[:, tile : tile + 1]
        place = jnp.where(place < 0, -1, place % DEVS * HALF + place // DEVS)
        unit = 2 * (tile // 2 * TILE + iota((TILE, slots), 0)) + tile % 2
        total += jnp.sum(jnp.where(place == iota((TILE, slots), 1), unit, 0), axis=0, keepdims=True)
    units_ref[...] = jnp.broadcast_to(total, (8, slots))
    plane_copy.wait()


def z_kernel(forward_ref, adjoint_ref, in_ref, back_hbm, ratio, back_ref, sems):
    group = SLAB * HALF
    rows = DEVS * group
    blocks = rows // ZB
    edge = ZB // 2
    block = ZB // group
    none = jnp.zeros((edge, TILE), BF16)

    def window(block_at):
        first, last = block_at * block - block // 2, (block_at + 1) * block + block // 2
        inner = in_ref[max(first, 0) : min(last, DEVS), 0:group, :]
        inner = inner.reshape(inner.shape[0] * group, TILE)
        return jnp.concatenate([none] * (first < 0) + [inner] + [none] * (last > DEVS), axis=0)

    ratio[0:edge, :] = none
    ratio[edge + rows :, :] = none
    for i in range(blocks // 2):
        pair = (i, i + blocks // 2)
        both = dot(forward_ref[...], jnp.concatenate([window(j) for j in pair], axis=1))
        for half, j in enumerate(pair):
            seen = in_ref[j * block : (j + 1) * block, 2 * group :, :].reshape(ZB, TILE)
            ratio[edge + j * ZB : edge + (j + 1) * ZB, :] = (
                seen.astype(F32) / both[:, half * TILE : (half + 1) * TILE]
            ).astype(BF16)
    part = ZB // SLAB
    copies = []
    for i in range(blocks // 2):
        pair = (i, i + blocks // 2)
        both = dot(
            adjoint_ref[...], jnp.concatenate([ratio[j * ZB : j * ZB + 2 * ZB, :] for j in pair], axis=1)
        ).astype(BF16)
        for half, j in enumerate(pair):
            for plane in range(SLAB):
                back_ref[plane, j * part : (j + 1) * part, :] = both[
                    plane * part : (plane + 1) * part, half * TILE : (half + 1) * TILE
                ]
        if i % 2:
            for half, j in enumerate(pair):
                here = pl.ds((j - 1) * part, 2 * part)
                copies.append(
                    pltpu.make_async_copy(back_ref.at[:, here, :], back_hbm.at[:, here, :], sems.at[i // 2, half])
                )
                copies[-1].start()
    for copy in copies:
        copy.wait()


def column_kernel(forward_ref, count_ref, in_ref, column_ref, padded):
    group = SLAB * HALF
    rows = DEVS * group
    edge = ZB // 2
    padded[0:edge, :] = jnp.zeros((edge, 2 * TILE), BF16)
    padded[edge + rows :, :] = jnp.zeros((edge, 2 * TILE), BF16)
    padded[edge : edge + rows, 0:TILE] = in_ref[:, 0:group, :].reshape(rows, TILE)
    padded[edge : edge + rows, TILE:] = in_ref[:, group : 2 * group, :].reshape(rows, TILE)
    count = count_ref[pl.ds(lax.axis_index("space"), 1), :].reshape(1, 1, TILE)
    planes = ZB // HALF
    pairs = planes // 2
    sub = iota((pairs, 8, TILE), 1)
    live = sub < count
    for block in range(rows // ZB):
        values = dot(forward_ref[...], padded[block * ZB : block * ZB + 2 * ZB, :])
        own = values[:, :TILE].reshape(pairs, 8, TILE)
        more = values[:, TILE:].reshape(pairs, 8, TILE)
        first = jnp.where(sub < HALF, own, pltpu.roll(more, HALF, 1))
        second = jnp.where(sub < HALF, pltpu.roll(own, HALF, 1), more)
        both = jnp.stack([jnp.where(live, first, 0.0), jnp.where(live, second, 0.0)], axis=1)
        column_ref[block * planes : (block + 1) * planes] = both.reshape(planes, 8, TILE).astype(BF16)


def back_kernel(
    mask_hbm, units_ref, rows_ref, in_ref, est_ref, out_ref, mask_ref, back_z, padded, mask_sem,
):
    mask_copy = pltpu.make_async_copy(mask_hbm, mask_ref, mask_sem)
    mask_copy.start()
    edge = XB // 2
    back_z[...] = jnp.ones((VIEWS, NX, NY), BF16)
    bands, matrix_y = [], []
    for view in range(VIEWS):
        bands.append(rolled(rows_ref[view : view + 1, :], XB).astype(BF16))
        matrix_y.append(band(rows_ref[VIEWS + view : VIEWS + view + 1, :], NY, TAPS_XY // 2))
        padded[view, 0:edge, :] = jnp.zeros((edge, NY), BF16)
        padded[view, edge + NX :, :] = jnp.zeros((edge, NY), BF16)
    cols = jnp.concatenate([in_ref[view] for view in range(VIEWS)], axis=1)
    units = units_ref[0:1, :]
    slots = HALF * DEVS
    mask_copy.wait()
    chosen = tissue_tiles(mask_ref)
    here = [units == 2 * (tile // 2 * TILE + iota((TILE, slots), 0)) + tile % 2 for tile in chosen]
    found = dot(jnp.concatenate([one_hot(h) for h in here], axis=0), cols).astype(BF16)
    for i, tile in enumerate(chosen):
        row = pl.multiple_of(tile // 2 * TILE, TILE)
        lane = pl.multiple_of(tile % 2 * TILE, TILE)
        for view in range(VIEWS):
            back_z[view, pl.ds(row, TILE), pl.ds(lane, TILE)] = found[
                i * TILE : (i + 1) * TILE, view * TILE : (view + 1) * TILE
            ]
    for view in range(VIEWS):
        padded[view, edge : edge + NX, :] = dot(back_z[view], matrix_y[view]).astype(BF16)
    for block in range(NX // XB):
        here = pl.ds(block * XB, XB)
        summed = jnp.zeros((XB, NY), F32)
        for view in range(VIEWS):
            summed += dot(bands[view], padded[view, block * XB : block * XB + 2 * XB, :])
        updated = (est_ref[here, :].astype(F32) * summed / VIEWS).astype(BF16)
        for view in range(VIEWS):
            out_ref[view, here, :] = updated


def call(kernel, name, out_shape, in_specs, out_specs, scratch, limit, flops, moved):
    return pl.pallas_call(
        kernel,
        out_shape=out_shape,
        in_specs=in_specs,
        out_specs=out_specs,
        scratch_shapes=scratch,
        compiler_params=pltpu.CompilerParams(vmem_limit_bytes=limit * 1024 * 1024),
        cost_estimate=pl.CostEstimate(flops=flops, bytes_accessed=moved, transcendentals=0),
        name=name,
    )


def pack(estimate, measured, psf_x, psf_y, tissue_mask, column_owner):
    return call(
        pack_kernel,
        "pack",
        (shape(DEVS, MSG, TILE), shape(UNITS // TILE, TILE, dtype=I32), shape(DEVS, TILE, dtype=I32)),
        [ANY] * 6,
        (ANY, ANY, ANY),
        [
            pltpu.SMEM((UNITS // TILE,), I32),
            pltpu.SMEM((1, TAPS_XY), F32),
            pltpu.SMEM((1, TAPS_XY), F32),
            pltpu.VMEM((1, UNITS), I32),
            pltpu.VMEM((SLAB, NX, NY), BF16),
            pltpu.VMEM((1, SLAB, NX, NY), BF16),
            pltpu.VMEM((SLAB, NX, NY), BF16),
            pltpu.VMEM((2 * UNITS // TILE, TILE), F32),
            pltpu.VMEM((NY, NY), BF16),
            pltpu.VMEM((DEVS, MSG, TILE), BF16),
            pltpu.VMEM((UNITS // TILE, TILE), I32),
            pltpu.VMEM((DEVS, TILE), I32),
            pltpu.SemaphoreType.DMA((8,)),
            pltpu.SemaphoreType.DMA((DEVS * SLAB * HALF // ZB,)),
        ],
        WIDE_LIMIT,
        flops=2_000_000_000,
        moved=4_000_000,
    )(tissue_mask, psf_x, psf_y, column_owner.reshape(1, UNITS), estimate, measured)


def bands(psf_z):
    return call(
        bands_kernel,
        "bands",
        (shape(ZB, 2 * ZB), shape(ZB, 2 * ZB)),
        [SMEM],
        (VMEM, VMEM),
        [],
        LIMIT,
        flops=70_000_000,
        moved=500_000,
    )(psf_z)


def prep(taps_x, taps_y, table, estimate):
    return call(
        prep_kernel,
        "prep",
        (shape(2 * VIEWS, NY, dtype=F32), shape(8, HALF * DEVS, dtype=I32), shape(NX, NY)),
        [SMEM, SMEM, VMEM, ANY],
        (VMEM,) * 3,
        [pltpu.SemaphoreType.DMA],
        WIDE_LIMIT,
        flops=10_000_000,
        moved=1_000_000,
    )(taps_x, taps_y, table, estimate)


def z_pair(forward, adjoint, arrived):
    rows = DEVS * SLAB * HALF
    return call(
        z_kernel,
        "zpair",
        shape(VIEWS, HALF * DEVS, TILE),
        [VMEM, VMEM, VMEM],
        ANY,
        [
            pltpu.VMEM((rows + ZB, TILE), BF16),
            pltpu.VMEM((VIEWS, HALF * DEVS, TILE), BF16),
            pltpu.SemaphoreType.DMA((rows // ZB // 4, 2)),
        ],
        LIMIT,
        flops=540_000_000,
        moved=3_000_000,
    )(forward, adjoint, arrived)


def column(forward, count, arrived):
    rows = DEVS * SLAB * HALF
    return call(
        column_kernel,
        "column",
        shape(SLAB * DEVS, 2 * HALF, TILE),
        [VMEM, VMEM, VMEM],
        VMEM,
        [pltpu.VMEM((rows + ZB, 2 * TILE), BF16)],
        LIMIT,
        flops=540_000_000,
        moved=3_000_000,
    )(forward, count, arrived)


def back(tissue_mask, units, rows, returned, plane):
    return call(
        back_kernel,
        "back",
        shape(VIEWS, NX, NY),
        [ANY, VMEM, VMEM, VMEM, VMEM],
        VMEM,
        [
            pltpu.SMEM((UNITS // TILE,), I32),
            pltpu.VMEM((VIEWS, NX, NY), BF16),
            pltpu.VMEM((VIEWS, NX + XB, NY), BF16),
            pltpu.SemaphoreType.DMA,
        ],
        LIMIT,
        flops=1_400_000_000,
        moved=5_000_000,
    )(tissue_mask, units, rows, returned, plane)


def shards(estimate, measured, psf_x, psf_y, psf_z, tissue_mask, column_owner):
    message, table, count = pack(estimate, measured, psf_x, psf_y, tissue_mask, column_owner)
    message, psf_z = lax.optimization_barrier((message, psf_z))
    arrived = lax.all_to_all(message, "space", split_axis=0, concat_axis=0, tiled=True)
    forward, adjoint = bands(psf_z)
    arrived, psf_x, psf_y = lax.optimization_barrier((arrived, psf_x, psf_y))
    sent = z_pair(forward, adjoint, arrived)
    returned = lax.all_to_all(
        sent.reshape(VIEWS * DEVS, HALF, TILE),
        ("view", "space"),
        split_axis=0,
        concat_axis=0,
        tiled=True,
    ).reshape(VIEWS, HALF * DEVS, TILE)
    taps = lax.all_gather(jnp.concatenate([psf_x, psf_y], axis=1), "view", axis=0, tiled=True)
    rows, units, plane = prep(taps[:, :TAPS_XY], taps[:, TAPS_XY:], table, estimate)
    returned, column_blur = lax.optimization_barrier((returned, column(forward, count, arrived)))
    updated = back(tissue_mask, units, rows, returned, plane)
    updated = lax.all_to_all(updated, "view", split_axis=0, concat_axis=0, tiled=True)
    return updated, column_blur[None]


def solution(mesh):
    placed = (
        P("space", None, None),
        P("view", "space", None, None),
        P("view", None),
        P("view", None),
        P("view", None),
        P(),
        P(),
    )
    return jax.shard_map(
        shards,
        mesh=mesh,
        in_specs=placed,
        out_specs=(P("space", None, None), P("view", None, "space", None)),
        check_vma=False,
    )
```

```python
import jax
import jax.numpy as jnp
from jax import lax
from jax.experimental import pallas as pl
from jax.experimental.pallas import tpu as pltpu
from jax.sharding import PartitionSpec as P

F32 = jnp.float32
BF16 = jnp.bfloat16
I32 = jnp.int32

VIEWS, DEVS = 4, 128
SLAB, NX, NY, TILE = 4, 512, 256, 128
UNITS = 1024
HALF = 4
MSG = 3 * SLAB * HALF
TAPS_XY, TAPS_Z = 31, 63
ZB = 256
XB = 128
WIDE_LIMIT, LIMIT = 60, 24

SMEM = pl.BlockSpec(memory_space=pltpu.SMEM)
VMEM = pl.BlockSpec(memory_space=pltpu.VMEM)
ANY = pl.BlockSpec(memory_space=pl.ANY)


def shape(*dims, dtype=BF16):
    return jax.ShapeDtypeStruct(dims, dtype)


def iota(shape, dim):
    return lax.broadcasted_iota(I32, shape, dim)


def placed_taps(read, count, lanes, place):
    lane = iota((1, lanes), 1)
    total = read(0)
    for m in range(1, count):
        total = total + read(m)
    row = jnp.zeros((1, lanes), F32)
    for m in range(count):
        row = jnp.where(lane == place(m) % lanes, read(m), row)
    return (row / jnp.full((1, lanes), total, F32)).astype(BF16).astype(F32)


def rolled(row, rows):
    return pltpu.roll(
        jnp.broadcast_to(row, (rows, row.shape[1])), 0, 1, stride=1, stride_axis=0
    )


def band(row, n, half):
    distance = jnp.abs(iota((n, n), 1) - iota((n, n), 0))
    return jnp.where(distance <= half, rolled(row, n), 0.0).astype(BF16)


def dot(a, b, dims=((1,), (0,))):
    return lax.dot_general(a, b, (dims, ((), ())), preferred_element_type=F32)


def one_hot(condition):
    return jnp.where(condition, 1.0, 0.0).astype(BF16)


def slot_rows(mask_ref, owner_ref):
    pairs = UNITS // ZB
    square = (DEVS, TILE)
    device = iota(square, 0).astype(F32)
    w = iota((ZB, ZB), 1)
    unit = 2 * (w % TILE) + w // TILE
    deal = one_hot(iota((ZB, ZB), 0) == unit)
    owners = jnp.concatenate([owner_ref[0:1, i * ZB : (i + 1) * ZB] for i in range(pairs)] * 2, axis=0)
    owners = dot(owners.astype(F32).astype(BF16), deal)
    row = iota((ZB, ZB), 0)
    earlier = one_hot(2 * (row % TILE) + row // TILE < unit)
    sums = jnp.concatenate([earlier, jnp.ones((ZB, TILE), BF16)], axis=1)
    count = jnp.zeros(square, F32)
    owner, member, before = [], [], []
    for pair in range(pairs):
        for t in range(2):
            here = owners[pair : pair + 1, t * TILE : (t + 1) * TILE]
            owner.append(jnp.where(mask_ref[2 * pair + t] > 0, here, -1.0))
            member.append(device == owner[-1])
        found = dot(jnp.concatenate([one_hot(m) for m in member[-2:]], axis=1), sums)
        before.append(found[:, :TILE] + count)
        before.append(found[:, TILE:ZB] + count)
        count += found[:, ZB:]
    over = jnp.maximum(count - HALF, 0.0)
    free = jnp.maximum(HALF - count, 0.0)
    lower = one_hot(iota((DEVS, DEVS), 1) < iota((DEVS, DEVS), 0))
    starts = dot(lower, jnp.concatenate([over, free], axis=1).astype(BF16))
    over_start, free_start = starts[:, :TILE], starts[:, TILE:]
    free_end = free_start + free
    place = (count - free_start) * DEVS + device
    balanced, overflow = [], []
    for mine, inside, ahead in zip(owner, member, before):
        position = jnp.sum(jnp.where(inside, ahead, 0.0), axis=0, keepdims=True)
        start = jnp.sum(jnp.where(inside, over_start, 0.0), axis=0, keepdims=True)
        rank = start + position - HALF
        found = jnp.where((free_start <= rank) & (rank < free_end), place + rank * DEVS, 0.0)
        filled = jnp.sum(found, axis=0, keepdims=True)
        own = position * DEVS + mine
        balanced.append(jnp.where(mine < 0, -1.0, jnp.where(position < HALF, own, filled)))
        overflow.append(jnp.where((mine >= 0) & (position >= HALF), own - HALF * DEVS, -1.0))
    return balanced, overflow, count


def tissue_tiles(mask_ref):
    tiles = UNITS // TILE
    found = jnp.int32(0)
    chosen = [jnp.int32(0)] * (tiles // 2)
    for tile in range(tiles):
        here = mask_ref[tile] > 0
        chosen = [jnp.where(here & (found == i), tile, old) for i, old in enumerate(chosen)]
        found += here.astype(I32)
    return chosen


def pack_kernel(
    mask_hbm, px_hbm, py_hbm, owner_hbm, est_hbm, meas_hbm, out_hbm, table_hbm, count_hbm,
    mask_ref, px_ref, py_ref, owner_ref, est_ref, meas_ref, along, places, matrix_y,
    out_ref, table_ref, count_ref, sems, out_sem,
):
    reads = [
        pltpu.make_async_copy(source, target, sems.at[i])
        for i, (source, target) in enumerate(
            zip(
                (mask_hbm, owner_hbm, px_hbm, py_hbm, est_hbm, meas_hbm),
                (mask_ref, owner_ref, px_ref, py_ref, est_ref, meas_ref),
            )
        )
    ]
    for copy in reads:
        copy.start()
    est_copy, meas_copy = reads[4:]
    for copy in reads[:2]:
        copy.wait()
    slots = HALF * DEVS
    group = SLAB * HALF
    tiles = UNITS // TILE
    balanced, overflow, count = slot_rows(mask_ref, owner_ref)
    count_ref[...] = count.astype(I32)
    table_ref[...] = jnp.concatenate(balanced, axis=0).astype(I32)
    copies = [
        pltpu.make_async_copy(table_ref, table_hbm, sems.at[6]),
        pltpu.make_async_copy(count_ref, count_hbm, sems.at[7]),
    ]
    for copy in copies:
        copy.start()
    places[...] = jnp.concatenate(balanced + overflow, axis=0)
    for copy in reads[2:4]:
        copy.wait()
    half_xy = TAPS_XY // 2
    starts = [min(max(i * XB - XB // 2, 0), NX - 2 * XB) for i in range(NX // XB)]
    bands_x = {}
    for i, start in enumerate(starts):
        lead = i * XB - start
        if lead not in bands_x:
            row = placed_taps(lambda m: px_ref[0, m], TAPS_XY, 2 * XB, lambda m: lead + m - half_xy)
            distance = iota((XB, 2 * XB), 1) - iota((XB, 2 * XB), 0) - lead
            bands_x[lead] = jnp.where(jnp.abs(distance) <= half_xy, rolled(row, XB), 0.0).astype(BF16)
    matrix_y[...] = band(placed_taps(lambda m: py_ref[0, m], TAPS_XY, NY, lambda m: half_xy - m), NY, half_xy)

    est_copy.wait()
    for plane in range(SLAB):
        for i, start in enumerate(starts):
            along[plane, i * XB : (i + 1) * XB, :] = dot(
                bands_x[i * XB - start], est_ref[plane, start : start + 2 * XB, :]
            ).astype(BF16)
    chosen = tissue_tiles(mask_ref)
    row_of = [pl.multiple_of(tile // 2 * TILE, TILE) for tile in chosen]
    lane_of = [pl.multiple_of(tile % 2 * TILE, TILE) for tile in chosen]
    index = iota((slots, TILE), 0).astype(F32)
    pick, pick_more = [
        jnp.concatenate([one_hot(index == places[pl.ds(first + tile, 1), :]) for tile in chosen], axis=1)
        for first in (0, tiles)
    ]
    block = ZB // group
    r = iota((ZB, ZB), 0)
    turn = one_hot(iota((ZB, ZB), 1) == r % group * block + r // group)

    def rows_of(values, i):
        return jnp.concatenate(
            [
                values[slot * DEVS + i * block : slot * DEVS + (i + 1) * block, plane * TILE : (plane + 1) * TILE]
                for plane in range(SLAB)
                for slot in range(HALF)
            ],
            axis=0,
        )

    meas_copy.wait()
    seen = jnp.concatenate(
        [
            jnp.concatenate(
                [meas_ref[0, plane, pl.ds(row, TILE), pl.ds(lane, TILE)] for plane in range(SLAB)], axis=1
            )
            for row, lane in zip(row_of, lane_of)
        ],
        axis=0,
    )
    seen = dot(pick, seen).astype(BF16)
    blurred = []
    for row, lane in zip(row_of, lane_of):
        rows = jnp.concatenate([along[plane, pl.ds(row, TILE), :] for plane in range(SLAB)], axis=0)
        tile = dot(rows, matrix_y[:, pl.ds(lane, TILE)]).astype(BF16)
        blurred.append(
            jnp.concatenate([tile[plane * TILE : (plane + 1) * TILE] for plane in range(SLAB)], axis=1)
        )
    blurred = jnp.concatenate(blurred, axis=0)
    both = dot(jnp.concatenate([pick, pick_more], axis=0), blurred).astype(BF16)
    parts = [both[:slots], both[slots:], seen]
    for i in range(DEVS // block):
        turned = dot(turn, jnp.concatenate([rows_of(part, i) for part in parts], axis=1)).astype(BF16)
        for k in range(len(parts)):
            out_ref[i * block : (i + 1) * block, k * group : (k + 1) * group, :] = turned[
                :, k * TILE : (k + 1) * TILE
            ].reshape(block, group, TILE)
        here = pl.ds(i * block, block)
        copies.append(pltpu.make_async_copy(out_ref.at[here], out_hbm.at[here], out_sem.at[i]))
        copies[-1].start()
    for copy in copies:
        copy.wait()


def bands_kernel(pz_ref, forward_ref, adjoint_ref):
    group = SLAB * HALF
    edge = ZB // 2
    half_z = TAPS_Z // 2
    near = edge - HALF * half_z
    far = edge + HALF * half_z
    forward_ref[...] = rolled(
        placed_taps(lambda m: pz_ref[0, m], TAPS_Z, 2 * ZB, lambda m: near + HALF * m), ZB
    ).astype(BF16)
    adjoint = rolled(
        placed_taps(lambda m: pz_ref[0, m], TAPS_Z, 2 * ZB, lambda m: far - HALF * m), ZB
    ).astype(BF16)
    r = iota((ZB, ZB), 0)
    part = ZB // SLAB
    source = r % part // HALF * group + r // part * HALF + r % HALF
    adjoint_ref[...] = dot(one_hot(iota((ZB, ZB), 1) == source), adjoint).astype(BF16)


def prep_kernel(px_ref, py_ref, table_ref, est_hbm, rows_ref, units_ref, plane_ref, sem):
    plane_copy = pltpu.make_async_copy(est_hbm.at[lax.axis_index("view")], plane_ref, sem)
    plane_copy.start()
    half_xy = TAPS_XY // 2
    for view in range(VIEWS):
        rows_ref[view : view + 1, :] = placed_taps(
            lambda m: px_ref[view, m], TAPS_XY, 2 * XB, lambda m: XB // 2 + half_xy - m
        )
        rows_ref[VIEWS + view : VIEWS + view + 1, :] = placed_taps(
            lambda m: py_ref[view, m], TAPS_XY, NY, lambda m: m - half_xy
        )
    slots = HALF * DEVS
    tiles = UNITS // TILE
    table = table_ref[...].astype(F32)
    table = jnp.concatenate([table] * (TILE // tiles), axis=0).T.astype(I32)
    total = jnp.zeros((1, slots), I32)
    for tile in range(tiles):
        place = table[:, tile : tile + 1]
        place = jnp.where(place < 0, -1, place % DEVS * HALF + place // DEVS)
        unit = 2 * (tile // 2 * TILE + iota((TILE, slots), 0)) + tile % 2
        total += jnp.sum(jnp.where(place == iota((TILE, slots), 1), unit, 0), axis=0, keepdims=True)
    units_ref[...] = jnp.broadcast_to(total, (8, slots))
    plane_copy.wait()


def z_kernel(forward_ref, adjoint_ref, in_ref, back_hbm, ratio, back_ref, sems):
    group = SLAB * HALF
    rows = DEVS * group
    blocks = rows // ZB
    edge = ZB // 2
    block = ZB // group
    none = jnp.zeros((edge, TILE), BF16)

    def window(block_at):
        first, last = block_at * block - block // 2, (block_at + 1) * block + block // 2
        inner = in_ref[max(first, 0) : min(last, DEVS), 0:group, :]
        inner = inner.reshape(inner.shape[0] * group, TILE)
        return jnp.concatenate([none] * (first < 0) + [inner] + [none] * (last > DEVS), axis=0)

    ratio[0:edge, :] = none
    ratio[edge + rows :, :] = none
    for i in range(blocks // 2):
        pair = (i, i + blocks // 2)
        both = dot(forward_ref[...], jnp.concatenate([window(j) for j in pair], axis=1))
        for half, j in enumerate(pair):
            seen = in_ref[j * block : (j + 1) * block, 2 * group :, :].reshape(ZB, TILE)
            ratio[edge + j * ZB : edge + (j + 1) * ZB, :] = (
                seen.astype(F32) / both[:, half * TILE : (half + 1) * TILE]
            ).astype(BF16)
    part = ZB // SLAB
    copies = []
    for i in range(blocks // 2):
        pair = (i, i + blocks // 2)
        both = dot(
            adjoint_ref[...], jnp.concatenate([ratio[j * ZB : j * ZB + 2 * ZB, :] for j in pair], axis=1)
        ).astype(BF16)
        for half, j in enumerate(pair):
            for plane in range(SLAB):
                back_ref[plane, j * part : (j + 1) * part, :] = both[
                    plane * part : (plane + 1) * part, half * TILE : (half + 1) * TILE
                ]
        if i % 2:
            for half, j in enumerate(pair):
                here = pl.ds((j - 1) * part, 2 * part)
                copies.append(
                    pltpu.make_async_copy(back_ref.at[:, here, :], back_hbm.at[:, here, :], sems.at[i // 2, half])
                )
                copies[-1].start()
    for copy in copies:
        copy.wait()


def column_kernel(forward_ref, count_ref, in_ref, column_ref, padded):
    group = SLAB * HALF
    rows = DEVS * group
    edge = ZB // 2
    padded[0:edge, :] = jnp.zeros((edge, 2 * TILE), BF16)
    padded[edge + rows :, :] = jnp.zeros((edge, 2 * TILE), BF16)
    padded[edge : edge + rows, 0:TILE] = in_ref[:, 0:group, :].reshape(rows, TILE)
    padded[edge : edge + rows, TILE:] = in_ref[:, group : 2 * group, :].reshape(rows, TILE)
    count = count_ref[pl.ds(lax.axis_index("space"), 1), :].reshape(1, 1, TILE)
    planes = ZB // HALF
    pairs = planes // 2
    sub = iota((pairs, 8, TILE), 1)
    live = sub < count
    for block in range(rows // ZB):
        values = dot(forward_ref[...], padded[block * ZB : block * ZB + 2 * ZB, :])
        own = values[:, :TILE].reshape(pairs, 8, TILE)
        more = values[:, TILE:].reshape(pairs, 8, TILE)
        first = jnp.where(sub < HALF, own, pltpu.roll(more, HALF, 1))
        second = jnp.where(sub < HALF, pltpu.roll(own, HALF, 1), more)
        both = jnp.stack([jnp.where(live, first, 0.0), jnp.where(live, second, 0.0)], axis=1)
        column_ref[block * planes : (block + 1) * planes] = both.reshape(planes, 8, TILE).astype(BF16)


def back_kernel(
    mask_hbm, units_ref, rows_ref, in_ref, est_ref, out_ref, mask_ref, back_z, padded, mask_sem,
):
    mask_copy = pltpu.make_async_copy(mask_hbm, mask_ref, mask_sem)
    mask_copy.start()
    edge = XB // 2
    back_z[...] = jnp.ones((VIEWS, NX, NY), BF16)
    bands, matrix_y = [], []
    for view in range(VIEWS):
        bands.append(rolled(rows_ref[view : view + 1, :], XB).astype(BF16))
        matrix_y.append(band(rows_ref[VIEWS + view : VIEWS + view + 1, :], NY, TAPS_XY // 2))
        padded[view, 0:edge, :] = jnp.zeros((edge, NY), BF16)
        padded[view, edge + NX :, :] = jnp.zeros((edge, NY), BF16)
    cols = jnp.concatenate([in_ref[view] for view in range(VIEWS)], axis=1)
    units = units_ref[0:1, :]
    slots = HALF * DEVS
    mask_copy.wait()
    chosen = tissue_tiles(mask_ref)
    here = [units == 2 * (tile // 2 * TILE + iota((TILE, slots), 0)) + tile % 2 for tile in chosen]
    found = dot(jnp.concatenate([one_hot(h) for h in here], axis=0), cols).astype(BF16)
    for i, tile in enumerate(chosen):
        row = pl.multiple_of(tile // 2 * TILE, TILE)
        lane = pl.multiple_of(tile % 2 * TILE, TILE)
        for view in range(VIEWS):
            back_z[view, pl.ds(row, TILE), pl.ds(lane, TILE)] = found[
                i * TILE : (i + 1) * TILE, view * TILE : (view + 1) * TILE
            ]
    for view in range(VIEWS):
        padded[view, edge : edge + NX, :] = dot(back_z[view], matrix_y[view]).astype(BF16)
    for block in range(NX // XB):
        here = pl.ds(block * XB, XB)
        summed = jnp.zeros((XB, NY), F32)
        for view in range(VIEWS):
            summed += dot(bands[view], padded[view, block * XB : block * XB + 2 * XB, :])
        updated = (est_ref[here, :].astype(F32) * summed / VIEWS).astype(BF16)
        out_ref[0, here, :] = updated


def call(kernel, name, out_shape, in_specs, out_specs, scratch, limit, flops, moved):
    return pl.pallas_call(
        kernel,
        out_shape=out_shape,
        in_specs=in_specs,
        out_specs=out_specs,
        scratch_shapes=scratch,
        compiler_params=pltpu.CompilerParams(vmem_limit_bytes=limit * 1024 * 1024),
        cost_estimate=pl.CostEstimate(flops=flops, bytes_accessed=moved, transcendentals=0),
        name=name,
    )


def pack(estimate, measured, psf_x, psf_y, tissue_mask, column_owner):
    return call(
        pack_kernel,
        "pack",
        (shape(DEVS, MSG, TILE), shape(UNITS // TILE, TILE, dtype=I32), shape(DEVS, TILE, dtype=I32)),
        [ANY] * 6,
        (ANY, ANY, ANY),
        [
            pltpu.SMEM((UNITS // TILE,), I32),
            pltpu.SMEM((1, TAPS_XY), F32),
            pltpu.SMEM((1, TAPS_XY), F32),
            pltpu.VMEM((1, UNITS), I32),
            pltpu.VMEM((SLAB, NX, NY), BF16),
            pltpu.VMEM((1, SLAB, NX, NY), BF16),
            pltpu.VMEM((SLAB, NX, NY), BF16),
            pltpu.VMEM((2 * UNITS // TILE, TILE), F32),
            pltpu.VMEM((NY, NY), BF16),
            pltpu.VMEM((DEVS, MSG, TILE), BF16),
            pltpu.VMEM((UNITS // TILE, TILE), I32),
            pltpu.VMEM((DEVS, TILE), I32),
            pltpu.SemaphoreType.DMA((8,)),
            pltpu.SemaphoreType.DMA((DEVS * SLAB * HALF // ZB,)),
        ],
        WIDE_LIMIT,
        flops=2_000_000_000,
        moved=4_000_000,
    )(tissue_mask, psf_x, psf_y, column_owner.reshape(1, UNITS), estimate, measured)


def bands(psf_z):
    return call(
        bands_kernel,
        "bands",
        (shape(ZB, 2 * ZB), shape(ZB, 2 * ZB)),
        [SMEM],
        (VMEM, VMEM),
        [],
        LIMIT,
        flops=70_000_000,
        moved=500_000,
    )(psf_z)


def prep(taps_x, taps_y, table, estimate):
    return call(
        prep_kernel,
        "prep",
        (shape(2 * VIEWS, NY, dtype=F32), shape(8, HALF * DEVS, dtype=I32), shape(NX, NY)),
        [SMEM, SMEM, VMEM, ANY],
        (VMEM,) * 3,
        [pltpu.SemaphoreType.DMA],
        WIDE_LIMIT,
        flops=10_000_000,
        moved=1_000_000,
    )(taps_x, taps_y, table, estimate)


def z_pair(forward, adjoint, arrived):
    rows = DEVS * SLAB * HALF
    return call(
        z_kernel,
        "zpair",
        shape(VIEWS, HALF * DEVS, TILE),
        [VMEM, VMEM, VMEM],
        ANY,
        [
            pltpu.VMEM((rows + ZB, TILE), BF16),
            pltpu.VMEM((VIEWS, HALF * DEVS, TILE), BF16),
            pltpu.SemaphoreType.DMA((rows // ZB // 4, 2)),
        ],
        LIMIT,
        flops=540_000_000,
        moved=3_000_000,
    )(forward, adjoint, arrived)


def column(forward, count, arrived):
    rows = DEVS * SLAB * HALF
    return call(
        column_kernel,
        "column",
        shape(SLAB * DEVS, 2 * HALF, TILE),
        [VMEM, VMEM, VMEM],
        VMEM,
        [pltpu.VMEM((rows + ZB, 2 * TILE), BF16)],
        LIMIT,
        flops=540_000_000,
        moved=3_000_000,
    )(forward, count, arrived)


def back(tissue_mask, units, rows, returned, plane):
    return call(
        back_kernel,
        "back",
        shape(1, NX, NY),
        [ANY, VMEM, VMEM, VMEM, VMEM],
        VMEM,
        [
            pltpu.SMEM((UNITS // TILE,), I32),
            pltpu.VMEM((VIEWS, NX, NY), BF16),
            pltpu.VMEM((VIEWS, NX + XB, NY), BF16),
            pltpu.SemaphoreType.DMA,
        ],
        LIMIT,
        flops=1_400_000_000,
        moved=5_000_000,
    )(tissue_mask, units, rows, returned, plane)


def shards(estimate, measured, psf_x, psf_y, psf_z, tissue_mask, column_owner):
    message, table, count = pack(estimate, measured, psf_x, psf_y, tissue_mask, column_owner)
    message, psf_z = lax.optimization_barrier((message, psf_z))
    arrived = lax.all_to_all(message, "space", split_axis=0, concat_axis=0, tiled=True)
    forward, adjoint = bands(psf_z)
    arrived, psf_x, psf_y = lax.optimization_barrier((arrived, psf_x, psf_y))
    sent = z_pair(forward, adjoint, arrived)
    returned = lax.all_to_all(
        sent.reshape(VIEWS * DEVS, HALF, TILE),
        ("view", "space"),
        split_axis=0,
        concat_axis=0,
        tiled=True,
    ).reshape(VIEWS, HALF * DEVS, TILE)
    taps = lax.all_gather(jnp.concatenate([psf_x, psf_y], axis=1), "view", axis=0, tiled=True)
    rows, units, plane = prep(taps[:, :TAPS_XY], taps[:, TAPS_XY:], table, estimate)
    returned, column_blur = lax.optimization_barrier((returned, column(forward, count, arrived)))
    updated = back(tissue_mask, units, rows, returned, plane)
    view = lax.axis_index("view")
    gathered = jnp.zeros((VIEWS, NX, NY), BF16)
    for step in (0, 2, 1, 3):
        plane = updated
        if step:
            plane = lax.ppermute(updated, "view", [(i, (i + step) % VIEWS) for i in range(VIEWS)])
        gathered = lax.dynamic_update_slice(gathered, plane, ((view - step) % VIEWS, 0, 0))
    return gathered, column_blur[None]


def solution(mesh):
    placed = (
        P("space", None, None),
        P("view", "space", None, None),
        P("view", None),
        P("view", None),
        P("view", None),
        P(),
        P(),
    )
    return jax.shard_map(
        shards,
        mesh=mesh,
        in_specs=placed,
        out_specs=(P("space", None, None), P("view", None, "space", None)),
        check_vma=False,
    )
```

```python
import jax
import jax.numpy as jnp
from jax import lax
from jax.experimental import pallas as pl
from jax.experimental.pallas import tpu as pltpu
from jax.sharding import PartitionSpec as P

F32 = jnp.float32
BF16 = jnp.bfloat16
I32 = jnp.int32

VIEWS, DEVS = 4, 128
SLAB, NX, NY, TILE = 4, 512, 256, 128
UNITS = 1024
HALF = 4
MSG = 3 * SLAB * HALF
TAPS_XY, TAPS_Z = 31, 63
ZB = 256
XB = 128
WIDE_LIMIT, LIMIT = 60, 24

SMEM = pl.BlockSpec(memory_space=pltpu.SMEM)
VMEM = pl.BlockSpec(memory_space=pltpu.VMEM)
ANY = pl.BlockSpec(memory_space=pl.ANY)


def shape(*dims, dtype=BF16):
    return jax.ShapeDtypeStruct(dims, dtype)


def iota(shape, dim):
    return lax.broadcasted_iota(I32, shape, dim)


def placed_taps(read, count, lanes, place):
    lane = iota((1, lanes), 1)
    total = read(0)
    for m in range(1, count):
        total = total + read(m)
    row = jnp.zeros((1, lanes), F32)
    for m in range(count):
        row = jnp.where(lane == place(m) % lanes, read(m), row)
    return (row / jnp.full((1, lanes), total, F32)).astype(BF16).astype(F32)


def rolled(row, rows):
    return pltpu.roll(
        jnp.broadcast_to(row, (rows, row.shape[1])), 0, 1, stride=1, stride_axis=0
    )


def band(row, n, half):
    distance = jnp.abs(iota((n, n), 1) - iota((n, n), 0))
    return jnp.where(distance <= half, rolled(row, n), 0.0).astype(BF16)


def dot(a, b, dims=((1,), (0,))):
    return lax.dot_general(a, b, (dims, ((), ())), preferred_element_type=F32)


def one_hot(condition):
    return jnp.where(condition, 1.0, 0.0).astype(BF16)


def slot_rows(mask_ref, owner_ref):
    pairs = UNITS // ZB
    square = (DEVS, TILE)
    device = iota(square, 0).astype(F32)
    w = iota((ZB, ZB), 1)
    unit = 2 * (w % TILE) + w // TILE
    deal = one_hot(iota((ZB, ZB), 0) == unit)
    owners = jnp.concatenate([owner_ref[0:1, i * ZB : (i + 1) * ZB] for i in range(pairs)] * 2, axis=0)
    owners = dot(owners.astype(F32).astype(BF16), deal)
    row = iota((ZB, ZB), 0)
    earlier = one_hot(2 * (row % TILE) + row // TILE < unit)
    sums = jnp.concatenate([earlier, jnp.ones((ZB, TILE), BF16)], axis=1)
    count = jnp.zeros(square, F32)
    owner, member, before = [], [], []
    for pair in range(pairs):
        for t in range(2):
            here = owners[pair : pair + 1, t * TILE : (t + 1) * TILE]
            owner.append(jnp.where(mask_ref[2 * pair + t] > 0, here, -1.0))
            member.append(device == owner[-1])
        found = dot(jnp.concatenate([one_hot(m) for m in member[-2:]], axis=1), sums)
        before.append(found[:, :TILE] + count)
        before.append(found[:, TILE:ZB] + count)
        count += found[:, ZB:]
    over = jnp.maximum(count - HALF, 0.0)
    free = jnp.maximum(HALF - count, 0.0)
    lower = one_hot(iota((DEVS, DEVS), 1) < iota((DEVS, DEVS), 0))
    starts = dot(lower, jnp.concatenate([over, free], axis=1).astype(BF16))
    over_start, free_start = starts[:, :TILE], starts[:, TILE:]
    free_end = free_start + free
    place = (count - free_start) * DEVS + device
    balanced, overflow = [], []
    for mine, inside, ahead in zip(owner, member, before):
        position = jnp.sum(jnp.where(inside, ahead, 0.0), axis=0, keepdims=True)
        start = jnp.sum(jnp.where(inside, over_start, 0.0), axis=0, keepdims=True)
        rank = start + position - HALF
        found = jnp.where((free_start <= rank) & (rank < free_end), place + rank * DEVS, 0.0)
        filled = jnp.sum(found, axis=0, keepdims=True)
        own = position * DEVS + mine
        balanced.append(jnp.where(mine < 0, -1.0, jnp.where(position < HALF, own, filled)))
        overflow.append(jnp.where((mine >= 0) & (position >= HALF), own - HALF * DEVS, -1.0))
    return balanced, overflow, count


def tissue_tiles(mask_ref):
    tiles = UNITS // TILE
    found = jnp.int32(0)
    chosen = [jnp.int32(0)] * (tiles // 2)
    for tile in range(tiles):
        here = mask_ref[tile] > 0
        chosen = [jnp.where(here & (found == i), tile, old) for i, old in enumerate(chosen)]
        found += here.astype(I32)
    return chosen


def pack_kernel(
    mask_hbm, px_hbm, py_hbm, owner_hbm, est_hbm, meas_hbm, out_hbm, table_hbm, count_hbm,
    mask_ref, px_ref, py_ref, owner_ref, est_ref, meas_ref, along, places, matrix_y,
    out_ref, table_ref, count_ref, sems, out_sem,
):
    reads = [
        pltpu.make_async_copy(source, target, sems.at[i])
        for i, (source, target) in enumerate(
            zip(
                (mask_hbm, owner_hbm, px_hbm, py_hbm, est_hbm, meas_hbm),
                (mask_ref, owner_ref, px_ref, py_ref, est_ref, meas_ref),
            )
        )
    ]
    for copy in reads:
        copy.start()
    est_copy, meas_copy = reads[4:]
    for copy in reads[:2]:
        copy.wait()
    slots = HALF * DEVS
    group = SLAB * HALF
    tiles = UNITS // TILE
    balanced, overflow, count = slot_rows(mask_ref, owner_ref)
    count_ref[...] = count.astype(I32)
    table_ref[...] = jnp.concatenate(balanced, axis=0).astype(I32)
    copies = [
        pltpu.make_async_copy(table_ref, table_hbm, sems.at[6]),
        pltpu.make_async_copy(count_ref, count_hbm, sems.at[7]),
    ]
    for copy in copies:
        copy.start()
    places[...] = jnp.concatenate(balanced + overflow, axis=0)
    for copy in reads[2:4]:
        copy.wait()
    half_xy = TAPS_XY // 2
    starts = [min(max(i * XB - XB // 2, 0), NX - 2 * XB) for i in range(NX // XB)]
    bands_x = {}
    for i, start in enumerate(starts):
        lead = i * XB - start
        if lead not in bands_x:
            row = placed_taps(lambda m: px_ref[0, m], TAPS_XY, 2 * XB, lambda m: lead + m - half_xy)
            distance = iota((XB, 2 * XB), 1) - iota((XB, 2 * XB), 0) - lead
            bands_x[lead] = jnp.where(jnp.abs(distance) <= half_xy, rolled(row, XB), 0.0).astype(BF16)
    matrix_y[...] = band(placed_taps(lambda m: py_ref[0, m], TAPS_XY, NY, lambda m: half_xy - m), NY, half_xy)

    est_copy.wait()
    for plane in range(SLAB):
        for i, start in enumerate(starts):
            along[plane, i * XB : (i + 1) * XB, :] = dot(
                bands_x[i * XB - start], est_ref[plane, start : start + 2 * XB, :]
            ).astype(BF16)
    chosen = tissue_tiles(mask_ref)
    row_of = [pl.multiple_of(tile // 2 * TILE, TILE) for tile in chosen]
    lane_of = [pl.multiple_of(tile % 2 * TILE, TILE) for tile in chosen]
    index = iota((slots, TILE), 0).astype(F32)
    pick, pick_more = [
        jnp.concatenate([one_hot(index == places[pl.ds(first + tile, 1), :]) for tile in chosen], axis=1)
        for first in (0, tiles)
    ]
    block = ZB // group
    r = iota((ZB, ZB), 0)
    turn = one_hot(iota((ZB, ZB), 1) == r % group * block + r // group)

    def rows_of(values, i):
        return jnp.concatenate(
            [
                values[slot * DEVS + i * block : slot * DEVS + (i + 1) * block, plane * TILE : (plane + 1) * TILE]
                for plane in range(SLAB)
                for slot in range(HALF)
            ],
            axis=0,
        )

    meas_copy.wait()
    seen = jnp.concatenate(
        [
            jnp.concatenate(
                [meas_ref[0, plane, pl.ds(row, TILE), pl.ds(lane, TILE)] for plane in range(SLAB)], axis=1
            )
            for row, lane in zip(row_of, lane_of)
        ],
        axis=0,
    )
    seen = dot(pick, seen).astype(BF16)
    blurred = []
    for row, lane in zip(row_of, lane_of):
        rows = jnp.concatenate([along[plane, pl.ds(row, TILE), :] for plane in range(SLAB)], axis=0)
        tile = dot(rows, matrix_y[:, pl.ds(lane, TILE)]).astype(BF16)
        blurred.append(
            jnp.concatenate([tile[plane * TILE : (plane + 1) * TILE] for plane in range(SLAB)], axis=1)
        )
    blurred = jnp.concatenate(blurred, axis=0)
    both = dot(jnp.concatenate([pick, pick_more], axis=0), blurred).astype(BF16)
    parts = [both[:slots], both[slots:], seen]
    for i in range(DEVS // block):
        turned = dot(turn, jnp.concatenate([rows_of(part, i) for part in parts], axis=1)).astype(BF16)
        for k in range(len(parts)):
            out_ref[i * block : (i + 1) * block, k * group : (k + 1) * group, :] = turned[
                :, k * TILE : (k + 1) * TILE
            ].reshape(block, group, TILE)
        here = pl.ds(i * block, block)
        copies.append(pltpu.make_async_copy(out_ref.at[here], out_hbm.at[here], out_sem.at[i]))
        copies[-1].start()
    for copy in copies:
        copy.wait()


def bands_kernel(pz_ref, forward_ref, adjoint_ref):
    group = SLAB * HALF
    edge = ZB // 2
    half_z = TAPS_Z // 2
    near = edge - HALF * half_z
    far = edge + HALF * half_z
    forward_ref[...] = rolled(
        placed_taps(lambda m: pz_ref[0, m], TAPS_Z, 2 * ZB, lambda m: near + HALF * m), ZB
    ).astype(BF16)
    adjoint = rolled(
        placed_taps(lambda m: pz_ref[0, m], TAPS_Z, 2 * ZB, lambda m: far - HALF * m), ZB
    ).astype(BF16)
    r = iota((ZB, ZB), 0)
    part = ZB // SLAB
    source = r % part // HALF * group + r // part * HALF + r % HALF
    adjoint_ref[...] = dot(one_hot(iota((ZB, ZB), 1) == source), adjoint).astype(BF16)


def prep_kernel(px_ref, py_ref, table_ref, est_hbm, rows_ref, units_ref, plane_ref, sem):
    plane_copy = pltpu.make_async_copy(est_hbm.at[lax.axis_index("view")], plane_ref, sem)
    plane_copy.start()
    half_xy = TAPS_XY // 2
    for view in range(VIEWS):
        rows_ref[view : view + 1, :] = placed_taps(
            lambda m: px_ref[view, m], TAPS_XY, 2 * XB, lambda m: XB // 2 + half_xy - m
        )
        rows_ref[VIEWS + view : VIEWS + view + 1, :] = placed_taps(
            lambda m: py_ref[view, m], TAPS_XY, NY, lambda m: m - half_xy
        )
    slots = HALF * DEVS
    tiles = UNITS // TILE
    table = table_ref[...].astype(F32)
    table = jnp.concatenate([table] * (TILE // tiles), axis=0).T.astype(I32)
    total = jnp.zeros((1, slots), I32)
    for tile in range(tiles):
        place = table[:, tile : tile + 1]
        place = jnp.where(place < 0, -1, place % DEVS * HALF + place // DEVS)
        unit = 2 * (tile // 2 * TILE + iota((TILE, slots), 0)) + tile % 2
        total += jnp.sum(jnp.where(place == iota((TILE, slots), 1), unit, 0), axis=0, keepdims=True)
    units_ref[...] = jnp.broadcast_to(total, (8, slots))
    plane_copy.wait()


def z_kernel(forward_ref, adjoint_ref, in_ref, back_hbm, ratio, back_ref, sems):
    group = SLAB * HALF
    rows = DEVS * group
    blocks = rows // ZB
    edge = ZB // 2
    block = ZB // group
    none = jnp.zeros((edge, TILE), BF16)

    def window(block_at):
        first, last = block_at * block - block // 2, (block_at + 1) * block + block // 2
        inner = in_ref[max(first, 0) : min(last, DEVS), 0:group, :]
        inner = inner.reshape(inner.shape[0] * group, TILE)
        return jnp.concatenate([none] * (first < 0) + [inner] + [none] * (last > DEVS), axis=0)

    ratio[0:edge, :] = none
    ratio[edge + rows :, :] = none
    for i in range(blocks // 2):
        pair = (i, i + blocks // 2)
        both = dot(forward_ref[...], jnp.concatenate([window(j) for j in pair], axis=1))
        for half, j in enumerate(pair):
            seen = in_ref[j * block : (j + 1) * block, 2 * group :, :].reshape(ZB, TILE)
            ratio[edge + j * ZB : edge + (j + 1) * ZB, :] = (
                seen.astype(F32) / both[:, half * TILE : (half + 1) * TILE]
            ).astype(BF16)
    part = ZB // SLAB
    copies = []
    for i in range(blocks // 2):
        pair = (i, i + blocks // 2)
        both = dot(
            adjoint_ref[...], jnp.concatenate([ratio[j * ZB : j * ZB + 2 * ZB, :] for j in pair], axis=1)
        ).astype(BF16)
        for half, j in enumerate(pair):
            for plane in range(SLAB):
                back_ref[plane, j * part : (j + 1) * part, :] = both[
                    plane * part : (plane + 1) * part, half * TILE : (half + 1) * TILE
                ]
        if i % 2:
            for half, j in enumerate(pair):
                here = pl.ds((j - 1) * part, 2 * part)
                copies.append(
                    pltpu.make_async_copy(back_ref.at[:, here, :], back_hbm.at[:, here, :], sems.at[i // 2, half])
                )
                copies[-1].start()
    for copy in copies:
        copy.wait()


def column_kernel(forward_ref, count_ref, in_ref, column_ref, padded):
    group = SLAB * HALF
    rows = DEVS * group
    edge = ZB // 2
    padded[0:edge, :] = jnp.zeros((edge, 2 * TILE), BF16)
    padded[edge + rows :, :] = jnp.zeros((edge, 2 * TILE), BF16)
    padded[edge : edge + rows, 0:TILE] = in_ref[:, 0:group, :].reshape(rows, TILE)
    padded[edge : edge + rows, TILE:] = in_ref[:, group : 2 * group, :].reshape(rows, TILE)
    count = count_ref[pl.ds(lax.axis_index("space"), 1), :].reshape(1, 1, TILE)
    planes = ZB // HALF
    pairs = planes // 2
    sub = iota((pairs, 8, TILE), 1)
    live = sub < count
    for block in range(rows // ZB):
        values = dot(forward_ref[...], padded[block * ZB : block * ZB + 2 * ZB, :])
        own = values[:, :TILE].reshape(pairs, 8, TILE)
        more = values[:, TILE:].reshape(pairs, 8, TILE)
        first = jnp.where(sub < HALF, own, pltpu.roll(more, HALF, 1))
        second = jnp.where(sub < HALF, pltpu.roll(own, HALF, 1), more)
        both = jnp.stack([jnp.where(live, first, 0.0), jnp.where(live, second, 0.0)], axis=1)
        column_ref[block * planes : (block + 1) * planes] = both.reshape(planes, 8, TILE).astype(BF16)


def back_kernel(
    mask_hbm, units_ref, rows_ref, in_ref, est_ref, out_ref, mask_ref, back_z, padded, mask_sem,
):
    mask_copy = pltpu.make_async_copy(mask_hbm, mask_ref, mask_sem)
    mask_copy.start()
    edge = XB // 2
    back_z[...] = jnp.ones((VIEWS, NX, NY), BF16)
    bands, matrix_y = [], []
    for view in range(VIEWS):
        bands.append(rolled(rows_ref[view : view + 1, :], XB).astype(BF16))
        matrix_y.append(band(rows_ref[VIEWS + view : VIEWS + view + 1, :], NY, TAPS_XY // 2))
        padded[view, 0:edge, :] = jnp.zeros((edge, NY), BF16)
        padded[view, edge + NX :, :] = jnp.zeros((edge, NY), BF16)
    cols = jnp.concatenate([in_ref[view] for view in range(VIEWS)], axis=1)
    units = units_ref[0:1, :]
    slots = HALF * DEVS
    mask_copy.wait()
    chosen = tissue_tiles(mask_ref)
    here = [units == 2 * (tile // 2 * TILE + iota((TILE, slots), 0)) + tile % 2 for tile in chosen]
    found = dot(jnp.concatenate([one_hot(h) for h in here], axis=0), cols).astype(BF16)
    for i, tile in enumerate(chosen):
        row = pl.multiple_of(tile // 2 * TILE, TILE)
        lane = pl.multiple_of(tile % 2 * TILE, TILE)
        for view in range(VIEWS):
            back_z[view, pl.ds(row, TILE), pl.ds(lane, TILE)] = found[
                i * TILE : (i + 1) * TILE, view * TILE : (view + 1) * TILE
            ]
    for view in range(VIEWS):
        padded[view, edge : edge + NX, :] = dot(back_z[view], matrix_y[view]).astype(BF16)
    for block in range(NX // XB):
        here = pl.ds(block * XB, XB)
        summed = jnp.zeros((XB, NY), F32)
        for view in range(VIEWS):
            summed += dot(bands[view], padded[view, block * XB : block * XB + 2 * XB, :])
        updated = (est_ref[here, :].astype(F32) * summed / VIEWS).astype(BF16)
        for view in range(VIEWS):
            out_ref[view, here, :] = updated


def call(kernel, name, out_shape, in_specs, out_specs, scratch, limit, flops, moved):
    return pl.pallas_call(
        kernel,
        out_shape=out_shape,
        in_specs=in_specs,
        out_specs=out_specs,
        scratch_shapes=scratch,
        compiler_params=pltpu.CompilerParams(vmem_limit_bytes=limit * 1024 * 1024),
        cost_estimate=pl.CostEstimate(flops=flops, bytes_accessed=moved, transcendentals=0),
        name=name,
    )


def pack(estimate, measured, psf_x, psf_y, tissue_mask, column_owner):
    return call(
        pack_kernel,
        "pack",
        (shape(DEVS, MSG, TILE), shape(UNITS // TILE, TILE, dtype=I32), shape(DEVS, TILE, dtype=I32)),
        [ANY] * 6,
        (ANY, ANY, ANY),
        [
            pltpu.SMEM((UNITS // TILE,), I32),
            pltpu.SMEM((1, TAPS_XY), F32),
            pltpu.SMEM((1, TAPS_XY), F32),
            pltpu.VMEM((1, UNITS), I32),
            pltpu.VMEM((SLAB, NX, NY), BF16),
            pltpu.VMEM((1, SLAB, NX, NY), BF16),
            pltpu.VMEM((SLAB, NX, NY), BF16),
            pltpu.VMEM((2 * UNITS // TILE, TILE), F32),
            pltpu.VMEM((NY, NY), BF16),
            pltpu.VMEM((DEVS, MSG, TILE), BF16),
            pltpu.VMEM((UNITS // TILE, TILE), I32),
            pltpu.VMEM((DEVS, TILE), I32),
            pltpu.SemaphoreType.DMA((8,)),
            pltpu.SemaphoreType.DMA((DEVS * SLAB * HALF // ZB,)),
        ],
        WIDE_LIMIT,
        flops=2_000_000_000,
        moved=4_000_000,
    )(tissue_mask, psf_x, psf_y, column_owner.reshape(1, UNITS), estimate, measured)


def bands(psf_z):
    return call(
        bands_kernel,
        "bands",
        (shape(ZB, 2 * ZB), shape(ZB, 2 * ZB)),
        [SMEM],
        (VMEM, VMEM),
        [],
        LIMIT,
        flops=70_000_000,
        moved=500_000,
    )(psf_z)


def prep(taps_x, taps_y, table, estimate):
    return call(
        prep_kernel,
        "prep",
        (shape(2 * VIEWS, NY, dtype=F32), shape(8, HALF * DEVS, dtype=I32), shape(NX, NY)),
        [SMEM, SMEM, VMEM, ANY],
        (VMEM,) * 3,
        [pltpu.SemaphoreType.DMA],
        WIDE_LIMIT,
        flops=10_000_000,
        moved=1_000_000,
    )(taps_x, taps_y, table, estimate)


def z_pair(forward, adjoint, arrived):
    rows = DEVS * SLAB * HALF
    return call(
        z_kernel,
        "zpair",
        shape(VIEWS, HALF * DEVS, TILE),
        [VMEM, VMEM, VMEM],
        ANY,
        [
            pltpu.VMEM((rows + ZB, TILE), BF16),
            pltpu.VMEM((VIEWS, HALF * DEVS, TILE), BF16),
            pltpu.SemaphoreType.DMA((rows // ZB // 4, 2)),
        ],
        LIMIT,
        flops=540_000_000,
        moved=3_000_000,
    )(forward, adjoint, arrived)


def column(forward, count, arrived):
    rows = DEVS * SLAB * HALF
    return call(
        column_kernel,
        "column",
        shape(SLAB * DEVS, 2 * HALF, TILE),
        [VMEM, VMEM, VMEM],
        VMEM,
        [pltpu.VMEM((rows + ZB, 2 * TILE), BF16)],
        LIMIT,
        flops=540_000_000,
        moved=3_000_000,
    )(forward, count, arrived)


def back(tissue_mask, units, rows, returned, plane):
    return call(
        back_kernel,
        "back",
        shape(VIEWS, NX, NY),
        [ANY, VMEM, VMEM, VMEM, VMEM],
        VMEM,
        [
            pltpu.SMEM((UNITS // TILE,), I32),
            pltpu.VMEM((VIEWS, NX, NY), BF16),
            pltpu.VMEM((VIEWS, NX + XB, NY), BF16),
            pltpu.SemaphoreType.DMA,
        ],
        LIMIT,
        flops=1_400_000_000,
        moved=5_000_000,
    )(tissue_mask, units, rows, returned, plane)


def shards(estimate, measured, psf_x, psf_y, psf_z, tissue_mask, column_owner):
    message, table, count = pack(estimate, measured, psf_x, psf_y, tissue_mask, column_owner)
    message, psf_z = lax.optimization_barrier((message, psf_z))
    arrived = lax.all_to_all(message, "space", split_axis=0, concat_axis=0, tiled=True)
    forward, adjoint = bands(psf_z)
    arrived, psf_x, psf_y = lax.optimization_barrier((arrived, psf_x, psf_y))
    sent = z_pair(forward, adjoint, arrived)
    returned = lax.all_to_all(
        sent.reshape(VIEWS * DEVS, HALF, TILE),
        ("view", "space"),
        split_axis=0,
        concat_axis=0,
        tiled=True,
    ).reshape(VIEWS, HALF * DEVS, TILE)
    taps = lax.all_gather(jnp.concatenate([psf_x, psf_y], axis=1), "view", axis=0, tiled=True)
    rows, units, plane = prep(taps[:, :TAPS_XY], taps[:, TAPS_XY:], table, estimate)
    returned, column_blur = lax.optimization_barrier((returned, column(forward, count, arrived)))
    updated = back(tissue_mask, units, rows, returned, plane)
    updated = lax.all_to_all(updated, "view", split_axis=0, concat_axis=0, tiled=True)
    return updated, column_blur[None]


def solution(mesh):
    placed = (
        P("space", None, None),
        P("view", "space", None, None),
        P("view", None),
        P("view", None),
        P("view", None),
        P(),
        P(),
    )
    return jax.shard_map(
        shards,
        mesh=mesh,
        in_specs=placed,
        out_specs=(P("space", None, None), P("view", None, "space", None)),
        check_vma=False,
    )
```

```python
import jax
import jax.numpy as jnp
from jax import lax
from jax.experimental import pallas as pl
from jax.experimental.pallas import tpu as pltpu
from jax.sharding import PartitionSpec as P

F32 = jnp.float32
BF16 = jnp.bfloat16
I32 = jnp.int32

VIEWS, DEVS = 4, 128
SLAB, NX, NY, TILE = 4, 512, 256, 128
UNITS = 1024
HALF = 4
MSG = 3 * SLAB * HALF
TAPS_XY, TAPS_Z = 31, 63
ZB = 256
XB = 128
WIDE_LIMIT, LIMIT = 60, 24

SMEM = pl.BlockSpec(memory_space=pltpu.SMEM)
VMEM = pl.BlockSpec(memory_space=pltpu.VMEM)
ANY = pl.BlockSpec(memory_space=pl.ANY)


def shape(*dims, dtype=BF16):
    return jax.ShapeDtypeStruct(dims, dtype)


def iota(shape, dim):
    return lax.broadcasted_iota(I32, shape, dim)


def placed_taps(read, count, lanes, place):
    lane = iota((1, lanes), 1)
    total = read(0)
    for m in range(1, count):
        total = total + read(m)
    row = jnp.zeros((1, lanes), F32)
    for m in range(count):
        row = jnp.where(lane == place(m) % lanes, read(m), row)
    return (row / jnp.full((1, lanes), total, F32)).astype(BF16).astype(F32)


def rolled(row, rows):
    return pltpu.roll(
        jnp.broadcast_to(row, (rows, row.shape[1])), 0, 1, stride=1, stride_axis=0
    )


def band(row, n, half):
    distance = jnp.abs(iota((n, n), 1) - iota((n, n), 0))
    return jnp.where(distance <= half, rolled(row, n), 0.0).astype(BF16)


def dot(a, b, dims=((1,), (0,))):
    return lax.dot_general(a, b, (dims, ((), ())), preferred_element_type=F32)


def one_hot(condition):
    return jnp.where(condition, 1.0, 0.0).astype(BF16)


def slot_rows(mask_ref, owner_ref):
    pairs = UNITS // ZB
    square = (DEVS, TILE)
    device = iota(square, 0).astype(F32)
    w = iota((ZB, ZB), 1)
    unit = 2 * (w % TILE) + w // TILE
    deal = one_hot(iota((ZB, ZB), 0) == unit)
    owners = jnp.concatenate([owner_ref[0:1, i * ZB : (i + 1) * ZB] for i in range(pairs)] * 2, axis=0)
    owners = dot(owners.astype(F32).astype(BF16), deal)
    row = iota((ZB, ZB), 0)
    earlier = one_hot(2 * (row % TILE) + row // TILE < unit)
    sums = jnp.concatenate([earlier, jnp.ones((ZB, TILE), BF16)], axis=1)
    count = jnp.zeros(square, F32)
    owner, member, before = [], [], []
    for pair in range(pairs):
        for t in range(2):
            here = owners[pair : pair + 1, t * TILE : (t + 1) * TILE]
            owner.append(jnp.where(mask_ref[2 * pair + t] > 0, here, -1.0))
            member.append(device == owner[-1])
        found = dot(jnp.concatenate([one_hot(m) for m in member[-2:]], axis=1), sums)
        before.append(found[:, :TILE] + count)
        before.append(found[:, TILE:ZB] + count)
        count += found[:, ZB:]
    over = jnp.maximum(count - HALF, 0.0)
    free = jnp.maximum(HALF - count, 0.0)
    lower = one_hot(iota((DEVS, DEVS), 1) < iota((DEVS, DEVS), 0))
    starts = dot(lower, jnp.concatenate([over, free], axis=1).astype(BF16))
    over_start, free_start = starts[:, :TILE], starts[:, TILE:]
    free_end = free_start + free
    place = (count - free_start) * DEVS + device
    balanced, overflow = [], []
    for mine, inside, ahead in zip(owner, member, before):
        position = jnp.sum(jnp.where(inside, ahead, 0.0), axis=0, keepdims=True)
        start = jnp.sum(jnp.where(inside, over_start, 0.0), axis=0, keepdims=True)
        rank = start + position - HALF
        found = jnp.where((free_start <= rank) & (rank < free_end), place + rank * DEVS, 0.0)
        filled = jnp.sum(found, axis=0, keepdims=True)
        own = position * DEVS + mine
        balanced.append(jnp.where(mine < 0, -1.0, jnp.where(position < HALF, own, filled)))
        overflow.append(jnp.where((mine >= 0) & (position >= HALF), own - HALF * DEVS, -1.0))
    return balanced, overflow, count


def tissue_tiles(mask_ref):
    tiles = UNITS // TILE
    found = jnp.int32(0)
    chosen = [jnp.int32(0)] * (tiles // 2)
    for tile in range(tiles):
        here = mask_ref[tile] > 0
        chosen = [jnp.where(here & (found == i), tile, old) for i, old in enumerate(chosen)]
        found += here.astype(I32)
    return chosen


def pack_kernel(
    mask_hbm, px_hbm, py_hbm, owner_hbm, est_hbm, meas_hbm, out_hbm, table_hbm, count_hbm,
    mask_ref, px_ref, py_ref, owner_ref, est_ref, meas_ref, along, places, matrix_y,
    out_ref, table_ref, count_ref, sems, out_sem,
):
    reads = [
        pltpu.make_async_copy(source, target, sems.at[i])
        for i, (source, target) in enumerate(
            zip(
                (mask_hbm, owner_hbm, px_hbm, py_hbm, est_hbm, meas_hbm),
                (mask_ref, owner_ref, px_ref, py_ref, est_ref, meas_ref),
            )
        )
    ]
    for copy in reads:
        copy.start()
    est_copy, meas_copy = reads[4:]
    for copy in reads[:2]:
        copy.wait()
    slots = HALF * DEVS
    group = SLAB * HALF
    tiles = UNITS // TILE
    balanced, overflow, count = slot_rows(mask_ref, owner_ref)
    count_ref[...] = count.astype(I32)
    table_ref[...] = jnp.concatenate(balanced, axis=0).astype(I32)
    copies = [
        pltpu.make_async_copy(table_ref, table_hbm, sems.at[6]),
        pltpu.make_async_copy(count_ref, count_hbm, sems.at[7]),
    ]
    for copy in copies:
        copy.start()
    places[...] = jnp.concatenate(balanced + overflow, axis=0)
    for copy in reads[2:4]:
        copy.wait()
    half_xy = TAPS_XY // 2
    starts = [min(max(i * XB - XB // 2, 0), NX - 2 * XB) for i in range(NX // XB)]
    bands_x = {}
    for i, start in enumerate(starts):
        lead = i * XB - start
        if lead not in bands_x:
            row = placed_taps(lambda m: px_ref[0, m], TAPS_XY, 2 * XB, lambda m: lead + m - half_xy)
            distance = iota((XB, 2 * XB), 1) - iota((XB, 2 * XB), 0) - lead
            bands_x[lead] = jnp.where(jnp.abs(distance) <= half_xy, rolled(row, XB), 0.0).astype(BF16)
    matrix_y[...] = band(placed_taps(lambda m: py_ref[0, m], TAPS_XY, NY, lambda m: half_xy - m), NY, half_xy)

    est_copy.wait()
    for plane in range(SLAB):
        for i, start in enumerate(starts):
            along[plane, i * XB : (i + 1) * XB, :] = dot(
                bands_x[i * XB - start], est_ref[plane, start : start + 2 * XB, :]
            ).astype(BF16)
    chosen = tissue_tiles(mask_ref)
    row_of = [pl.multiple_of(tile // 2 * TILE, TILE) for tile in chosen]
    lane_of = [pl.multiple_of(tile % 2 * TILE, TILE) for tile in chosen]
    index = iota((slots, TILE), 0).astype(F32)
    pick, pick_more = [
        jnp.concatenate([one_hot(index == places[pl.ds(first + tile, 1), :]) for tile in chosen], axis=1)
        for first in (0, tiles)
    ]
    block = ZB // group
    r = iota((ZB, ZB), 0)
    turn = one_hot(iota((ZB, ZB), 1) == r % group * block + r // group)

    def rows_of(values, i):
        return jnp.concatenate(
            [
                values[slot * DEVS + i * block : slot * DEVS + (i + 1) * block, plane * TILE : (plane + 1) * TILE]
                for plane in range(SLAB)
                for slot in range(HALF)
            ],
            axis=0,
        )

    meas_copy.wait()
    seen = jnp.concatenate(
        [
            jnp.concatenate(
                [meas_ref[0, plane, pl.ds(row, TILE), pl.ds(lane, TILE)] for plane in range(SLAB)], axis=1
            )
            for row, lane in zip(row_of, lane_of)
        ],
        axis=0,
    )
    seen = dot(pick, seen).astype(BF16)
    blurred = []
    for row, lane in zip(row_of, lane_of):
        rows = jnp.concatenate([along[plane, pl.ds(row, TILE), :] for plane in range(SLAB)], axis=0)
        tile = dot(rows, matrix_y[:, pl.ds(lane, TILE)]).astype(BF16)
        blurred.append(
            jnp.concatenate([tile[plane * TILE : (plane + 1) * TILE] for plane in range(SLAB)], axis=1)
        )
    blurred = jnp.concatenate(blurred, axis=0)
    both = dot(jnp.concatenate([pick, pick_more], axis=0), blurred).astype(BF16)
    parts = [both[:slots], both[slots:], seen]
    for i in range(DEVS // block):
        turned = dot(turn, jnp.concatenate([rows_of(part, i) for part in parts], axis=1)).astype(BF16)
        for k in range(len(parts)):
            out_ref[i * block : (i + 1) * block, k * group : (k + 1) * group, :] = turned[
                :, k * TILE : (k + 1) * TILE
            ].reshape(block, group, TILE)
        here = pl.ds(i * block, block)
        copies.append(pltpu.make_async_copy(out_ref.at[here], out_hbm.at[here], out_sem.at[i]))
        copies[-1].start()
    for copy in copies:
        copy.wait()


def bands_kernel(pz_ref, forward_ref, adjoint_ref):
    group = SLAB * HALF
    edge = ZB // 2
    half_z = TAPS_Z // 2
    near = edge - HALF * half_z
    far = edge + HALF * half_z
    forward_ref[...] = rolled(
        placed_taps(lambda m: pz_ref[0, m], TAPS_Z, 2 * ZB, lambda m: near + HALF * m), ZB
    ).astype(BF16)
    adjoint = rolled(
        placed_taps(lambda m: pz_ref[0, m], TAPS_Z, 2 * ZB, lambda m: far - HALF * m), ZB
    ).astype(BF16)
    r = iota((ZB, ZB), 0)
    part = ZB // SLAB
    source = r % part // HALF * group + r // part * HALF + r % HALF
    adjoint_ref[...] = dot(one_hot(iota((ZB, ZB), 1) == source), adjoint).astype(BF16)


def prep_kernel(mask_ref, px_ref, py_ref, table_ref, est_hbm, rows_ref, units_ref, plane_ref, sem):
    plane_copy = pltpu.make_async_copy(est_hbm.at[lax.axis_index("view")], plane_ref, sem)
    plane_copy.start()
    half_xy = TAPS_XY // 2
    for view in range(VIEWS):
        rows_ref[view : view + 1, :] = placed_taps(
            lambda m: px_ref[view, m], TAPS_XY, 2 * XB, lambda m: XB // 2 + half_xy - m
        )
        rows_ref[VIEWS + view : VIEWS + view + 1, :] = placed_taps(
            lambda m: py_ref[view, m], TAPS_XY, NY, lambda m: m - half_xy
        )
    slots = HALF * DEVS
    tiles = UNITS // TILE
    table = table_ref[...].astype(F32)
    table = jnp.concatenate([table] * (TILE // tiles), axis=0).T.astype(I32)
    total = jnp.zeros((1, slots), I32)
    rank = jnp.int32(0)
    for tile in range(tiles):
        place = table[:, tile : tile + 1]
        place = jnp.where(place < 0, -1, place % DEVS * HALF + place // DEVS)
        unit = rank * TILE + iota((TILE, slots), 0)
        rank += mask_ref[tile]
        total += jnp.sum(jnp.where(place == iota((TILE, slots), 1), unit, 0), axis=0, keepdims=True)
    units_ref[...] = jnp.broadcast_to(total, (8, slots))
    plane_copy.wait()


def z_kernel(forward_ref, adjoint_ref, in_ref, back_hbm, ratio, back_ref, sems):
    group = SLAB * HALF
    rows = DEVS * group
    blocks = rows // ZB
    edge = ZB // 2
    block = ZB // group
    none = jnp.zeros((edge, TILE), BF16)

    def window(block_at):
        first, last = block_at * block - block // 2, (block_at + 1) * block + block // 2
        inner = in_ref[max(first, 0) : min(last, DEVS), 0:group, :]
        inner = inner.reshape(inner.shape[0] * group, TILE)
        return jnp.concatenate([none] * (first < 0) + [inner] + [none] * (last > DEVS), axis=0)

    ratio[0:edge, :] = none
    ratio[edge + rows :, :] = none
    for i in range(blocks // 2):
        pair = (i, i + blocks // 2)
        both = dot(forward_ref[...], jnp.concatenate([window(j) for j in pair], axis=1))
        for half, j in enumerate(pair):
            seen = in_ref[j * block : (j + 1) * block, 2 * group :, :].reshape(ZB, TILE)
            ratio[edge + j * ZB : edge + (j + 1) * ZB, :] = (
                seen.astype(F32) / both[:, half * TILE : (half + 1) * TILE]
            ).astype(BF16)
    part = ZB // SLAB
    copies = []
    for i in range(blocks // 2):
        pair = (i, i + blocks // 2)
        both = dot(
            adjoint_ref[...], jnp.concatenate([ratio[j * ZB : j * ZB + 2 * ZB, :] for j in pair], axis=1)
        ).astype(BF16)
        for half, j in enumerate(pair):
            for plane in range(SLAB):
                back_ref[plane, j * part : (j + 1) * part, :] = both[
                    plane * part : (plane + 1) * part, half * TILE : (half + 1) * TILE
                ]
        if i % 2:
            for half, j in enumerate(pair):
                here = pl.ds((j - 1) * part, 2 * part)
                copies.append(
                    pltpu.make_async_copy(back_ref.at[:, here, :], back_hbm.at[:, here, :], sems.at[i // 2, half])
                )
                copies[-1].start()
    for copy in copies:
        copy.wait()


def column_kernel(forward_ref, count_ref, in_ref, column_ref, padded):
    group = SLAB * HALF
    rows = DEVS * group
    edge = ZB // 2
    padded[0:edge, :] = jnp.zeros((edge, 2 * TILE), BF16)
    padded[edge + rows :, :] = jnp.zeros((edge, 2 * TILE), BF16)
    padded[edge : edge + rows, 0:TILE] = in_ref[:, 0:group, :].reshape(rows, TILE)
    padded[edge : edge + rows, TILE:] = in_ref[:, group : 2 * group, :].reshape(rows, TILE)
    count = count_ref[pl.ds(lax.axis_index("space"), 1), :].reshape(1, 1, TILE)
    planes = ZB // HALF
    pairs = planes // 2
    sub = iota((pairs, 8, TILE), 1)
    live = sub < count
    for block in range(rows // ZB):
        values = dot(forward_ref[...], padded[block * ZB : block * ZB + 2 * ZB, :])
        own = values[:, :TILE].reshape(pairs, 8, TILE)
        more = values[:, TILE:].reshape(pairs, 8, TILE)
        first = jnp.where(sub < HALF, own, pltpu.roll(more, HALF, 1))
        second = jnp.where(sub < HALF, pltpu.roll(own, HALF, 1), more)
        both = jnp.stack([jnp.where(live, first, 0.0), jnp.where(live, second, 0.0)], axis=1)
        column_ref[block * planes : (block + 1) * planes] = both.reshape(planes, 8, TILE).astype(BF16)


def back_kernel(
    mask_hbm, units_ref, rows_ref, in_ref, est_ref, out_ref, mask_ref, back_z, padded, mask_sem,
):
    mask_copy = pltpu.make_async_copy(mask_hbm, mask_ref, mask_sem)
    mask_copy.start()
    edge = XB // 2
    back_z[...] = jnp.ones((VIEWS, NX, NY), BF16)
    bands, matrix_y = [], []
    for view in range(VIEWS):
        bands.append(rolled(rows_ref[view : view + 1, :], XB).astype(BF16))
        matrix_y.append(band(rows_ref[VIEWS + view : VIEWS + view + 1, :], NY, TAPS_XY // 2))
        padded[view, 0:edge, :] = jnp.zeros((edge, NY), BF16)
        padded[view, edge + NX :, :] = jnp.zeros((edge, NY), BF16)
    cols = jnp.concatenate([in_ref[view] for view in range(VIEWS)], axis=1)
    units = units_ref[0:1, :]
    slots = HALF * DEVS
    found = dot(one_hot(units == iota((slots, slots), 0)), cols).astype(BF16)
    mask_copy.wait()
    chosen = tissue_tiles(mask_ref)
    for i, tile in enumerate(chosen):
        row = pl.multiple_of(tile // 2 * TILE, TILE)
        lane = pl.multiple_of(tile % 2 * TILE, TILE)
        for view in range(VIEWS):
            back_z[view, pl.ds(row, TILE), pl.ds(lane, TILE)] = found[
                i * TILE : (i + 1) * TILE, view * TILE : (view + 1) * TILE
            ]
    for view in range(VIEWS):
        padded[view, edge : edge + NX, :] = dot(back_z[view], matrix_y[view]).astype(BF16)
    for block in range(NX // XB):
        here = pl.ds(block * XB, XB)
        summed = jnp.zeros((XB, NY), F32)
        for view in range(VIEWS):
            summed += dot(bands[view], padded[view, block * XB : block * XB + 2 * XB, :])
        updated = (est_ref[here, :].astype(F32) * summed / VIEWS).astype(BF16)
        for view in range(VIEWS):
            out_ref[view, here, :] = updated


def call(kernel, name, out_shape, in_specs, out_specs, scratch, limit, flops, moved):
    return pl.pallas_call(
        kernel,
        out_shape=out_shape,
        in_specs=in_specs,
        out_specs=out_specs,
        scratch_shapes=scratch,
        compiler_params=pltpu.CompilerParams(vmem_limit_bytes=limit * 1024 * 1024),
        cost_estimate=pl.CostEstimate(flops=flops, bytes_accessed=moved, transcendentals=0),
        name=name,
    )


def pack(estimate, measured, psf_x, psf_y, tissue_mask, column_owner):
    return call(
        pack_kernel,
        "pack",
        (shape(DEVS, MSG, TILE), shape(UNITS // TILE, TILE, dtype=I32), shape(DEVS, TILE, dtype=I32)),
        [ANY] * 6,
        (ANY, ANY, ANY),
        [
            pltpu.SMEM((UNITS // TILE,), I32),
            pltpu.SMEM((1, TAPS_XY), F32),
            pltpu.SMEM((1, TAPS_XY), F32),
            pltpu.VMEM((1, UNITS), I32),
            pltpu.VMEM((SLAB, NX, NY), BF16),
            pltpu.VMEM((1, SLAB, NX, NY), BF16),
            pltpu.VMEM((SLAB, NX, NY), BF16),
            pltpu.VMEM((2 * UNITS // TILE, TILE), F32),
            pltpu.VMEM((NY, NY), BF16),
            pltpu.VMEM((DEVS, MSG, TILE), BF16),
            pltpu.VMEM((UNITS // TILE, TILE), I32),
            pltpu.VMEM((DEVS, TILE), I32),
            pltpu.SemaphoreType.DMA((8,)),
            pltpu.SemaphoreType.DMA((DEVS * SLAB * HALF // ZB,)),
        ],
        WIDE_LIMIT,
        flops=2_000_000_000,
        moved=4_000_000,
    )(tissue_mask, psf_x, psf_y, column_owner.reshape(1, UNITS), estimate, measured)


def bands(psf_z):
    return call(
        bands_kernel,
        "bands",
        (shape(ZB, 2 * ZB), shape(ZB, 2 * ZB)),
        [SMEM],
        (VMEM, VMEM),
        [],
        LIMIT,
        flops=70_000_000,
        moved=500_000,
    )(psf_z)


def prep(tissue_mask, taps_x, taps_y, table, estimate):
    return call(
        prep_kernel,
        "prep",
        (shape(2 * VIEWS, NY, dtype=F32), shape(8, HALF * DEVS, dtype=I32), shape(NX, NY)),
        [SMEM, SMEM, SMEM, VMEM, ANY],
        (VMEM,) * 3,
        [pltpu.SemaphoreType.DMA],
        WIDE_LIMIT,
        flops=10_000_000,
        moved=1_000_000,
    )(tissue_mask, taps_x, taps_y, table, estimate)


def z_pair(forward, adjoint, arrived):
    rows = DEVS * SLAB * HALF
    return call(
        z_kernel,
        "zpair",
        shape(VIEWS, HALF * DEVS, TILE),
        [VMEM, VMEM, VMEM],
        ANY,
        [
            pltpu.VMEM((rows + ZB, TILE), BF16),
            pltpu.VMEM((VIEWS, HALF * DEVS, TILE), BF16),
            pltpu.SemaphoreType.DMA((rows // ZB // 4, 2)),
        ],
        LIMIT,
        flops=540_000_000,
        moved=3_000_000,
    )(forward, adjoint, arrived)


def column(forward, count, arrived):
    rows = DEVS * SLAB * HALF
    return call(
        column_kernel,
        "column",
        shape(SLAB * DEVS, 2 * HALF, TILE),
        [VMEM, VMEM, VMEM],
        VMEM,
        [pltpu.VMEM((rows + ZB, 2 * TILE), BF16)],
        LIMIT,
        flops=540_000_000,
        moved=3_000_000,
    )(forward, count, arrived)


def back(tissue_mask, units, rows, returned, plane):
    return call(
        back_kernel,
        "back",
        shape(VIEWS, NX, NY),
        [ANY, VMEM, VMEM, VMEM, VMEM],
        VMEM,
        [
            pltpu.SMEM((UNITS // TILE,), I32),
            pltpu.VMEM((VIEWS, NX, NY), BF16),
            pltpu.VMEM((VIEWS, NX + XB, NY), BF16),
            pltpu.SemaphoreType.DMA,
        ],
        LIMIT,
        flops=1_400_000_000,
        moved=5_000_000,
    )(tissue_mask, units, rows, returned, plane)


def shards(estimate, measured, psf_x, psf_y, psf_z, tissue_mask, column_owner):
    message, table, count = pack(estimate, measured, psf_x, psf_y, tissue_mask, column_owner)
    message, psf_z = lax.optimization_barrier((message, psf_z))
    arrived = lax.all_to_all(message, "space", split_axis=0, concat_axis=0, tiled=True)
    forward, adjoint = bands(psf_z)
    arrived, psf_x, psf_y = lax.optimization_barrier((arrived, psf_x, psf_y))
    sent = z_pair(forward, adjoint, arrived)
    returned = lax.all_to_all(
        sent.reshape(VIEWS * DEVS, HALF, TILE),
        ("view", "space"),
        split_axis=0,
        concat_axis=0,
        tiled=True,
    ).reshape(VIEWS, HALF * DEVS, TILE)
    taps = lax.all_gather(jnp.concatenate([psf_x, psf_y], axis=1), "view", axis=0, tiled=True)
    rows, units, plane = prep(tissue_mask, taps[:, :TAPS_XY], taps[:, TAPS_XY:], table, estimate)
    returned, column_blur = lax.optimization_barrier((returned, column(forward, count, arrived)))
    updated = back(tissue_mask, units, rows, returned, plane)
    updated = lax.all_to_all(updated, "view", split_axis=0, concat_axis=0, tiled=True)
    return updated, column_blur[None]


def solution(mesh):
    placed = (
        P("space", None, None),
        P("view", "space", None, None),
        P("view", None),
        P("view", None),
        P("view", None),
        P(),
        P(),
    )
    return jax.shard_map(
        shards,
        mesh=mesh,
        in_specs=placed,
        out_specs=(P("space", None, None), P("view", None, "space", None)),
        check_vma=False,
    )
```
